32 devices in a mesh: dp: 8 (over y, x, core), tensor: 4 (over z).
Axes of the slice: x: 2, y: 2, z: 4, core: 2. Of those that a mesh axis runs over, the one named last changes fastest.
Arguments:
- tokens: bfloat16 [16, 512, 768], P('dp', 'tensor'), may hold values from -6 to 6
- time_embed: float32 [16, 768], P('dp'), may hold values from -6 to 6
- class_embed: float32 [16, 768], P('dp'), may hold values from -6 to 6
- valid_mask: int32 [16, 512], P('dp'), may hold values from 0 to 1, as said below
- routes: int32 [16, 512, 2], P('dp'), may hold values from 0 to 7, all different within a row; in each aligned block of 512 rows (0 to 511, 512 to 1023, ..., all dimensions but the last counted through in order) at most 192 rows name the same one
- gate_logits: float32 [16, 512, 2], P('dp'), may hold values from -4 to 4
- ada_weight: bfloat16 [768, 6, 768], P(None, None, 'tensor'), may hold values from -0.21875 to 0.21875
- ada_bias: bfloat16 [6, 768], replicated, may hold values from -3 to 3
- qkv_weight: bfloat16 [768, 3, 768], P(None, None, 'tensor'), may hold values from -0.21875 to 0.21875
- out_weight: bfloat16 [768, 768], P(None, 'tensor'), may hold values from -0.875 to 0.875
- out_bias: bfloat16 [768], replicated, may hold values from -3 to 3
- fc1_weight: bfloat16 [768, 3072], P(None, 'tensor'), may hold values from -0.21875 to 0.21875
- fc1_bias: bfloat16 [3072], P('tensor'), may hold values from -3 to 3
- fc2_weight: bfloat16 [768, 3072], P(None, 'tensor'), may hold values from -0.109375 to 0.109375
- fc2_bias: bfloat16 [768], replicated, may hold values from -3 to 3
- expert_in: bfloat16 [768, 8, 3072], P(None, None, 'tensor'), may hold values from -0.21875 to 0.21875
- expert_out: bfloat16 [768, 8, 3072], P(None, None, 'tensor'), may hold values from -0.109375 to 0.109375
- out_grad: bfloat16 [16, 512, 768], P('dp', 'tensor'), may hold values from -6 to 6
Outputs:
- output: bfloat16 [16, 512, 768], P('dp', 'tensor')
- tokens_grad: bfloat16 [16, 512, 768], P('dp', 'tensor')
- condition_grad: float32 [16, 768], P('dp', 'tensor')
- gate_logits_grad: float32 [16, 512, 2], P('dp', 'tensor')
- ada_weight_grad: float32 [768, 6, 768], P('dp', None, 'tensor')
- ada_bias_grad: float32 [6, 768], P(None, ('tensor', 'dp'))
- qkv_weight_grad: float32 [768, 3, 768], P('dp', None, 'tensor')
- out_weight_grad: float32 [768, 768], P('dp', 'tensor')
- out_bias_grad: float32 [768], P(('dp', 'tensor'))
- fc1_weight_grad: float32 [768, 3072], P('dp', 'tensor')
- fc1_bias_grad: float32 [3072], P(('tensor', 'dp'))
- fc2_weight_grad: float32 [768, 3072], P('dp', 'tensor')
- fc2_bias_grad: float32 [768], P(('dp', 'tensor'))
- expert_in_grad: float32 [768, 8, 3072], P('dp', None, 'tensor')
- expert_out_grad: float32 [768, 8, 3072], P('dp', None, 'tensor')
The draws below stay inside these ranges and needn't reach their ends.
Inputs may be any that keep to these rules, and one draw needn't show every extreme that they name: `valid_mask`: each item's real patches are its first 256 or all 512; among items i * 2 to (i + 1) * 2 - 1 at least one is all real. `routes`: the two experts of a patch differ; no expert is named by more than 192 pairs of one item, padded patches included, and some item reaches 192.
All inputs are finite; a program needn't handle non-finite values.
Results may differ from the reference program's by a relative error of at most 0.02.
The reference program's roundings to bfloat16 on the way count: a program that leaves them out, or rounds other values in their place, can miss the bound.
Values may be sent and summed in bfloat16 or wider, within the bound.
No kernel may reach another device: no remote copies, remote signals or barrier semaphores. Data moves between devices by JAX's collectives and lax.ppermute only.
A program may use at most 256 MiB of HBM per device.

```python
import math
import jax
import jax.numpy as jnp
import numpy as np
from jax import lax

D = 768
HD = 64
FF = 3072
FFE = 3072
E = 8
SEQ = 512
ITEMS_DEV = 2
CAP = 192
ITEMS = 16


def draw_valid_mask(key, part):
    key = jax.random.fold_in(key, 11)
    first_key, second_key = jax.random.split(key)
    halved = jax.random.randint(first_key, (ITEMS,), 0, 2)
    full_pick = jax.random.randint(second_key, (ITEMS // ITEMS_DEV,), 0, ITEMS_DEV)
    item_ids = jnp.arange(ITEMS, dtype=jnp.int32)
    forced = item_ids % ITEMS_DEV == jnp.repeat(full_pick, ITEMS_DEV)
    halved = jnp.where(forced, 0, halved)
    length = SEQ - halved * (SEQ // 2)
    position = jnp.arange(SEQ, dtype=jnp.int32)
    return (position[None, :] < length[:, None]).astype(jnp.int32)


def raised(array, key, source, target, blocks, factor):
    def block_of(axis_at):
        return (jnp.arange(array.shape[axis_at]) // (array.shape[axis_at] // blocks)).reshape((-1,) + (1,) * (array.ndim - 1 - axis_at))

    one_side = jax.random.permutation(key, blocks)[block_of(target)]
    second = (block_of(target) + blocks // 2) % blocks
    return jnp.where((block_of(source) == one_side) | (block_of(source) == second), factor * array, array)


def levels(key, extent, pieces, low, largest):
    def one(axis_at, shards_of):
        draws = jax.random.uniform(jax.random.fold_in(jax.random.fold_in(key, 6), axis_at), (shards_of,), jnp.float32, low / len(pieces), largest / len(pieces))
        return jnp.repeat(jnp.exp(draws), extent[axis_at] // shards_of).reshape((-1,) + (1,) * (len(extent) - axis_at - 1))

    loudness = one(*pieces[0])
    for cut in pieces[1:]:
        loudness = loudness * one(*cut)
    return loudness


def deal_out(rng, own, number, rows, amount, top, most, slope):
    order = jax.random.permutation(rng, amount)
    packed, usual = shares(amount, rows * top, most, slope, True), shares(amount, rows * top, most, slope, False)
    places = jnp.arange(amount)

    def named(sizes, rotation):
        used = int((sizes > 0).sum())
        fixed = max(1, used // 4)
        shifted = fixed + (places - fixed + rotation * (used - fixed)) % max(1, amount - fixed)
        return jnp.zeros((amount,), jnp.int32).at[order[jnp.where(places < fixed, places, shifted)]].set(jnp.asarray(sizes, jnp.int32))

    sizes = jnp.where(number % 4 == 0, named(packed, number // 4), named(usual, number - number // 4 - 1))
    mixed = jax.random.permutation(jax.random.fold_in(own, 3), amount)
    giver, receiver = mixed[0:amount // 2 * 2:2], mixed[1:amount // 2 * 2:2]
    slack = jnp.minimum(sizes[giver] - 1, most - sizes[receiver]) // 2
    slack = jnp.where((giver == order[0]) | (receiver == order[0]) | (sizes[receiver] == 0), 0, jnp.maximum(slack, 0))
    shifted = jax.random.randint(jax.random.fold_in(own, 4), (amount // 2,), 0, 1 << 20) % (slack + 1)
    sizes = sizes.at[giver].add(-shifted).at[receiver].add(shifted)
    items = jnp.searchsorted(jnp.cumsum(sizes), jnp.arange(rows * top), side="right").astype(jnp.int32)
    grid = items.reshape(top, rows).T
    grid = grid[jax.random.permutation(jax.random.fold_in(own, 1), rows)]
    rotation = jax.random.randint(jax.random.fold_in(own, 2), (rows, 1), 0, top)
    return jnp.take_along_axis(grid, (jnp.arange(top)[None, :] + rotation) % top, axis=1)


def shares(amount, total, bound, slope, full):
    weights = [(1 << 20) // math.isqrt(standing ** slope) + 1 for standing in range(1, amount + 1)]
    largest = bound if full else min(bound, max(-(-total // amount), total * weights[0] // sum(weights)))
    least = 1 if total - largest >= amount - 1 else 0
    counts, rest = [largest] + [least] * (amount - 1), total - largest - least * (amount - 1)
    while rest > 0:
        candidates = [i for i in range(1, amount) if counts[i] < largest] or [i for i in range(1, amount) if counts[i] < bound]
        whole, budget = sum([weights[i] for i in candidates]), rest
        for i in candidates:
            addition = min(bound - counts[i], max(1, budget * weights[i] // whole), rest)
            counts[i] = counts[i] + addition
            rest = rest - addition
    return np.array(counts)


def normal_values(stream_key, shape, width, bound, shards=(), kind=jnp.bfloat16):
    gain = levels(stream_key, shape, shards, -0.22, 0.18) if shards else 1.0
    values = jax.random.normal(stream_key, shape, jnp.float32) * width * gain
    return jnp.minimum(jnp.maximum(values, -bound), bound).astype(kind)


def gaussian_with(stream_key, shape, deviation, most, cuts, heavy, kind=jnp.bfloat16):
    values = deviation * jax.random.normal(stream_key, shape, jnp.float32)
    if cuts:
        values = values * levels(stream_key, shape, cuts, -0.22, 0.18)
    return jnp.clip(raised(values, jax.random.fold_in(stream_key, 3), *heavy), -most, most).astype(kind)


def setup_inputs(seed: int = 0) -> dict:
    key_list = jax.random.split(jax.random.key(seed), 19)
    tokens = normal_values(key_list[0], (ITEMS, SEQ, D), 1.0, 6.0, ((0, 8), (1, 4)))
    time_embed = normal_values(key_list[1], (ITEMS, D), 1.0, 6.0, ((0, 8),), jnp.float32)
    class_embed = normal_values(key_list[2], (ITEMS, D), 1.0, 6.0, ((0, 8),), jnp.float32)
    valid_mask = draw_valid_mask(jax.random.fold_in(key_list[18], 71), 0)
    routes_keys = jax.random.split(jax.random.fold_in(key_list[4], 1), ITEMS * SEQ // SEQ)
    routes_turns = jax.random.permutation(jax.random.fold_in(key_list[4], 3), ITEMS * SEQ // SEQ)
    routes = jax.vmap(lambda own, number: deal_out(jax.random.fold_in(key_list[4], 2), own, number, SEQ, E, 2, CAP, 1))(routes_keys, routes_turns).reshape((ITEMS, SEQ, 2))
    gate_logits = normal_values(key_list[5], (ITEMS, SEQ, 2), 0.7, 4.0, ((0, 8),), jnp.float32)
    ada_weight = normal_values(key_list[6], (D, 6, D), D ** -0.5, 0.21875, ((2, 4),))
    ada_bias = normal_values(key_list[7], (6, D), 0.5, 3.0)
    qkv_weight = normal_values(key_list[8], (D, 3, D), D ** -0.5, 0.21875, ((2, 4),))
    out_weight = normal_values(key_list[9], (D, D), (D // 16) ** -0.5, 0.875, ((1, 4),))
    out_bias = normal_values(key_list[10], (D,), 0.5, 3.0)
    fc1_weight = normal_values(key_list[11], (D, FF), D ** -0.5, 0.21875, ((1, 4),))
    fc1_bias = normal_values(key_list[12], (FF,), 0.5, 3.0, ((0, 4),))
    fc2_weight = normal_values(key_list[13], (D, FF), FF ** -0.5, 0.109375, ((1, 4),))
    fc2_bias = normal_values(key_list[14], (D,), 0.5, 3.0)
    expert_in = normal_values(key_list[15], (D, E, FFE), D ** -0.5, 0.21875, ((2, 4),))
    expert_out = normal_values(key_list[16], (D, E, FFE), FFE ** -0.5, 0.109375, ((2, 4),))
    out_grad = gaussian_with(key_list[17], (ITEMS, SEQ, D), 1.0, 6.0, ((0, 8), (1, 4)), (0, 2, 8, 2.0))
    return {"tokens": tokens, "time_embed": time_embed, "class_embed": class_embed, "valid_mask": valid_mask, "routes": routes, "gate_logits": gate_logits, "ada_weight": ada_weight, "ada_bias": ada_bias, "qkv_weight": qkv_weight, "out_weight": out_weight, "out_bias": out_bias, "fc1_weight": fc1_weight, "fc1_bias": fc1_bias, "fc2_weight": fc2_weight, "fc2_bias": fc2_bias, "expert_in": expert_in, "expert_out": expert_out, "out_grad": out_grad}


@jax.custom_vjp
def low(v):
    return lax.optimization_barrier(v.astype(jnp.bfloat16)).astype(jnp.float32)

@jax.custom_vjp
def low_back(v):
    return v

def low_keep(v):
    return (low(v), None)

def low_pass(kept, grad):
    return (grad,)

def back_keep(v):
    return (v, None)

def back_low(kept, grad):
    return (low(grad),)
low.defvjp(low_keep, low_pass)
low_back.defvjp(back_keep, back_low)
highest = lax.Precision.HIGHEST

def layer_norm(values):
    center = values - lax.optimization_barrier(jnp.mean(values, axis=-1, keepdims=True))
    spread = lax.optimization_barrier(jnp.mean(center * center, axis=-1, keepdims=True))
    return center * lax.rsqrt(spread + 1e-06)

def smooth_gelu(values):
    return jax.nn.gelu(values, approximate=True)

def slot_tables(routes, valid_mask):
    batch_items = routes.shape[0]
    pair_count = routes.shape[1] * 2
    flat_routes = routes.reshape(batch_items, pair_count).astype(jnp.int32)
    live_pair = jnp.repeat(valid_mask, 2, axis=1).astype(jnp.int32)
    expert_ids = jnp.arange(E, dtype=jnp.int32)
    choose = ((flat_routes[:, :, None] == expert_ids[None, None, :]) & (live_pair[:, :, None] > 0)).astype(jnp.int32)
    before = (jnp.cumsum(choose, axis=1) - choose).astype(jnp.int32)
    position = lax.optimization_barrier(jnp.sum(before * choose, axis=2)).astype(jnp.int32)
    slot_index = jnp.where(live_pair > 0, flat_routes * CAP + position, 0).astype(jnp.int32)
    target = jnp.where(live_pair > 0, flat_routes * CAP + position, E * CAP).astype(jnp.int32)
    source = jnp.broadcast_to(jnp.arange(pair_count, dtype=jnp.int32)[None, :], (batch_items, pair_count))
    item_ids = jnp.broadcast_to(jnp.arange(batch_items, dtype=jnp.int32)[:, None], (batch_items, pair_count))
    slot_source = jnp.zeros((batch_items, E * CAP), jnp.int32).at[item_ids, target].set(source, mode='drop')
    slot_filled = jnp.zeros((batch_items, E * CAP), jnp.float32).at[item_ids, target].set(1.0, mode='drop')
    return (slot_index, live_pair, slot_source, slot_filled)

def block_forward(weights, tokens, time_embed, class_embed, gate_logits, valid_mask, slot_index, live_pair, slot_source):
    ada_weight, ada_bias, qkv_weight, out_weight, out_bias, fc1_weight, fc1_bias, fc2_weight, fc2_bias, expert_in, expert_out = weights
    batch_items = tokens.shape[0]
    seq_length = tokens.shape[1]
    head_count = D // HD
    condition = time_embed + class_embed
    cond_act = low(jax.nn.silu(condition))
    modulation = low_back(jnp.einsum('gd,dsk->gsk', cond_act, ada_weight, precision=highest) + ada_bias[None])
    parts = [modulation[:, column][:, None, :] for column in range(6)]
    shift_attn, scale_attn, gate_attn, shift_mlp, scale_mlp, gate_mlp = parts
    normed_attn = low(layer_norm(tokens) * (1.0 + scale_attn) + shift_attn)
    projected = jnp.einsum('gsd,dcf->gscf', normed_attn, qkv_weight, precision=highest)
    projected = low_back(low(projected))
    queries = projected[:, :, 0].reshape(batch_items, seq_length, head_count, HD)
    key_rows = projected[:, :, 1].reshape(batch_items, seq_length, head_count, HD)
    value_rows = projected[:, :, 2].reshape(batch_items, seq_length, head_count, HD)
    scores = low_back(jnp.einsum('gshe,gthe->ghst', queries, key_rows, precision=highest) * 0.125)
    scores = jnp.where(valid_mask[:, None, None, :] > 0, scores, -1e+30)
    attn_probs = jax.nn.softmax(scores, axis=-1)
    mixed_heads = jnp.einsum('ghst,gthe->gshe', low(attn_probs), value_rows, precision=highest)
    mixed_heads = low_back(low(mixed_heads.reshape(batch_items, seq_length, D)))
    branch_attn = low_back(jnp.einsum('gsf,df->gsd', mixed_heads, out_weight, precision=highest) + out_bias)
    middle = tokens + gate_attn * branch_attn
    normed_mlp = low(layer_norm(middle) * (1.0 + scale_mlp) + shift_mlp)
    hidden = low_back(jnp.einsum('gsd,df->gsf', normed_mlp, fc1_weight, precision=highest) + fc1_bias)
    shared = jnp.einsum('gsf,df->gsd', low(smooth_gelu(hidden)), fc2_weight, precision=highest)
    slot_token = slot_source // 2
    buffer = jnp.take_along_axis(normed_mlp, slot_token[:, :, None], axis=1).reshape(batch_items, E, CAP, D)
    upward = low_back(jnp.einsum('gecd,def->gecf', buffer, expert_in, precision=highest))
    returned = jnp.einsum('gecf,def->gecd', low(smooth_gelu(upward)), expert_out, precision=highest)
    returned = low_back(returned).reshape(batch_items, E * CAP, D)
    picked = jnp.take_along_axis(returned, slot_index[:, :, None], axis=1).reshape(batch_items, seq_length, 2, D)
    live_share = live_pair.reshape(batch_items, seq_length, 2).astype(jnp.float32)
    gate_share = jax.nn.softmax(gate_logits, axis=-1) * live_share
    mixture = lax.optimization_barrier(jnp.sum(picked * gate_share[..., None], axis=2))
    branch_mlp = low_back(shared + fc2_bias + mixture)
    return middle + gate_mlp * branch_mlp

def reference(tokens, time_embed, class_embed, valid_mask, routes, gate_logits, ada_weight, ada_bias, qkv_weight, out_weight, out_bias, fc1_weight, fc1_bias, fc2_weight, fc2_bias, expert_in, expert_out, out_grad):
    weights = tuple((matrix.astype(jnp.float32) for matrix in (ada_weight, ada_bias, qkv_weight, out_weight, out_bias, fc1_weight, fc1_bias, fc2_weight, fc2_bias, expert_in, expert_out)))
    group = math.gcd(ITEMS, max(1, 4096 // SEQ))
    rounds = ITEMS // group

    def split(values):
        return values.reshape((rounds, group) + values.shape[1:])
    slot_index, live_pair, slot_source, slot_filled = slot_tables(routes, valid_mask)
    inputs = (split(tokens.astype(jnp.float32)), split(time_embed.astype(jnp.float32)), split(class_embed.astype(jnp.float32)), split(gate_logits.astype(jnp.float32)), split(valid_mask), split(slot_index), split(live_pair), split(slot_source), split(out_grad.astype(jnp.float32)))

    def advance(totals, blocks):
        token_block, time_block, class_block, logit_block, valid_block, slot_block, live_block, source_block, grad_block = blocks

        def apply(params, token_part, time_part, class_part, logit_part):
            return block_forward(params, token_part, time_part, class_part, logit_part, valid_block, slot_block, live_block, source_block)
        result, pull = jax.vjp(apply, weights, token_block, time_block, class_block, logit_block)
        grads = pull(grad_block)
        totals = jax.tree.map(jnp.add, totals, grads[0])
        return (totals, (result.astype(jnp.bfloat16), grads[1].astype(jnp.bfloat16), grads[2], grads[4]))
    zeros = jax.tree.map(jnp.zeros_like, weights)
    totals, results = lax.scan(advance, zeros, inputs)
    output = results[0].reshape(ITEMS, SEQ, D)
    tokens_grad = results[1].reshape(ITEMS, SEQ, D)
    condition_grad = results[2].reshape(ITEMS, D)
    gate_logits_grad = results[3].reshape(ITEMS, SEQ, 2)
    return (output, tokens_grad, condition_grad, gate_logits_grad, totals[0], totals[1], totals[2], totals[3], totals[4], totals[5], totals[6], totals[7], totals[8], totals[9], totals[10])
```

```python
import functools

import jax
import jax.numpy as jnp
from jax import lax
from jax.experimental import pallas as pl
from jax.experimental.pallas import tpu as pltpu
from jax.sharding import PartitionSpec as P

HD = 64
E = 8
CAP = 192
F32 = jnp.float32
BF16 = jnp.bfloat16
I32 = jnp.int32
VMEM_BYTES = 56 * 1024 * 1024


def dot(spec, left, right):
    return jnp.einsum(spec, left, right, preferred_element_type=F32)


def mm(left, right):
    return jnp.dot(left, right, preferred_element_type=F32)


def mm_nt(left, right):
    return lax.dot_general(left, right, (((1,), (1,)), ((), ())), preferred_element_type=F32)


def mm_tn(left, right):
    return lax.dot_general(left, right, (((0,), (0,)), ((), ())), preferred_element_type=F32)


def after(values, *others):
    return lax.optimization_barrier((values,) + others)[0]


def from_rank(values, step):
    size = lax.axis_size("tensor")
    return lax.ppermute(values, "tensor", [(i, (i - step) % size) for i in range(size)])


def to_rank(values, step):
    size = lax.axis_size("tensor")
    return lax.ppermute(values, "tensor", [(i, (i + step) % size) for i in range(size)])


def gather_parts(values):
    size = lax.axis_size("tensor")
    return [values] + [from_rank(values, step) for step in range(1, size)]


def scatter_sum(parts):
    total = parts[0].astype(F32)
    for step in range(1, len(parts)):
        total = total + to_rank(parts[step], step).astype(F32)
    return total


def swing(values, amount, axis):
    twice = jnp.concatenate([values, values], axis=axis)
    return lax.dynamic_slice_in_dim(twice, amount, values.shape[axis], axis)


def dp_exchange(values, bit):
    size = lax.axis_size("dp")
    return lax.ppermute(values, "dp", [(i, i ^ (1 << bit)) for i in range(size)])


def to_relative(blocks):
    size = lax.axis_size("dp")
    rank = lax.axis_index("dp")
    for bit in range(size.bit_length() - 1):
        paired = blocks.reshape((size >> (bit + 1), 2, 1 << bit) + blocks.shape[1:])
        swapped = jnp.where(((rank >> bit) & 1) == 0, paired, paired[:, ::-1])
        blocks = swapped.reshape(blocks.shape)
    return blocks


def dp_scatter(blocks, order, kind):
    current = blocks.reshape((2,) * len(order) + blocks.shape[1:])
    left = sorted(order, reverse=True)
    for bit in order:
        axis = left.index(bit)
        keep = lax.index_in_dim(current, 0, axis, keepdims=False)
        send = lax.index_in_dim(current, 1, axis, keepdims=False)
        other = dp_exchange(send, bit)
        current = (keep.astype(F32) + other.astype(F32)).astype(kind)
        left.pop(axis)
    return current


def dp_gather(values):
    size = lax.axis_size("dp")
    rank = lax.axis_index("dp")
    current = values[None]
    for bit in range(size.bit_length() - 1):
        other = dp_exchange(current, bit)
        mine = (rank >> bit) & 1
        low = jnp.where(mine == 0, current, other)
        high = jnp.where(mine == 0, other, current)
        current = jnp.concatenate([low, high], axis=0)
    return current


def norm_parts(values):
    center = values - jnp.mean(values, axis=-1, keepdims=True)
    spread = jnp.mean(center * center, axis=-1, keepdims=True)
    scale = lax.rsqrt(spread + 1e-06)
    return center * scale, scale


def norm_pull(normed, scale, grad):
    return scale * (
        grad
        - jnp.mean(grad, axis=-1, keepdims=True)
        - normed * jnp.mean(grad * normed, axis=-1, keepdims=True)
    )


def gelu_both(values):
    factor = 0.7978845608028654
    square = values * values
    inner = jnp.tanh(values * (factor + (factor * 0.044715) * square))
    half = 0.5 + 0.5 * inner
    slope = half + values * (half * (1.0 - inner)) * (factor + (factor * 0.134145) * square)
    return values * half, slope


def call(kernel, out_shape, in_specs, out_specs, args, grid=(), scratch=(), flops=0, moved=0, name=None, alias=None):
    return pl.pallas_call(
        kernel,
        out_shape=out_shape,
        grid=grid,
        in_specs=in_specs,
        out_specs=out_specs,
        scratch_shapes=scratch,
        input_output_aliases=alias or {},
        compiler_params=pltpu.CompilerParams(
            vmem_limit_bytes=VMEM_BYTES, dimension_semantics=("arbitrary",) * len(grid)
        ),
        cost_estimate=pl.CostEstimate(flops=flops, bytes_accessed=moved, transcendentals=0),
        name=name,
    )(*args)


def whole(shape):
    zeros = (0,) * len(shape)
    return pl.BlockSpec(shape, lambda *_: zeros)


def shaped(shape, kind):
    return jax.ShapeDtypeStruct(shape, kind)


def pack_heads(values):
    half = values.shape[0] // 2
    rest = jnp.concatenate([values[:half, 128:], values[half:, 128:]], axis=1)
    return jnp.concatenate([values[:, :128], rest], axis=0)


def unpack_heads(values):
    half = values.shape[0] // 3
    rest = values[2 * half :]
    upper = jnp.concatenate([values[:half], rest[:, :64]], axis=1)
    lower = jnp.concatenate([values[half : 2 * half], rest[:, 64:]], axis=1)
    return jnp.concatenate([upper, lower], axis=0)


def attention_kernel(heads, tokens_ref, mod_ref, weight_ref, valid_ref, projected_ref, mixed_ref):
    width = heads * HD
    normed, _ = norm_parts(tokens_ref[0].astype(F32))
    normed = normed * (1.0 + mod_ref[0, 1:2]) + mod_ref[0, 0:1]
    projected = mm(normed.astype(BF16), weight_ref[...]).astype(BF16)
    projected_ref[0] = projected
    live = valid_ref[0] > 0
    mixed = []
    for head in range(heads):
        low = head * HD
        query = projected[:, low : low + HD] * jnp.asarray(0.125, BF16)
        key = projected[:, width + low : width + low + HD]
        value = projected[:, 2 * width + low : 2 * width + low + HD]
        scores = jnp.where(live, mm_nt(query, key), -1e30)
        exponent = jnp.exp(scores - jnp.max(scores, axis=1, keepdims=True))
        probs = exponent * (1.0 / jnp.sum(exponent, axis=1, keepdims=True))
        mixed.append(mm(probs.astype(BF16), value))
    mixed_ref[0] = pack_heads(jnp.concatenate(mixed, axis=1).astype(BF16))


def attention(tokens, mod, weight, valid):
    items, length, width = tokens.shape
    head_width = weight.shape[1] // 3
    return call(
        functools.partial(attention_kernel, head_width // HD),
        (shaped((items, length, 3 * head_width), BF16), shaped((items, 3 * length // 2, 128), BF16)),
        [
            pl.BlockSpec((1, length, width), lambda i: (i, 0, 0)),
            pl.BlockSpec((1, 6, width), lambda i: (i, 0, 0)),
            whole(weight.shape),
            pl.BlockSpec((1, 1, length), lambda i: (i, 0, 0)),
        ],
        (
            pl.BlockSpec((1, length, 3 * head_width), lambda i: (i, 0, 0)),
            pl.BlockSpec((1, 3 * length // 2, 128), lambda i: (i, 0, 0)),
        ),
        (tokens, mod, weight, valid),
        grid=(items,),
        flops=8_000_000_000,
        moved=6_000_000,
        name="attention_forward",
    )


def middle_kernel(ranks, mixed_ref, rest_ref, weight_ref, bias_ref, tokens_ref, mod_ref, middle_ref, branch_ref, normed_ref):
    upper = pl.program_id(1) == 0
    branch = bias_ref[...].astype(F32)
    for rank in range(ranks):
        rest = jnp.where(upper, rest_ref[rank, 0, :, :64], rest_ref[rank, 0, :, 64:])
        branch = branch + mm(jnp.concatenate([mixed_ref[rank, 0], rest], axis=1), weight_ref[rank])
    middle = tokens_ref[0].astype(F32) + mod_ref[0, 2:3] * branch
    middle_ref[0] = middle
    branch_ref[0] = branch.astype(BF16)
    normed, _ = norm_parts(middle)
    normed_ref[0] = (normed * (1.0 + mod_ref[0, 4:5]) + mod_ref[0, 3:4]).astype(BF16)


def middle_part(mixed, weight, bias, tokens, mod):
    items, length, width = tokens.shape
    ranks = mixed.shape[0]
    block = length // 2
    rows = pl.BlockSpec((1, block, width), lambda i, r: (i, r, 0))
    return call(
        functools.partial(middle_kernel, ranks),
        (
            shaped(tokens.shape, F32),
            shaped(tokens.shape, BF16),
            shaped(tokens.shape, BF16),
        ),
        [
            pl.BlockSpec((ranks, 1, block, 128), lambda i, r: (0, i, r, 0)),
            pl.BlockSpec((ranks, 1, block, 128), lambda i, r: (0, i, 2, 0)),
            whole(weight.shape),
            whole(bias.shape),
            rows,
            pl.BlockSpec((1, 6, width), lambda i, r: (i, 0, 0)),
        ],
        (rows, rows, rows),
        (mixed, mixed, weight, bias, tokens, mod),
        grid=(items, 2),
        flops=3_000_000_000,
        moved=12_000_000,
        name="middle",
    )


def hot_rows(expert, marks):
    slots = lax.broadcasted_iota(I32, (CAP, marks.shape[1]), 0) + expert * CAP
    return slots == marks[0:1], slots == marks[1:2]


def as_hot(mask):
    return jnp.where(mask, 1.0, 0.0).astype(BF16)


def forward_kernel(
    items,
    normed_ref,
    marks_ref,
    share_ref,
    columns_ref,
    fc1_ref,
    bias_ref,
    fc2_ref,
    first_ref,
    second_ref,
    buffer_ref,
    act_ref,
    slope_ref,
    hidden_ref,
    hidden_slope_ref,
    out_ref,
    slots_ref,
):
    expert = pl.program_id(0)
    length = normed_ref.shape[1]

    @pl.when(expert == 0)
    def _():
        for item in range(items):
            hidden = mm(normed_ref[item], fc1_ref[...]) + bias_ref[...].astype(F32)
            value, slope = gelu_both(hidden)
            hidden_ref[item] = value.astype(BF16)
            hidden_slope_ref[item] = slope.astype(BF16)

    shares = []
    for item in range(items):
        one, two = hot_rows(expert, marks_ref[item])
        buffer_ref[0, item * CAP : (item + 1) * CAP] = mm(as_hot(one | two), normed_ref[item]).astype(BF16)
        held = jnp.where(one, share_ref[item, 0:1], 0.0) + jnp.where(two, share_ref[item, 1:2], 0.0)
        shares.append(jnp.sum(held, axis=1, keepdims=True))
    share = jnp.concatenate(shares, axis=0)
    value, slope = gelu_both(mm(buffer_ref[0], first_ref[0]))
    act_ref[0] = (share * value).astype(BF16)
    slope_ref[0] = (share * slope).astype(BF16)
    returned = mm_nt(act_ref[0], second_ref[0]).astype(BF16)
    place = pl.ds(pl.multiple_of(expert * CAP, 64), CAP)
    for item in range(items):
        slots_ref[item, place] = returned[item * CAP : (item + 1) * CAP]

    @pl.when(expert == E - 1)
    def _():
        lanes = lax.broadcasted_iota(I32, (length, E * CAP), 1)
        for item in range(items):
            marks = columns_ref[item]
            hot = as_hot((lanes == marks[:, 0:1]) | (lanes == marks[:, 1:2]))
            total = mm(hot, slots_ref[item]) + mm_nt(hidden_ref[item], fc2_ref[...])
            out_ref[item] = total.astype(BF16)


def forward_part(normed, marks, share, columns, fc1, bias, fc2, first, second):
    items, length, width = normed.shape
    units = fc1.shape[1]
    slots = items * CAP
    inner = pl.BlockSpec((1, slots, units), lambda e: (e, 0, 0))
    weight = pl.BlockSpec((1, width, units), lambda e: (e, 0, 0))
    hidden = (items, length, units)
    return call(
        functools.partial(forward_kernel, items),
        (
            shaped((E, slots, width), BF16),
            shaped((E, slots, units), BF16),
            shaped((E, slots, units), BF16),
            shaped(hidden, BF16),
            shaped(hidden, BF16),
            shaped(normed.shape, BF16),
        ),
        [
            whole(normed.shape),
            whole(marks.shape),
            whole(share.shape),
            whole(columns.shape),
            whole(fc1.shape),
            whole(bias.shape),
            whole(fc2.shape),
            weight,
            weight,
        ],
        (
            pl.BlockSpec((1, slots, width), lambda e: (e, 0, 0)),
            inner,
            inner,
            whole(hidden),
            whole(hidden),
            whole(normed.shape),
        ),
        (normed, marks, share, columns, fc1, bias, fc2, first, second),
        grid=(E,),
        scratch=[pltpu.VMEM((items, E * CAP, width), BF16)],
        flops=14_000_000_000,
        moved=40_000_000,
        name="mlp_forward",
    )


def store_blocks(keep_ref, send_ref, rank, index, grad):
    blocks, rows = 2 * keep_ref.shape[0], keep_ref.shape[2]
    for pair in range(blocks // 2):
        place = lax.bitwise_xor(rank // 2, pair)
        low = grad[2 * pair * rows : (2 * pair + 1) * rows]
        high = grad[(2 * pair + 1) * rows : (2 * pair + 2) * rows]
        odd = rank % 2 == 1

        @pl.when(odd)
        def _():
            keep_ref[place, index] = high
            send_ref[place, index] = low

        @pl.when(jnp.logical_not(odd))
        def _():
            keep_ref[place, index] = low
            send_ref[place, index] = high


def split_blocks(grads, dp_size):
    count, width, units = grads.shape
    blocks = to_relative(grads.reshape(count, dp_size, width // dp_size, units).swapaxes(0, 1))
    pairs = blocks.reshape((dp_size // 2, 2) + blocks.shape[1:])
    return pairs[:, 0], pairs[:, 1]


def call_grads(kernel, steps, rank, dp_size, shape, outs, out_specs, specs, args, alias=None):
    width, units = shape
    rows = width // dp_size
    smooth = rows % 16 == 0
    block = pl.BlockSpec((dp_size // 2, 1, rows, units), lambda e: (0, e, 0, 0))
    part = shaped((dp_size // 2, steps, rows, units), BF16)
    return call(
        kernel,
        outs + ((part, part) if smooth else ()),
        [pl.BlockSpec(memory_space=pltpu.SMEM)] + specs,
        out_specs + ((block, block) if smooth else ()),
        (rank,) + args,
        grid=(steps,),
        flops=5_000_000_000,
        moved=20_000_000,
        name="weight_grads",
        alias=alias,
    )


def expert_block(start, count, shape):
    return pl.BlockSpec((1,) + shape, lambda e: (jnp.minimum(e, count - 1) + start, 0, 0))


def slots_kernel(items, start, count, rank_ref, marks_ref, act_ref, *refs):
    expert = pl.program_id(0)
    if start == 0:
        grad_ref, mod_ref, hidden_ref, branch_ref, slots_ref, *grad_refs = refs

        @pl.when(expert == 0)
        def _():
            for item in range(items):
                branch_ref[item] = (grad_ref[item].astype(F32) * mod_ref[item, 5:6]).astype(BF16)

    else:
        branch_ref, _, slots_ref, *grad_refs = refs

    @pl.when(expert < count)
    def _():
        for item in range(items):
            one, two = hot_rows(expert + start, marks_ref[item])
            slots_ref[0, item * CAP : (item + 1) * CAP] = mm(as_hot(one | two), branch_ref[item]).astype(BF16)
        if grad_refs:
            store_blocks(*grad_refs, rank_ref[0], 0, mm_tn(slots_ref[0], act_ref[0]).astype(BF16))

    if start == 0 and grad_refs:

        @pl.when(expert == count)
        def _():
            total = mm_tn(branch_ref[0], hidden_ref[0])
            for item in range(1, items):
                total = total + mm_tn(branch_ref[item], hidden_ref[item])
            store_blocks(*grad_refs, rank_ref[0], 0, total.astype(BF16))


def slots_part(start, count, marks, act, rank, dp_size, grad=None, mod=None, hidden=None, branch=None, held=None):
    items, length, width = (branch if grad is None else grad).shape
    units = act.shape[2]
    slots = items * CAP
    all_rows = whole((items, length, width))
    each = expert_block(start, count, (slots, width))
    filled = shaped((E, slots, width), BF16)
    if start == 0:
        specs, more = [all_rows, whole(mod.shape), whole(hidden.shape)], (grad, mod, hidden)
        outs, out_specs, alias = (shaped(grad.shape, BF16), filled), (all_rows, each), {}
    else:
        specs, more = [all_rows, pl.BlockSpec(memory_space=pl.ANY)], (branch, held)
        outs, out_specs, alias = (filled,), (each,), {4: 0}
    result = call_grads(
        functools.partial(slots_kernel, items, start, count),
        count + (start == 0),
        rank,
        dp_size,
        (width, units),
        outs,
        out_specs,
        [whole(marks.shape), expert_block(start, count, (slots, units))] + specs,
        (marks, act) + more,
        alias,
    )
    if (width // dp_size) % 16:
        picked = slice(start, start + count)
        grads = dot("ecd,ecf->edf", result[-1][picked], act[picked])
        if start == 0:
            grads = jnp.concatenate([grads, dot("isd,isf->df", result[0], hidden)[None]], axis=0)
        result = tuple(result) + split_blocks(grads.astype(BF16), dp_size)
    return result


def dense_right(packed, right_ref, item):
    if not packed:
        return right_ref[item]
    return jnp.concatenate([unpack_heads(right_ref[rank, item]) for rank in range(right_ref.shape[0])], axis=1)


def first_kernel(count, packed, rank_ref, left_ref, right_ref, dense_left_ref, dense_right_ref, *grad_refs):
    expert = pl.program_id(0)

    @pl.when(expert < count)
    def _():
        store_blocks(*grad_refs, rank_ref[0], 0, mm_tn(left_ref[0], right_ref[0]).astype(BF16))

    @pl.when(expert == count)
    def _():
        total = mm_tn(dense_left_ref[0], dense_right(packed, dense_right_ref, 0))
        for item in range(1, dense_left_ref.shape[0]):
            total = total + mm_tn(dense_left_ref[item], dense_right(packed, dense_right_ref, item))
        store_blocks(*grad_refs, rank_ref[0], 0, total.astype(BF16))


def first_part(start, count, left, right, dense, packed, rank, dp_size):
    _, slots, width = left.shape
    units = right.shape[2]
    rows = width // dp_size
    if rows % 16:
        picked = slice(start, start + count)
        items = dense[0].shape[0]
        extra = sum(mm_tn(dense[0][item], dense_right(packed, dense[1], item)) for item in range(items))
        grads = jnp.concatenate([dot("ecd,ecf->edf", left[picked], right[picked]), extra[None]], axis=0)
        return split_blocks(grads.astype(BF16), dp_size)
    return call_grads(
        functools.partial(first_kernel, count, packed),
        count + 1,
        rank,
        dp_size,
        (width, units),
        (),
        (),
        [
            expert_block(start, count, (slots, width)),
            expert_block(start, count, (slots, units)),
            whole(dense[0].shape),
            whole(dense[1].shape),
        ],
        (left, right) + tuple(dense),
    )


def halve_kernel(first, keep_ref, other_ref, kept_ref, sent_ref):
    total = (keep_ref[...].astype(F32) + other_ref[...].astype(F32)).astype(BF16)
    kept_ref[...] = total[0:1] if first else total[:, 0:1]
    sent_ref[...] = total[1:2] if first else total[:, 1:2]


def halve(keep, other, axis):
    lead = keep.shape[0]
    rest = keep.shape[1:]
    zeros = (0,) * len(rest)
    if lead == 2:
        shape, outer, axis = (2, 1) + rest, 1, 0
    else:
        shape, outer = (2, lead // 2) + rest, lead // 2
    if axis == 0:
        block, result = (2, 1) + rest, (1, outer) + rest
        spec = pl.BlockSpec(block, lambda i: (0, i) + zeros)
        out = pl.BlockSpec((1, 1) + rest, lambda i: (0, i) + zeros)
        steps = outer
    else:
        block, result = (1, 2) + rest, (2, 1) + rest
        spec = pl.BlockSpec(block, lambda i: (i, 0) + zeros)
        out = pl.BlockSpec((1, 1) + rest, lambda i: (i, 0) + zeros)
        steps = 2
    size = keep.size * 2
    kept, sent = call(
        functools.partial(halve_kernel, axis == 0),
        (shaped(result, BF16),) * 2,
        [spec, spec],
        (out, out),
        (keep.reshape(shape), other.reshape(shape)),
        grid=(steps,),
        flops=size,
        moved=3 * size,
        name="halve",
    )
    return kept.reshape((lead // 2,) + rest), sent.reshape((lead // 2,) + rest)


def last_kernel(halfway, counts, *refs):
    inputs, (out_ref, *dense_refs) = refs[: 2 * len(counts)], refs[2 * len(counts) :]
    dense = iter(dense_refs)
    place = 0
    for group, size in enumerate(counts):
        keep_ref, other_ref = inputs[2 * group], inputs[2 * group + 1]
        for index in range(size):
            total = keep_ref[index].astype(F32) + other_ref[index].astype(F32)
            if index < halfway:
                out_ref[:, place] = total
                place += 1
            else:
                next(dense)[...] = total


def last(pairs, halfway):
    counts = [keep.shape[0] for keep, _ in pairs]
    rows, units = pairs[0][0].shape[1:]
    args = [value for pair in pairs for value in pair]
    vmem = pl.BlockSpec(memory_space=pltpu.VMEM)
    extra = sum(size > halfway for size in counts)
    return call(
        functools.partial(last_kernel, halfway, counts),
        (shaped((rows, halfway * len(counts), units), F32),) + (shaped((rows, units), F32),) * extra,
        [vmem] * len(args),
        (vmem,) * (1 + extra),
        tuple(args),
        flops=sum(counts) * rows * units,
        moved=8 * sum(counts) * rows * units,
        name="last_sum",
    )


def back_kernel(
    items,
    branch_ref,
    columns_ref,
    fc1_ref,
    fc2_ref,
    hidden_slope_ref,
    slots_ref,
    act_ref,
    slope_ref,
    first_ref,
    second_ref,
    up_grad_ref,
    hidden_grad_ref,
    bias_grad_ref,
    grad_ref,
    gate_ref,
    held_ref,
    dots_ref,
):
    expert = pl.program_id(0)
    length = branch_ref.shape[1]

    @pl.when(expert == 0)
    def _():
        total = jnp.zeros(bias_grad_ref.shape, F32)
        for item in range(items):
            grad = mm(branch_ref[item], fc2_ref[...]) * hidden_slope_ref[item].astype(F32)
            grad = grad.astype(BF16)
            hidden_grad_ref[item] = grad
            total = total + jnp.sum(grad.astype(F32), axis=0, keepdims=True)
            grad_ref[item] = mm_nt(grad, fc1_ref[...])
        bias_grad_ref[...] = total

    pulled = mm(slots_ref[0], second_ref[0])
    up_grad = (pulled * slope_ref[0].astype(F32)).astype(BF16)
    up_grad_ref[0] = up_grad
    total = jnp.sum(act_ref[0].astype(F32) * pulled, axis=1, keepdims=True)
    high = total.astype(BF16).astype(F32)
    lane = lax.broadcasted_iota(I32, (items * CAP, 128), 1)
    split = jnp.where(lane == 0, high, jnp.where(lane == 1, total - high, 0.0)).astype(BF16)
    back = mm_nt(up_grad, first_ref[0]).astype(BF16)
    place = pl.ds(pl.multiple_of(expert * CAP, 64), CAP)
    for item in range(items):
        held_ref[item, place] = back[item * CAP : (item + 1) * CAP]
        dots_ref[item, place] = split[item * CAP : (item + 1) * CAP]

    @pl.when(expert == E - 1)
    def _():
        lanes = lax.broadcasted_iota(I32, (length, E * CAP), 1)
        for item in range(items):
            marks = columns_ref[item]
            one = lanes == marks[:, 0:1]
            two = lanes == marks[:, 1:2]
            grad_ref[item] += mm(as_hot(one | two), held_ref[item])
            gate_ref[item, 0] = mm(as_hot(one), dots_ref[item])
            gate_ref[item, 1] = mm(as_hot(two), dots_ref[item])


def back_part(branch, columns, fc1, fc2, hidden_slope, branch_slot, act, slope, first, second):
    items, length, width = branch.shape
    units = fc1.shape[1]
    slots = items * CAP
    inner = pl.BlockSpec((1, slots, units), lambda e: (e, 0, 0))
    weight = pl.BlockSpec((1, width, units), lambda e: (e, 0, 0))
    hidden = (items, length, units)
    return call(
        functools.partial(back_kernel, items),
        (
            shaped((E, slots, units), BF16),
            shaped(hidden, BF16),
            shaped((1, units), F32),
            shaped(branch.shape, F32),
            shaped((items, 2, length, 128), F32),
        ),
        [
            whole(branch.shape),
            whole(columns.shape),
            whole(fc1.shape),
            whole(fc2.shape),
            whole(hidden),
            pl.BlockSpec((1, slots, width), lambda e: (e, 0, 0)),
            inner,
            inner,
            weight,
            weight,
        ],
        (
            inner,
            whole(hidden),
            whole((1, units)),
            whole(branch.shape),
            whole((items, 2, length, 128)),
        ),
        (branch, columns, fc1, fc2, hidden_slope, branch_slot, act, slope, first, second),
        grid=(E,),
        scratch=[
            pltpu.VMEM((items, E * CAP, width), BF16),
            pltpu.VMEM((items, E * CAP, 128), BF16),
        ],
        flops=12_000_000_000,
        moved=40_000_000,
        name="mlp_back",
    )


def second_norm_kernel(
    ranks, grad_ref, middle_ref, branch_ref, cotangent_ref, mlp_ref, mod_ref, weight_ref, own_ref, middle_grad_ref, low_ref, mixed_ref, sums_ref
):
    step = pl.program_id(1)
    normed, scale = norm_parts(middle_ref[0])
    grad = grad_ref[0]
    block = grad.shape[0]
    shift_sum = jnp.sum(grad, axis=0, keepdims=True)
    scale_sum = jnp.sum(grad * normed, axis=0, keepdims=True)
    pulled = norm_pull(normed, scale, grad * (1.0 + mod_ref[0, 4:5]))
    place = lax.broadcasted_iota(I32, (block, 1), 0) + step * block
    own = (place >= own_ref[0]) & (place < own_ref[1])
    cotangent = cotangent_ref[0].astype(F32)
    mlp_sum = jnp.sum(cotangent * mlp_ref[0].astype(F32), axis=0, keepdims=True)
    pulled = pulled + jnp.where(own, cotangent, 0.0)
    middle_grad_ref[0] = pulled.astype(BF16)
    gate_sum = jnp.sum(pulled * branch_ref[0].astype(F32), axis=0, keepdims=True)
    low = (pulled * mod_ref[0, 2:3]).astype(BF16)
    low_ref[0] = low
    bias_sum = jnp.sum(low.astype(F32), axis=0, keepdims=True)
    for rank in range(ranks):
        mixed = mm_nt(low, weight_ref[rank]).astype(BF16)
        mixed_ref[rank, 0, pl.ds(pl.multiple_of(step * block, 128), block)] = mixed[:, :128]

        @pl.when(step == 0)
        def _():
            mixed_ref[rank, 0, 2 * block :, :64] = mixed[:, 128:]

        @pl.when(step > 0)
        def _():
            mixed_ref[rank, 0, 2 * block :, 64:] = mixed[:, 128:]

    sums = jnp.concatenate([shift_sum, scale_sum, gate_sum, bias_sum, mlp_sum], axis=0)

    @pl.when(step == 0)
    def _():
        sums_ref[0] = sums

    @pl.when(step > 0)
    def _():
        sums_ref[0] += sums


def second_norm_part(grad, middle, branch, cotangent, mlp, mod, weight, own):
    items, length, width = grad.shape
    ranks = weight.shape[0]
    block = length // 2
    rows = pl.BlockSpec((1, block, width), lambda i, r: (i, r, 0))
    return call(
        functools.partial(second_norm_kernel, ranks),
        (
            shaped(grad.shape, BF16),
            shaped(grad.shape, BF16),
            shaped((ranks, items, 3 * length // 2, 128), BF16),
            shaped((items, 5, width), F32),
        ),
        [
            rows,
            rows,
            rows,
            rows,
            rows,
            pl.BlockSpec((1, 6, width), lambda i, r: (i, 0, 0)),
            whole(weight.shape),
            pl.BlockSpec(memory_space=pltpu.SMEM),
        ],
        (
            rows,
            rows,
            pl.BlockSpec((ranks, 1, 3 * length // 2, 128), lambda i, r: (0, i, 0, 0)),
            pl.BlockSpec((1, 5, width), lambda i, r: (i, 0, 0)),
        ),
        (grad, middle, branch, cotangent, mlp, mod, weight, own),
        grid=(items, 2),
        flops=3_000_000_000,
        moved=15_000_000,
        name="second_norm_back",
    )


def attention_back_kernel(
    heads, rank_ref, tokens_ref, mod_ref, weight_ref, valid_ref, projected_ref, mixed_ref, middle_ref, part_ref, sums_ref, *rest
):
    *grad_refs, total_ref = rest
    item = pl.program_id(0)
    width = heads * HD
    base, scale = norm_parts(tokens_ref[0].astype(F32))
    normed = (base * (1.0 + mod_ref[0, 1:2]) + mod_ref[0, 0:1]).astype(BF16)
    projected = projected_ref[0]
    grads = [[], [], []]
    live = valid_ref[0] > 0
    mixed_grad = unpack_heads(mixed_ref[0])
    for head in range(heads):
        low = head * HD
        query = projected[:, low : low + HD] * jnp.asarray(0.125, BF16)
        key = projected[:, width + low : width + low + HD]
        value = projected[:, 2 * width + low : 2 * width + low + HD]
        mixed = mixed_grad[:, low : low + HD]
        scores = jnp.where(live, mm_nt(key, query), -1e30)
        exponent = jnp.exp(scores - jnp.max(scores, axis=0, keepdims=True))
        probs = exponent * (1.0 / jnp.sum(exponent, axis=0, keepdims=True))
        value_grad = mm(probs.astype(BF16), mixed)
        prob_grad = mm_nt(value, mixed)
        held = probs * prob_grad
        score_grad = (held - probs * jnp.sum(held, axis=0, keepdims=True)).astype(BF16)
        grads[0].append(mm_tn(score_grad, key) * 0.125)
        grads[1].append(mm(score_grad, query))
        grads[2].append(value_grad)
    project_grad = jnp.concatenate(grads[0] + grads[1] + grads[2], axis=1).astype(BF16)
    grad = mm_nt(project_grad, weight_ref[...])
    sums_ref[0] = jnp.concatenate(
        [jnp.sum(grad, axis=0, keepdims=True), jnp.sum(grad * base, axis=0, keepdims=True)], axis=0
    )
    part_ref[0] = (middle_ref[0].astype(F32) + norm_pull(base, scale, grad * (1.0 + mod_ref[0, 1:2]))).astype(BF16)
    weight_grad = mm_tn(normed, project_grad)

    @pl.when(item == 0)
    def _():
        total_ref[...] = weight_grad

    @pl.when(item > 0)
    def _():
        total_ref[...] += weight_grad

    @pl.when(item == pl.num_programs(0) - 1)
    def _():
        if len(grad_refs) == 1:
            grad_refs[0][...] = total_ref[...].astype(BF16)
        else:
            store_blocks(*grad_refs, rank_ref[0], 0, total_ref[...].astype(BF16))


def attention_back(tokens, mod, weight, valid, projected, mixed, middle, rank, dp_size):
    items, length, width = tokens.shape
    columns = weight.shape[1]
    rows = width // dp_size
    each = pl.BlockSpec((1, length, width), lambda i: (i, 0, 0))
    if rows % 16:
        grads, blocks = (shaped(weight.shape, BF16),), (whole(weight.shape),)
    else:
        part = (dp_size // 2, 1, rows, columns)
        grads, blocks = (shaped(part, BF16),) * 2, (whole(part),) * 2
    result = call(
        functools.partial(attention_back_kernel, columns // (3 * HD)),
        (shaped(tokens.shape, BF16), shaped((items, 2, width), F32)) + grads,
        [
            pl.BlockSpec(memory_space=pltpu.SMEM),
            each,
            pl.BlockSpec((1, 6, width), lambda i: (i, 0, 0)),
            whole(weight.shape),
            pl.BlockSpec((1, length, 1), lambda i: (i, 0, 0)),
            pl.BlockSpec((1, length, columns), lambda i: (i, 0, 0)),
            pl.BlockSpec((1, 3 * length // 2, 128), lambda i: (i, 0, 0)),
            each,
        ],
        (each, pl.BlockSpec((1, 2, width), lambda i: (i, 0, 0))) + blocks,
        (rank, tokens, mod, weight, valid, projected, mixed, middle),
        grid=(items,),
        scratch=[pltpu.VMEM(weight.shape, F32)],
        flops=10_000_000_000,
        moved=12_000_000,
        name="attention_back",
    )
    if rows % 16:
        result = tuple(result[:2]) + split_blocks(result[2][None], dp_size)
    return result


def body(
    tokens,
    time_embed,
    class_embed,
    valid_mask,
    routes,
    gate_logits,
    ada_weight,
    ada_bias,
    qkv_weight,
    out_weight,
    out_bias,
    fc1_weight,
    fc1_bias,
    fc2_weight,
    fc2_bias,
    expert_in,
    expert_out,
    out_grad,
):
    items, local, width = tokens.shape
    ranks = lax.axis_size("tensor")
    rank = lax.axis_index("tensor")
    dp_size = lax.axis_size("dp")
    dp_rank = lax.axis_index("dp")
    length = local * ranks
    head_width = qkv_weight.shape[2]
    cols = ada_weight.shape[2]
    rows = width // dp_size
    start = rank * local
    bits = dp_size.bit_length() - 1
    forth = list(range(bits))
    back = [0] + list(range(bits - 1, 0, -1))
    dp_index = dp_rank.astype(I32).reshape(1)

    def own_rows(values):
        return lax.dynamic_slice_in_dim(values, start, local, 1)

    tokens_full = lax.all_gather(tokens, "tensor", axis=1, tiled=True)
    out_turned = out_weight.T
    share_rows = head_width // dp_size
    piece = lax.dynamic_slice_in_dim(out_turned, dp_rank * share_rows, share_rows, 0)
    pieces = jnp.concatenate(gather_parts(piece), axis=0)
    condition = time_embed + class_embed
    cond_wide, silu_pull = jax.vjp(jax.nn.silu, condition)
    cond_low = cond_wide.astype(BF16)
    bias_cols = lax.dynamic_slice_in_dim(ada_bias, rank * cols, cols, 1)
    modulation_local = dot("id,dsk->isk", cond_low, ada_weight) + bias_cols.astype(F32)[None]
    modulation = jnp.concatenate(gather_parts(modulation_local), axis=2)
    modulation = swing(modulation, width - rank * cols, 2)

    first = after(expert_in, modulation).transpose(1, 0, 2)
    second = after(expert_out, modulation).transpose(1, 0, 2)
    qkv = qkv_weight.reshape(width, 3 * head_width)
    chosen = routes.transpose(0, 2, 1)
    live = valid_mask[:, None, :] > 0
    expert_ids = jnp.arange(E, dtype=I32)
    named = (chosen[:, :, None, :] == expert_ids[None, None, :, None]) & live[:, :, None, :]
    choose = jnp.any(named, axis=1)
    place = jnp.arange(length, dtype=I32)
    earlier = (place[:, None] < place[None, :]).astype(BF16)
    before = dot("iet,ts->ies", choose.astype(BF16), earlier).astype(I32)
    position = jnp.sum(jnp.where(named, before[:, None], 0), axis=2)
    marks = jnp.where(live, chosen * CAP + position, -1)
    columns = marks.transpose(0, 2, 1)
    gate_soft = jax.nn.softmax(gate_logits, axis=-1)
    share = gate_soft.transpose(0, 2, 1) * live

    every = dp_gather(jnp.concatenate([pieces, cond_low], axis=0))
    cond_every = every[:, ranks * share_rows :]
    out_full = every[:, : ranks * share_rows].reshape(dp_size, ranks, share_rows, width)
    out_full = out_full.swapaxes(0, 1).reshape(ranks, head_width, width)
    out_full = swing(out_full, ranks - rank, 0)
    modulation = after(modulation, first, second, marks, columns, share)
    projected, mixed = attention(tokens_full, modulation, qkv, valid_mask[:, None, :])
    mixed_full = lax.all_gather(mixed, "tensor", axis=0)
    grad_full = lax.all_gather(after(out_grad, mixed_full), "tensor", axis=1, tiled=True)

    middle, branch_attn, normed_mlp = middle_part(
        mixed_full, out_full, out_bias[None], tokens_full, modulation
    )
    buffer, expert_act, expert_slope, hidden_act, hidden_slope, mlp_part = forward_part(
        normed_mlp, marks, share, columns, fc1_weight, fc1_bias[None], fc2_weight, first, second
    )
    mlp_sum = lax.psum_scatter(mlp_part, "tensor", scatter_dimension=1, tiled=True)

    quick = rows % 16 == 0 and dp_size == 8
    halfway = E // 2

    def start_sum(keep, send):
        return keep, dp_exchange(send, 0)

    def second_step(pair, order):
        keep, other = pair
        if not quick:
            return keep, other
        kept, sent = halve(keep, other, 0 if order[0] == 2 else 1)
        return kept, sent

    def third_step(pair, order):
        if not quick:
            return pair
        kept, sent = pair
        return halve(kept, dp_exchange(sent, order[0]), 0)

    def final_step(pair, order):
        if not quick:
            keep, other = pair
            return dp_scatter((keep.astype(F32) + other.astype(F32)).astype(BF16), order, BF16)
        kept, sent = pair
        return kept[0], dp_exchange(sent, order[1])[0]

    def whole_sum(pairs):
        if quick:
            return last(pairs, halfway)
        experts = jnp.concatenate([pair[:halfway] for pair in pairs], axis=0).swapaxes(0, 1).astype(F32)
        return [experts] + [pair[halfway].astype(F32) for pair in pairs if pair.shape[0] > halfway]

    ahead, behind = forth[1:], back[1:]
    branch_grad, branch_slot, keep, send = slots_part(
        0, halfway, marks, expert_act, dp_index, dp_size, grad=grad_full, mod=modulation, hidden=hidden_act
    )
    out_low = start_sum(keep, send)
    branch_slot, keep, send = slots_part(
        halfway, E - halfway, marks, expert_act, dp_index, dp_size, branch=branch_grad, held=branch_slot
    )
    out_high = start_sum(keep, send)
    out_low = second_step(out_low, ahead)
    out_high = second_step(out_high, behind)
    up_grad, hidden_grad, fc1_bias_part, normed_mlp_grad, gate_part = back_part(
        branch_grad,
        after(columns, out_low[1], out_high[1]),
        fc1_weight,
        fc2_weight,
        hidden_slope,
        branch_slot,
        expert_act,
        expert_slope,
        first,
        second,
    )
    out_low = third_step(out_low, ahead)
    out_high = third_step(out_high, behind)
    own = jnp.stack([start, start + local]).astype(I32)
    middle_grad, low_grad, mixed_parts, sums = second_norm_part(
        normed_mlp_grad,
        middle,
        branch_attn,
        grad_full,
        mlp_part,
        after(modulation, out_low[1], out_high[1]),
        out_full,
        own,
    )
    mixed_grad = lax.psum_scatter(mixed_parts, "tensor", scatter_dimension=0)

    marker = after(dp_index, mixed_parts)
    in_low = start_sum(
        *first_part(0, halfway, buffer, up_grad, (normed_mlp, hidden_grad), False, marker, dp_size)
    )
    in_high = start_sum(
        *first_part(halfway, E - halfway, buffer, up_grad, (low_grad, mixed_full), True, marker, dp_size)
    )
    out_low = final_step(out_low, ahead)
    out_high = final_step(out_high, behind)
    in_low = second_step(in_low, ahead)
    in_high = second_step(in_high, behind)

    gate = after(modulation, in_low[1], in_high[1], out_low, out_high)
    tokens_part, attn_sums, qkv_keep, qkv_send = attention_back(
        tokens_full, gate, qkv, valid_mask[:, :, None], projected, mixed_grad, middle_grad, dp_index, dp_size
    )
    tokens_grad = lax.psum_scatter(tokens_part, "tensor", scatter_dimension=1, tiled=True)
    qkv_other = dp_exchange(qkv_send, 0)

    sums, mlp_sum, branch_grad, gate_part, fc1_bias_part, out_low, out_high = lax.optimization_barrier(
        (sums, mlp_sum, branch_grad, gate_part, fc1_bias_part, out_low, out_high, tokens_part)
    )[:7]
    gate_mlp_grad = sums[:, 4] + jnp.sum(out_grad.astype(F32) * fc2_bias.astype(F32), axis=1)
    branch_mlp = mlp_sum.astype(F32) + fc2_bias.astype(F32)
    output = (own_rows(middle) + modulation[:, 5][:, None] * branch_mlp).astype(BF16)
    expert_out_sum, fc2_sum = whole_sum([out_low, out_high])

    def finish(keep, other, order):
        total = keep.astype(F32) + other.astype(F32)
        return dp_scatter(total.astype(BF16), order, BF16)

    in_low = third_step(in_low, ahead)
    in_high = third_step(in_high, behind)
    expert_in_sum, fc1_sum, out_sum = whole_sum([final_step(in_low, ahead), final_step(in_high, behind)])
    out_sum = swing(out_sum, rank * head_width, 1)
    out_sum = scatter_sum(
        [out_sum[:, step * head_width : (step + 1) * head_width] for step in range(ranks)]
    )
    qkv_sum = finish(qkv_keep, qkv_other, ahead)[0]
    qkv_sum = qkv_sum.astype(F32).reshape(rows, 3, head_width)

    fine = rows // ranks
    gate_part = gate_part[..., 0] + gate_part[..., 1]
    gate_turn = swing(gate_part, start, 2).reshape(items, 2, ranks, local)
    gate_turn = gate_turn.transpose(2, 0, 1, 3).reshape(ranks, -1)
    fc2_bias_part = jnp.sum(own_rows(branch_grad).astype(F32), axis=(0, 1))
    bias_parts = jnp.stack([fc2_bias_part, jnp.sum(sums[:, 3], axis=0)])
    bias_turn = bias_parts.reshape(2, dp_size, ranks, fine).transpose(2, 0, 1, 3).reshape(ranks, -1)
    bias_turn = swing(bias_turn, rank, 0)
    small = jnp.concatenate([gate_turn, bias_turn], axis=1)
    small = scatter_sum([small[step] for step in range(ranks)])
    gate_grad = small[: items * 2 * local].reshape(items, 2, local).transpose(0, 2, 1)
    bias_own = small[items * 2 * local :].reshape(2, dp_size, fine)
    gate_logits_grad = gate_grad - own_rows(gate_soft) * jnp.sum(gate_grad, axis=-1, keepdims=True)
    bias_blocks = jnp.concatenate(
        [bias_own[0], bias_own[1], fc1_bias_part.reshape(dp_size, rows)], axis=1
    )
    bias_sum = dp_scatter(to_relative(bias_blocks), forth, F32)

    modulation_part = jnp.stack(
        [attn_sums[:, 0], attn_sums[:, 1], sums[:, 2], sums[:, 0], sums[:, 1], gate_mlp_grad],
        axis=1,
    )
    modulation_part = swing(modulation_part, rank * cols, 2)
    modulation_grad = scatter_sum(
        [modulation_part[:, :, step * cols : (step + 1) * cols] for step in range(ranks)]
    ).astype(BF16)
    cond_act_grad = dot("isk,dsk->id", modulation_grad, ada_weight)
    condition_part = silu_pull(cond_act_grad)[0]
    condition_part = swing(condition_part, rank * cols, 1)
    condition_grad = scatter_sum(
        [condition_part[:, step * cols : (step + 1) * cols] for step in range(ranks)]
    )
    modulation_every = dp_gather(modulation_grad)
    cond_every = cond_every.reshape(dp_size * items, width)
    cond_rows = lax.dynamic_slice_in_dim(cond_every, dp_rank * rows, rows, 1)
    modulation_every = modulation_every.reshape(dp_size * items, 6, cols)
    ada_weight_sum = dot("id,isk->dsk", cond_rows, modulation_every)
    ada_bias_sum = jnp.sum(modulation_every.astype(F32), axis=0)
    ada_bias_sum = lax.dynamic_slice_in_dim(
        ada_bias_sum, dp_rank * (cols // dp_size), cols // dp_size, 1
    )
    return (
        output,
        tokens_grad,
        condition_grad,
        gate_logits_grad,
        ada_weight_sum,
        ada_bias_sum,
        qkv_sum,
        out_sum,
        bias_sum[fine : 2 * fine],
        fc1_sum,
        bias_sum[2 * fine :],
        fc2_sum,
        bias_sum[:fine],
        expert_in_sum,
        expert_out_sum,
    )


def solution(mesh):
    in_specs = (
        P("dp", "tensor", None),
        P("dp", None),
        P("dp", None),
        P("dp", None),
        P("dp", None, None),
        P("dp", None, None),
        P(None, None, "tensor"),
        P(),
        P(None, None, "tensor"),
        P(None, "tensor"),
        P(),
        P(None, "tensor"),
        P("tensor"),
        P(None, "tensor"),
        P(),
        P(None, None, "tensor"),
        P(None, None, "tensor"),
        P("dp", "tensor", None),
    )
    out_specs = (
        P("dp", "tensor", None),
        P("dp", "tensor", None),
        P("dp", "tensor"),
        P("dp", "tensor", None),
        P("dp", None, "tensor"),
        P(None, ("tensor", "dp")),
        P("dp", None, "tensor"),
        P("dp", "tensor"),
        P(("dp", "tensor")),
        P("dp", "tensor"),
        P(("tensor", "dp")),
        P("dp", "tensor"),
        P(("dp", "tensor")),
        P("dp", None, "tensor"),
        P("dp", None, "tensor"),
    )
    return jax.shard_map(body, mesh=mesh, in_specs=in_specs, out_specs=out_specs, check_vma=False)
```

```python
import functools

import jax
import jax.numpy as jnp
from jax import lax
from jax.experimental import pallas as pl
from jax.experimental.pallas import tpu as pltpu
from jax.sharding import PartitionSpec as P

HD = 64
E = 8
CAP = 192
F32 = jnp.float32
BF16 = jnp.bfloat16
I32 = jnp.int32
VMEM_BYTES = 56 * 1024 * 1024


def dot(spec, left, right):
    return jnp.einsum(spec, left, right, preferred_element_type=F32)


def mm(left, right):
    return jnp.dot(left, right, preferred_element_type=F32)


def mm_nt(left, right):
    return lax.dot_general(left, right, (((1,), (1,)), ((), ())), preferred_element_type=F32)


def mm_tn(left, right):
    return lax.dot_general(left, right, (((0,), (0,)), ((), ())), preferred_element_type=F32)


def after(values, *others):
    return lax.optimization_barrier((values,) + others)[0]


def from_rank(values, step):
    size = lax.axis_size("tensor")
    return lax.ppermute(values, "tensor", [(i, (i - step) % size) for i in range(size)])


def to_rank(values, step):
    size = lax.axis_size("tensor")
    return lax.ppermute(values, "tensor", [(i, (i + step) % size) for i in range(size)])


def gather_parts(values):
    size = lax.axis_size("tensor")
    return [values] + [from_rank(values, step) for step in range(1, size)]


def scatter_sum(parts):
    total = parts[0].astype(F32)
    for step in range(1, len(parts)):
        total = total + to_rank(parts[step], step).astype(F32)
    return total


def swing(values, amount, axis):
    twice = jnp.concatenate([values, values], axis=axis)
    return lax.dynamic_slice_in_dim(twice, amount, values.shape[axis], axis)


def dp_exchange(values, bit):
    size = lax.axis_size("dp")
    return lax.ppermute(values, "dp", [(i, i ^ (1 << bit)) for i in range(size)])


def to_relative(blocks):
    size = lax.axis_size("dp")
    rank = lax.axis_index("dp")
    for bit in range(size.bit_length() - 1):
        paired = blocks.reshape((size >> (bit + 1), 2, 1 << bit) + blocks.shape[1:])
        swapped = jnp.where(((rank >> bit) & 1) == 0, paired, paired[:, ::-1])
        blocks = swapped.reshape(blocks.shape)
    return blocks


def dp_scatter(blocks, order, kind):
    current = blocks.reshape((2,) * len(order) + blocks.shape[1:])
    left = sorted(order, reverse=True)
    for bit in order:
        axis = left.index(bit)
        keep = lax.index_in_dim(current, 0, axis, keepdims=False)
        send = lax.index_in_dim(current, 1, axis, keepdims=False)
        other = dp_exchange(send, bit)
        current = (keep.astype(F32) + other.astype(F32)).astype(kind)
        left.pop(axis)
    return current


def dp_gather(values, held=None, stage=-1):
    size = lax.axis_size("dp")
    rank = lax.axis_index("dp")
    current = values[None]
    for bit in range(size.bit_length() - 1):
        if bit == stage:
            current = after(current, held)
        other = dp_exchange(current, bit)
        mine = (rank >> bit) & 1
        low = jnp.where(mine == 0, current, other)
        high = jnp.where(mine == 0, other, current)
        current = jnp.concatenate([low, high], axis=0)
    return current


def norm_parts(values):
    center = values - jnp.mean(values, axis=-1, keepdims=True)
    spread = jnp.mean(center * center, axis=-1, keepdims=True)
    scale = lax.rsqrt(spread + 1e-06)
    return center * scale, scale


def norm_pull(normed, scale, grad):
    return scale * (
        grad
        - jnp.mean(grad, axis=-1, keepdims=True)
        - normed * jnp.mean(grad * normed, axis=-1, keepdims=True)
    )


def gelu_both(values):
    factor = 0.7978845608028654
    square = values * values
    inner = jnp.tanh(values * (factor + (factor * 0.044715) * square))
    half = 0.5 + 0.5 * inner
    slope = half + values * (half * (1.0 - inner)) * (factor + (factor * 0.134145) * square)
    return values * half, slope


def call(kernel, out_shape, in_specs, out_specs, args, grid=(), scratch=(), flops=0, moved=0, name=None, alias=None):
    return pl.pallas_call(
        kernel,
        out_shape=out_shape,
        grid=grid,
        in_specs=in_specs,
        out_specs=out_specs,
        scratch_shapes=scratch,
        input_output_aliases=alias or {},
        compiler_params=pltpu.CompilerParams(
            vmem_limit_bytes=VMEM_BYTES, dimension_semantics=("arbitrary",) * len(grid)
        ),
        cost_estimate=pl.CostEstimate(flops=flops, bytes_accessed=moved, transcendentals=0),
        name=name,
    )(*args)


def whole(shape):
    zeros = (0,) * len(shape)
    return pl.BlockSpec(shape, lambda *_: zeros)


def once(shape):
    zeros = (0,) * len(shape)
    return pl.BlockSpec(shape, lambda *_: zeros, pipeline_mode=pl.Buffered(1))


def shaped(shape, kind):
    return jax.ShapeDtypeStruct(shape, kind)


def pack_heads(values):
    half = values.shape[0] // 2
    rest = jnp.concatenate([values[:half, 128:], values[half:, 128:]], axis=1)
    return jnp.concatenate([values[:, :128], rest], axis=0)


def unpack_heads(values):
    half = values.shape[0] // 3
    rest = values[2 * half :]
    upper = jnp.concatenate([values[:half], rest[:, :64]], axis=1)
    lower = jnp.concatenate([values[half : 2 * half], rest[:, 64:]], axis=1)
    return jnp.concatenate([upper, lower], axis=0)


def attention_kernel(heads, tokens_ref, mod_ref, weight_ref, valid_ref, projected_ref, mixed_ref):
    width = heads * HD
    normed, _ = norm_parts(tokens_ref[0].astype(F32))
    normed = normed * (1.0 + mod_ref[0, 1:2]) + mod_ref[0, 0:1]
    projected = mm(normed.astype(BF16), weight_ref[...]).astype(BF16)
    projected_ref[0] = projected
    live = valid_ref[0] > 0
    mixed = []
    for head in range(heads):
        low = head * HD
        query = projected[:, low : low + HD] * jnp.asarray(0.125, BF16)
        key = projected[:, width + low : width + low + HD]
        value = projected[:, 2 * width + low : 2 * width + low + HD]
        scores = jnp.where(live, mm_nt(query, key), -1e30)
        exponent = jnp.exp(scores - jnp.max(scores, axis=1, keepdims=True))
        probs = exponent * (1.0 / jnp.sum(exponent, axis=1, keepdims=True))
        mixed.append(mm(probs.astype(BF16), value))
    mixed_ref[0] = pack_heads(jnp.concatenate(mixed, axis=1).astype(BF16))


def attention(tokens, mod, weight, valid):
    items, length, width = tokens.shape
    head_width = weight.shape[1] // 3
    return call(
        functools.partial(attention_kernel, head_width // HD),
        (shaped((items, length, 3 * head_width), BF16), shaped((items, 3 * length // 2, 128), BF16)),
        [
            pl.BlockSpec((1, length, width), lambda i: (i, 0, 0)),
            pl.BlockSpec((1, 6, width), lambda i: (i, 0, 0)),
            whole(weight.shape),
            pl.BlockSpec((1, 1, length), lambda i: (i, 0, 0)),
        ],
        (
            pl.BlockSpec((1, length, 3 * head_width), lambda i: (i, 0, 0)),
            pl.BlockSpec((1, 3 * length // 2, 128), lambda i: (i, 0, 0)),
        ),
        (tokens, mod, weight, valid),
        grid=(items,),
        flops=8_000_000_000,
        moved=6_000_000,
        name="attention_forward",
    )


def middle_kernel(ranks, mixed_ref, rest_ref, weight_ref, bias_ref, tokens_ref, mod_ref, middle_ref, branch_ref, normed_ref):
    upper = pl.program_id(1) == 0
    branch = bias_ref[...].astype(F32)
    for rank in range(ranks):
        rest = jnp.where(upper, rest_ref[rank, 0, :, :64], rest_ref[rank, 0, :, 64:])
        branch = branch + mm(jnp.concatenate([mixed_ref[rank, 0], rest], axis=1), weight_ref[rank])
    middle = tokens_ref[0].astype(F32) + mod_ref[0, 2:3] * branch
    middle_ref[0] = middle
    branch_ref[0] = branch.astype(BF16)
    normed, _ = norm_parts(middle)
    normed_ref[0] = (normed * (1.0 + mod_ref[0, 4:5]) + mod_ref[0, 3:4]).astype(BF16)


def middle_part(mixed, weight, bias, tokens, mod):
    items, length, width = tokens.shape
    ranks = mixed.shape[0]
    block = length // 2
    rows = pl.BlockSpec((1, block, width), lambda i, r: (i, r, 0))
    return call(
        functools.partial(middle_kernel, ranks),
        (
            shaped(tokens.shape, F32),
            shaped(tokens.shape, BF16),
            shaped(tokens.shape, BF16),
        ),
        [
            pl.BlockSpec((ranks, 1, block, 128), lambda i, r: (0, i, r, 0)),
            pl.BlockSpec((ranks, 1, block, 128), lambda i, r: (0, i, 2, 0)),
            whole(weight.shape),
            whole(bias.shape),
            rows,
            pl.BlockSpec((1, 6, width), lambda i, r: (i, 0, 0)),
        ],
        (rows, rows, rows),
        (mixed, mixed, weight, bias, tokens, mod),
        grid=(items, 2),
        flops=3_000_000_000,
        moved=12_000_000,
        name="middle",
    )


def hot_rows(expert, marks):
    slots = lax.broadcasted_iota(I32, (CAP, marks.shape[1]), 0) + expert * CAP
    return slots == marks[0:1], slots == marks[1:2]


def as_hot(mask):
    return jnp.where(mask, 1.0, 0.0).astype(BF16)


def forward_kernel(
    items,
    normed_ref,
    marks_ref,
    share_ref,
    columns_ref,
    fc1_ref,
    bias_ref,
    fc2_ref,
    first_ref,
    second_ref,
    buffer_ref,
    act_ref,
    slope_ref,
    hidden_ref,
    hidden_slope_ref,
    out_ref,
    slots_ref,
):
    expert = pl.program_id(0)
    length = normed_ref.shape[1]

    @pl.when(expert == 0)
    def _():
        for item in range(items):
            hidden = mm(normed_ref[item], fc1_ref[...]) + bias_ref[...].astype(F32)
            value, slope = gelu_both(hidden)
            hidden_ref[item] = value.astype(BF16)
            hidden_slope_ref[item] = slope.astype(BF16)

    shares = []
    for item in range(items):
        one, two = hot_rows(expert, marks_ref[item])
        buffer_ref[0, item * CAP : (item + 1) * CAP] = mm(as_hot(one | two), normed_ref[item]).astype(BF16)
        held = jnp.where(one, share_ref[item, 0:1], 0.0) + jnp.where(two, share_ref[item, 1:2], 0.0)
        shares.append(jnp.sum(held, axis=1, keepdims=True))
    share = jnp.concatenate(shares, axis=0)
    value, slope = gelu_both(mm(buffer_ref[0], first_ref[0]))
    act_ref[0] = (share * value).astype(BF16)
    slope_ref[0] = (share * slope).astype(BF16)
    returned = mm_nt(act_ref[0], second_ref[0]).astype(BF16)
    place = pl.ds(pl.multiple_of(expert * CAP, 64), CAP)
    for item in range(items):
        slots_ref[item, place] = returned[item * CAP : (item + 1) * CAP]

    @pl.when(expert == E - 1)
    def _():
        lanes = lax.broadcasted_iota(I32, (length, E * CAP), 1)
        for item in range(items):
            marks = columns_ref[item]
            hot = as_hot((lanes == marks[:, 0:1]) | (lanes == marks[:, 1:2]))
            total = mm(hot, slots_ref[item]) + mm_nt(hidden_ref[item], fc2_ref[...])
            out_ref[item] = total.astype(BF16)


def forward_part(normed, marks, share, columns, fc1, bias, fc2, first, second):
    items, length, width = normed.shape
    units = fc1.shape[1]
    slots = items * CAP
    inner = pl.BlockSpec((1, slots, units), lambda e: (e, 0, 0))
    weight = pl.BlockSpec((1, width, units), lambda e: (e, 0, 0))
    hidden = (items, length, units)
    return call(
        functools.partial(forward_kernel, items),
        (
            shaped((E, slots, width), BF16),
            shaped((E, slots, units), BF16),
            shaped((E, slots, units), BF16),
            shaped(hidden, BF16),
            shaped(hidden, BF16),
            shaped(normed.shape, BF16),
        ),
        [
            whole(normed.shape),
            whole(marks.shape),
            whole(share.shape),
            whole(columns.shape),
            whole(fc1.shape),
            whole(bias.shape),
            whole(fc2.shape),
            weight,
            weight,
        ],
        (
            pl.BlockSpec((1, slots, width), lambda e: (e, 0, 0)),
            inner,
            inner,
            whole(hidden),
            whole(hidden),
            whole(normed.shape),
        ),
        (normed, marks, share, columns, fc1, bias, fc2, first, second),
        grid=(E,),
        scratch=[pltpu.VMEM((items, E * CAP, width), BF16)],
        flops=14_000_000_000,
        moved=40_000_000,
        name="mlp_forward",
    )


def store_blocks(keep_ref, send_ref, rank, index, grad):
    blocks, rows = 2 * keep_ref.shape[0], keep_ref.shape[2]
    for pair in range(blocks // 2):
        place = lax.bitwise_xor(rank // 2, pair)
        low = grad[2 * pair * rows : (2 * pair + 1) * rows]
        high = grad[(2 * pair + 1) * rows : (2 * pair + 2) * rows]
        odd = rank % 2 == 1

        @pl.when(odd)
        def _():
            keep_ref[place, index] = high
            send_ref[place, index] = low

        @pl.when(jnp.logical_not(odd))
        def _():
            keep_ref[place, index] = low
            send_ref[place, index] = high


def split_blocks(grads, dp_size):
    count, width, units = grads.shape
    blocks = to_relative(grads.reshape(count, dp_size, width // dp_size, units).swapaxes(0, 1))
    pairs = blocks.reshape((dp_size // 2, 2) + blocks.shape[1:])
    return pairs[:, 0], pairs[:, 1]


def call_grads(kernel, steps, rank, dp_size, shape, outs, out_specs, specs, args, alias=None, weight=20_000_000):
    width, units = shape
    rows = width // dp_size
    smooth = rows % 16 == 0
    block = pl.BlockSpec((dp_size // 2, 1, rows, units), lambda e: (0, e, 0, 0))
    part = shaped((dp_size // 2, steps, rows, units), BF16)
    return call(
        kernel,
        outs + ((part, part) if smooth else ()),
        [pl.BlockSpec(memory_space=pltpu.SMEM)] + specs,
        out_specs + ((block, block) if smooth else ()),
        (rank,) + args,
        grid=(steps,),
        flops=0,
        moved=weight,
        name="weight_grads",
        alias=alias,
    )


def expert_block(start, count, shape):
    return pl.BlockSpec((1,) + shape, lambda e: (jnp.minimum(e, count - 1) + start, 0, 0))


def slots_kernel(items, start, count, rank_ref, marks_ref, act_ref, *refs):
    expert = pl.program_id(0)
    if start == 0:
        grad_ref, mod_ref, hidden_ref, branch_ref, slots_ref, *grad_refs = refs

        @pl.when(expert == 0)
        def _():
            for item in range(items):
                branch_ref[item] = (grad_ref[item].astype(F32) * mod_ref[item, 5:6]).astype(BF16)

    else:
        branch_ref, _, slots_ref, *grad_refs = refs

    @pl.when(expert < count)
    def _():
        for item in range(items):
            one, two = hot_rows(expert + start, marks_ref[item])
            slots_ref[0, item * CAP : (item + 1) * CAP] = mm(as_hot(one | two), branch_ref[item]).astype(BF16)
        if grad_refs:
            store_blocks(*grad_refs, rank_ref[0], 0, mm_tn(slots_ref[0], act_ref[0]).astype(BF16))

    if start == 0 and grad_refs:

        @pl.when(expert == count)
        def _():
            total = mm_tn(branch_ref[0], hidden_ref[0])
            for item in range(1, items):
                total = total + mm_tn(branch_ref[item], hidden_ref[item])
            store_blocks(*grad_refs, rank_ref[0], 0, total.astype(BF16))


def slots_part(start, count, marks, act, rank, dp_size, grad=None, mod=None, hidden=None, branch=None, held=None):
    items, length, width = (branch if grad is None else grad).shape
    units = act.shape[2]
    slots = items * CAP
    all_rows = whole((items, length, width))
    each = expert_block(start, count, (slots, width))
    filled = shaped((E, slots, width), BF16)
    if start == 0:
        specs, more = [all_rows, whole(mod.shape), whole(hidden.shape)], (grad, mod, hidden)
        outs, out_specs, alias = (shaped(grad.shape, BF16), filled), (all_rows, each), {}
    else:
        specs, more = [all_rows, pl.BlockSpec(memory_space=pl.ANY)], (branch, held)
        outs, out_specs, alias = (filled,), (each,), {4: 0}
    result = call_grads(
        functools.partial(slots_kernel, items, start, count),
        count + (start == 0),
        rank,
        dp_size,
        (width, units),
        outs,
        out_specs,
        [whole(marks.shape), expert_block(start, count, (slots, units))] + specs,
        (marks, act) + more,
        alias,
    )
    if (width // dp_size) % 16:
        picked = slice(start, start + count)
        grads = dot("ecd,ecf->edf", result[-1][picked], act[picked])
        if start == 0:
            grads = jnp.concatenate([grads, dot("isd,isf->df", result[0], hidden)[None]], axis=0)
        result = tuple(result) + split_blocks(grads.astype(BF16), dp_size)
    return result


def out_grad_kernel(rank_ref, low_ref, mixed_ref, *out_refs):
    ranks = mixed_ref.shape[0]
    for rank in range(ranks):
        total = mm_tn(unpack_heads(mixed_ref[rank, 0]), low_ref[0])
        for item in range(1, low_ref.shape[0]):
            total = total + mm_tn(unpack_heads(mixed_ref[rank, item]), low_ref[item])
        total = total.astype(BF16)
        for step, out_ref in enumerate(out_refs):

            @pl.when(lax.rem(rank - rank_ref[0] + ranks, ranks) == step)
            def _():
                out_ref[...] = total


def out_grad_parts(low, mixed, head_width, rank):
    ranks, width = mixed.shape[0], low.shape[2]
    vmem = pl.BlockSpec(memory_space=pltpu.VMEM)
    return call(
        out_grad_kernel,
        (shaped((head_width, width), BF16),) * ranks,
        [pl.BlockSpec(memory_space=pltpu.SMEM), vmem, vmem],
        (vmem,) * ranks,
        (rank, low, mixed),
        flops=0,
        moved=4_000_000,
        name="out_weight_grad",
    )


def late_kernel(rank_ref, qkv_ref, *refs):
    *out_refs, keep_ref, send_ref = refs
    total = sum(out_ref[...].astype(F32) for out_ref in out_refs)
    grad = jnp.concatenate([qkv_ref[...], total.T], axis=1)
    store_blocks(keep_ref, send_ref, rank_ref[0], 0, grad.astype(BF16))


def late_part(qkv_grad, out_parts, rank, dp_size):
    width = qkv_grad.shape[0]
    columns = qkv_grad.shape[1] + out_parts[0].shape[0]
    rows = width // dp_size
    if rows % 16:
        total = sum(part.astype(F32) for part in out_parts)
        grads = jnp.concatenate([qkv_grad, total.T], axis=1).astype(BF16)
        return split_blocks(grads[None], dp_size)
    part = shaped((dp_size // 2, 1, rows, columns), BF16)
    vmem = pl.BlockSpec(memory_space=pltpu.VMEM)
    return call(
        late_kernel,
        (part, part),
        [pl.BlockSpec(memory_space=pltpu.SMEM), vmem] + [vmem] * len(out_parts),
        (vmem, vmem),
        (rank, qkv_grad, *out_parts),
        flops=0,
        moved=0,
        name="late_blocks",
    )


def first_kernel(count, rank_ref, left_ref, right_ref, *refs):
    expert = pl.program_id(0)
    grad_refs = refs[-2:]

    @pl.when(expert < count)
    def _():
        store_blocks(*grad_refs, rank_ref[0], 0, mm_tn(left_ref[0], right_ref[0]).astype(BF16))

    if len(refs) > 2:
        dense_left_ref, dense_right_ref = refs[:2]

        @pl.when(expert == count)
        def _():
            total = mm_tn(dense_left_ref[0], dense_right_ref[0])
            for item in range(1, dense_left_ref.shape[0]):
                total = total + mm_tn(dense_left_ref[item], dense_right_ref[item])
            store_blocks(*grad_refs, rank_ref[0], 0, total.astype(BF16))


def first_part(start, count, left, right, rank, dp_size, dense=()):
    _, slots, width = left.shape
    units = right.shape[2]
    rows = width // dp_size
    if rows % 16:
        picked = slice(start, start + count)
        grads = dot("ecd,ecf->edf", left[picked], right[picked])
        if dense:
            grads = jnp.concatenate([grads, dot("isd,isf->df", *dense)[None]], axis=0)
        return split_blocks(grads.astype(BF16), dp_size)
    return call_grads(
        functools.partial(first_kernel, count),
        count + (1 if dense else 0),
        rank,
        dp_size,
        (width, units),
        (),
        (),
        [expert_block(start, count, (slots, width)), expert_block(start, count, (slots, units))]
        + [whole(value.shape) for value in dense],
        (left, right) + tuple(dense),
        weight=20_000_000 if dense else 4_000_000,
    )


def halve_kernel(first, keep_ref, other_ref, kept_ref, sent_ref):
    total = (keep_ref[...].astype(F32) + other_ref[...].astype(F32)).astype(BF16)
    kept_ref[...] = total[0:1] if first else total[:, 0:1]
    sent_ref[...] = total[1:2] if first else total[:, 1:2]


def halve(keep, other, axis, weight):
    lead = keep.shape[0]
    rest = keep.shape[1:]
    zeros = (0,) * len(rest)
    if lead == 2:
        shape, outer, axis = (2, 1) + rest, 1, 0
    else:
        shape, outer = (2, lead // 2) + rest, lead // 2
    if axis == 0:
        block, result = (2, 1) + rest, (1, outer) + rest
        spec = pl.BlockSpec(block, lambda i: (0, i) + zeros)
        out = pl.BlockSpec((1, 1) + rest, lambda i: (0, i) + zeros)
        steps = outer
    else:
        block, result = (1, 2) + rest, (2, 1) + rest
        spec = pl.BlockSpec(block, lambda i: (i, 0) + zeros)
        out = pl.BlockSpec((1, 1) + rest, lambda i: (i, 0) + zeros)
        steps = 2
    kept, sent = call(
        functools.partial(halve_kernel, axis == 0),
        (shaped(result, BF16),) * 2,
        [spec, spec],
        (out, out),
        (keep.reshape(shape), other.reshape(shape)),
        grid=(steps,),
        flops=0,
        moved=weight,
        name="halve",
    )
    return kept.reshape((lead // 2,) + rest), sent.reshape((lead // 2,) + rest)


def last_kernel(halfway, counts, *refs):
    inputs, (out_ref, *dense_refs) = refs[: 2 * len(counts)], refs[2 * len(counts) :]
    dense = iter(dense_refs)
    place = 0
    for group, size in enumerate(counts):
        keep_ref, other_ref = inputs[2 * group], inputs[2 * group + 1]
        for index in range(size):
            total = keep_ref[index].astype(F32) + other_ref[index].astype(F32)
            if index < halfway:
                out_ref[:, place] = total
                place += 1
            else:
                next(dense)[...] = total


def last(pairs, halfway):
    counts = [keep.shape[0] for keep, _ in pairs]
    rows, units = pairs[0][0].shape[1:]
    args = [value for pair in pairs for value in pair]
    vmem = pl.BlockSpec(memory_space=pltpu.VMEM)
    extra = sum(size > halfway for size in counts)
    return call(
        functools.partial(last_kernel, halfway, counts),
        (shaped((rows, halfway * len(counts), units), F32),) + (shaped((rows, units), F32),) * extra,
        [vmem] * len(args),
        (vmem,) * (1 + extra),
        tuple(args),
        flops=sum(counts) * rows * units,
        moved=8 * sum(counts) * rows * units,
        name="last_sum",
    )


def back_kernel(
    items,
    ranks,
    own_ref,
    branch_ref,
    columns_ref,
    fc1_ref,
    fc2_ref,
    hidden_slope_ref,
    mod_ref,
    weight_ref,
    slots_ref,
    act_ref,
    slope_ref,
    first_ref,
    second_ref,
    middle_hbm,
    attn_hbm,
    cotangent_hbm,
    mlp_hbm,
    up_grad_ref,
    hidden_grad_ref,
    bias_grad_ref,
    dots_ref,
    middle_grad_ref,
    low_ref,
    mixed_ref,
    sums_ref,
    grad_ref,
    held_ref,
    middle_ref,
    attn_ref,
    cotangent_ref,
    mlp_ref,
    sems,
):
    expert = pl.program_id(0)
    length = branch_ref.shape[1]
    pairs = [(middle_hbm, middle_ref), (attn_hbm, attn_ref), (cotangent_hbm, cotangent_ref), (mlp_hbm, mlp_ref)]
    copies = [pltpu.make_async_copy(far, near, sems.at[index]) for index, (far, near) in enumerate(pairs)]

    @pl.when(expert == 0)
    def _():
        for copy in copies:
            copy.start()
        total = jnp.zeros(bias_grad_ref.shape, F32)
        for item in range(items):
            grad = mm(branch_ref[item], fc2_ref[...]) * hidden_slope_ref[item].astype(F32)
            grad = grad.astype(BF16)
            hidden_grad_ref[item] = grad
            total = total + jnp.sum(grad.astype(F32), axis=0, keepdims=True)
            grad_ref[item] = mm_nt(grad, fc1_ref[...])
        bias_grad_ref[...] = total

    pulled = mm(slots_ref[0], second_ref[0])
    up_grad = (pulled * slope_ref[0].astype(F32)).astype(BF16)
    up_grad_ref[0] = up_grad
    total = jnp.sum(act_ref[0].astype(F32) * pulled, axis=1, keepdims=True)
    high = total.astype(BF16).astype(F32)
    lane = lax.broadcasted_iota(I32, (items * CAP, 128), 1)
    split = jnp.where(lane == 0, high, jnp.where(lane == 1, total - high, 0.0)).astype(BF16)
    back = mm_nt(up_grad, first_ref[0]).astype(BF16)
    place = pl.ds(pl.multiple_of(expert * CAP, 64), CAP)
    for item in range(items):
        held_ref[item, place] = back[item * CAP : (item + 1) * CAP]
        dots_ref[item, place] = split[item * CAP : (item + 1) * CAP]

    @pl.when(expert == E - 1)
    def _():
        for copy in copies:
            copy.wait()
        block = length // 2
        lanes = lax.broadcasted_iota(I32, (block, E * CAP), 1)
        for item in range(items):
            sums = []
            for step in range(2):
                part = slice(step * block, (step + 1) * block)
                marks = columns_ref[item, part]
                hot = as_hot((lanes == marks[:, 0:1]) | (lanes == marks[:, 1:2]))
                grad = grad_ref[item, part] + mm(hot, held_ref[item])
                normed, scale = norm_parts(middle_ref[item, part])
                pulled = norm_pull(normed, scale, grad * (1.0 + mod_ref[item, 4:5]))
                at = lax.broadcasted_iota(I32, (block, 1), 0) + step * block
                own = (at >= own_ref[0]) & (at < own_ref[1])
                cotangent = cotangent_ref[item, part].astype(F32)
                pulled = pulled + jnp.where(own, cotangent, 0.0)
                middle_grad_ref[item, part] = pulled.astype(BF16)
                low = (pulled * mod_ref[item, 2:3]).astype(BF16)
                low_ref[item, part] = low
                for rank in range(ranks):
                    mixed = mm_nt(low, weight_ref[rank]).astype(BF16)
                    mixed_ref[rank, item, part] = mixed[:, :128]
                    mixed_ref[rank, item, 2 * block :, step * 64 : (step + 1) * 64] = mixed[:, 128:]
                terms = [
                    grad,
                    grad * normed,
                    pulled * attn_ref[item, part].astype(F32),
                    low.astype(F32),
                    cotangent * mlp_ref[item, part].astype(F32),
                ]
                sums.append(jnp.concatenate([jnp.sum(term, axis=0, keepdims=True) for term in terms], axis=0))
            sums_ref[item] = sums[0] + sums[1]


def back_part(
    branch, columns, fc1, fc2, hidden_slope, branch_slot, act, slope, first, second, middle, attn, cotangent, mlp, mod, weight, own
):
    items, length, width = branch.shape
    ranks = weight.shape[0]
    units = fc1.shape[1]
    slots = items * CAP
    inner = pl.BlockSpec((1, slots, units), lambda e: (e, 0, 0))
    expert_weight = pl.BlockSpec((1, width, units), lambda e: (e, 0, 0))
    hidden = (items, length, units)
    packed = (ranks, items, 3 * length // 2, 128)
    far = pl.BlockSpec(memory_space=pl.ANY)
    return call(
        functools.partial(back_kernel, items, ranks),
        (
            shaped((E, slots, units), BF16),
            shaped(hidden, BF16),
            shaped((1, units), F32),
            shaped((items, E * CAP, 128), BF16),
            shaped(branch.shape, BF16),
            shaped(branch.shape, BF16),
            shaped(packed, BF16),
            shaped((items, 5, width), F32),
        ),
        [
            pl.BlockSpec(memory_space=pltpu.SMEM),
            once(branch.shape),
            once(columns.shape),
            once(fc1.shape),
            once(fc2.shape),
            once(hidden),
            once(mod.shape),
            once(weight.shape),
            pl.BlockSpec((1, slots, width), lambda e: (e, 0, 0)),
            inner,
            inner,
            expert_weight,
            expert_weight,
            far,
            far,
            far,
            far,
        ],
        (
            inner,
            whole(hidden),
            whole((1, units)),
            whole((items, E * CAP, 128)),
            whole(branch.shape),
            whole(branch.shape),
            whole(packed),
            whole((items, 5, width)),
        ),
        (own, branch, columns, fc1, fc2, hidden_slope, mod, weight, branch_slot, act, slope, first, second, middle, attn, cotangent, mlp),
        grid=(E,),
        scratch=[
            pltpu.VMEM(branch.shape, F32),
            pltpu.VMEM((items, E * CAP, width), BF16),
            pltpu.VMEM(middle.shape, F32),
            pltpu.VMEM(attn.shape, BF16),
            pltpu.VMEM(cotangent.shape, BF16),
            pltpu.VMEM(mlp.shape, BF16),
            pltpu.SemaphoreType.DMA((4,)),
        ],
        flops=14_000_000_000,
        moved=50_000_000,
        name="mlp_back",
    )


def tail_kernel(
    ranks,
    rank_ref,
    dots_ref,
    marks_ref,
    sums_ref,
    attn_ref,
    bias_ref,
    grad_ref,
    bias_grad_ref,
    packed_ref,
):
    items, local, width = grad_ref.shape
    cols = width // ranks
    packed_ref[...] = jnp.zeros(packed_ref.shape, F32)
    bias = bias_ref[...].astype(F32)
    slots = lax.broadcasted_iota(I32, (dots_ref.shape[1], marks_ref.shape[2]), 0)
    gates, mods = [], []
    for item in range(items):
        for choice in range(2):
            both = mm_tn(dots_ref[item], as_hot(slots == marks_ref[item, choice : choice + 1]))
            gates.append(both[0:1] + both[1:2])
        sums = sums_ref[item]
        local_sum = jnp.sum(grad_ref[item].astype(F32), axis=0, keepdims=True)
        mods += [attn_ref[item], sums[2:3], sums[0:2], sums[4:5] + local_sum * bias]
    bias_grad = bias_grad_ref[...]
    out_bias_grad = jnp.zeros((1, width), F32)
    for item in range(items):
        out_bias_grad = out_bias_grad + sums_ref[item, 3:4]
    mod_grads = jnp.concatenate(mods, axis=0)
    gates = jnp.concatenate(gates, axis=0)
    six, two = 6 * items, 2 * items
    for rank in range(ranks):
        place = lax.rem(rank - rank_ref[0] + ranks, ranks)
        packed_ref[place, 0:six, 0:cols] = mod_grads[:, rank * cols : (rank + 1) * cols]
        packed_ref[place, six : six + two, 0:local] = gates[:, rank * local : (rank + 1) * local]
        for cut in range(width // 256):
            part = slice(cut * 256, (cut + 1) * 256)
            row = six + two + 2 * cut
            packed_ref[place, row : row + 1] = bias_grad[:, part]
            packed_ref[place, row + 1 : row + 2] = out_bias_grad[:, part]


def tail_part(ranks, rank, dots, marks, sums, attn_sums, bias, grad, bias_grad):
    items, local, width = grad.shape
    packed_rows = 8 * items + 2 * (width // 256)
    vmem = pl.BlockSpec(memory_space=pltpu.VMEM)
    return call(
        functools.partial(tail_kernel, ranks),
        shaped((ranks, packed_rows, 256), F32),
        [pl.BlockSpec(memory_space=pltpu.SMEM)] + [vmem] * 7,
        vmem,
        (rank, dots, marks, sums, attn_sums, bias, grad, bias_grad),
        flops=0,
        moved=0,
        name="tail",
    )


def attention_back_kernel(
    heads, tokens_ref, mod_ref, weight_ref, valid_ref, projected_ref, mixed_ref, middle_ref, part_ref, sums_ref, total_ref
):
    item = pl.program_id(0)
    width = heads * HD
    base, scale = norm_parts(tokens_ref[0].astype(F32))
    normed = (base * (1.0 + mod_ref[0, 1:2]) + mod_ref[0, 0:1]).astype(BF16)
    projected = projected_ref[0]
    grads = [[], [], []]
    live = valid_ref[0] > 0
    mixed_grad = unpack_heads(mixed_ref[0])
    for head in range(heads):
        low = head * HD
        query = projected[:, low : low + HD] * jnp.asarray(0.125, BF16)
        key = projected[:, width + low : width + low + HD]
        value = projected[:, 2 * width + low : 2 * width + low + HD]
        mixed = mixed_grad[:, low : low + HD]
        scores = jnp.where(live, mm_nt(key, query), -1e30)
        exponent = jnp.exp(scores - jnp.max(scores, axis=0, keepdims=True))
        probs = exponent * (1.0 / jnp.sum(exponent, axis=0, keepdims=True))
        value_grad = mm(probs.astype(BF16), mixed)
        prob_grad = mm_nt(value, mixed)
        held = probs * prob_grad
        score_grad = (held - probs * jnp.sum(held, axis=0, keepdims=True)).astype(BF16)
        grads[0].append(mm_tn(score_grad, key) * 0.125)
        grads[1].append(mm(score_grad, query))
        grads[2].append(value_grad)
    project_grad = jnp.concatenate(grads[0] + grads[1] + grads[2], axis=1).astype(BF16)
    grad = mm_nt(project_grad, weight_ref[...])
    sums_ref[0] = jnp.concatenate(
        [jnp.sum(grad, axis=0, keepdims=True), jnp.sum(grad * base, axis=0, keepdims=True)], axis=0
    )
    part_ref[0] = (middle_ref[0].astype(F32) + norm_pull(base, scale, grad * (1.0 + mod_ref[0, 1:2]))).astype(BF16)
    weight_grad = mm_tn(normed, project_grad)

    @pl.when(item == 0)
    def _():
        total_ref[...] = weight_grad

    @pl.when(item > 0)
    def _():
        total_ref[...] += weight_grad


def attention_back(tokens, mod, weight, valid, projected, mixed, middle):
    items, length, width = tokens.shape
    columns = weight.shape[1]
    each = pl.BlockSpec((1, length, width), lambda i: (i, 0, 0))
    return call(
        functools.partial(attention_back_kernel, columns // (3 * HD)),
        (shaped(tokens.shape, BF16), shaped((items, 2, width), F32), shaped(weight.shape, F32)),
        [
            each,
            pl.BlockSpec((1, 6, width), lambda i: (i, 0, 0)),
            whole(weight.shape),
            pl.BlockSpec((1, length, 1), lambda i: (i, 0, 0)),
            pl.BlockSpec((1, length, columns), lambda i: (i, 0, 0)),
            pl.BlockSpec((1, 3 * length // 2, 128), lambda i: (i, 0, 0)),
            each,
        ],
        (each, pl.BlockSpec((1, 2, width), lambda i: (i, 0, 0)), whole(weight.shape)),
        (tokens, mod, weight, valid, projected, mixed, middle),
        grid=(items,),
        flops=0,
        moved=0,
        name="attention_back",
    )


def body(
    tokens,
    time_embed,
    class_embed,
    valid_mask,
    routes,
    gate_logits,
    ada_weight,
    ada_bias,
    qkv_weight,
    out_weight,
    out_bias,
    fc1_weight,
    fc1_bias,
    fc2_weight,
    fc2_bias,
    expert_in,
    expert_out,
    out_grad,
):
    items, local, width = tokens.shape
    ranks = lax.axis_size("tensor")
    rank = lax.axis_index("tensor")
    dp_size = lax.axis_size("dp")
    dp_rank = lax.axis_index("dp")
    length = local * ranks
    head_width = qkv_weight.shape[2]
    cols = ada_weight.shape[2]
    rows = width // dp_size
    start = rank * local
    bits = dp_size.bit_length() - 1
    forth = list(range(bits))
    back = [0] + list(range(bits - 1, 0, -1))
    dp_index = dp_rank.astype(I32).reshape(1)

    def own_rows(values):
        return lax.dynamic_slice_in_dim(values, start, local, 1)

    tokens_full = lax.all_gather(tokens, "tensor", axis=1, tiled=True)
    out_turned = out_weight.T
    share_rows = head_width // dp_size
    piece = lax.dynamic_slice_in_dim(out_turned, dp_rank * share_rows, share_rows, 0)
    pieces = jnp.concatenate(gather_parts(piece), axis=0)
    condition = time_embed + class_embed
    cond_wide, silu_pull = jax.vjp(jax.nn.silu, condition)
    cond_low = cond_wide.astype(BF16)
    bias_cols = lax.dynamic_slice_in_dim(ada_bias, rank * cols, cols, 1)
    modulation_local = dot("id,dsk->isk", cond_low, ada_weight) + bias_cols.astype(F32)[None]
    modulation = jnp.concatenate(gather_parts(modulation_local), axis=2)
    modulation = swing(modulation, width - rank * cols, 2)

    first = after(expert_in, modulation).transpose(1, 0, 2)
    second = after(expert_out, modulation).transpose(1, 0, 2)
    qkv = qkv_weight.reshape(width, 3 * head_width)
    chosen = routes.transpose(0, 2, 1)
    live = valid_mask[:, None, :] > 0
    expert_ids = jnp.arange(E, dtype=I32)
    named = (chosen[:, :, None, :] == expert_ids[None, None, :, None]) & live[:, :, None, :]
    choose = jnp.any(named, axis=1)
    place = jnp.arange(length, dtype=I32)
    earlier = (place[:, None] < place[None, :]).astype(BF16)
    before = dot("iet,ts->ies", choose.astype(BF16), earlier).astype(I32)
    position = jnp.sum(jnp.where(named, before[:, None], 0), axis=2)
    marks = jnp.where(live, chosen * CAP + position, -1)
    columns = marks.transpose(0, 2, 1)
    gate_soft = jax.nn.softmax(gate_logits, axis=-1)
    share = gate_soft.transpose(0, 2, 1) * live

    every = dp_gather(jnp.concatenate([pieces, cond_low], axis=0))
    cond_every = every[:, ranks * share_rows :]
    out_full = every[:, : ranks * share_rows].reshape(dp_size, ranks, share_rows, width)
    out_full = out_full.swapaxes(0, 1).reshape(ranks, head_width, width)
    out_full = swing(out_full, ranks - rank, 0)
    valid_column = valid_mask[:, :, None] + 0
    fc2_row = fc2_bias[None] * 1
    modulation = after(modulation, first, second, marks, columns, share, valid_column, fc2_row)
    projected, mixed = attention(tokens_full, modulation, qkv, valid_mask[:, None, :])
    mixed_full = lax.all_gather(mixed, "tensor", axis=0)
    grad_full = lax.all_gather(after(out_grad, mixed_full), "tensor", axis=1, tiled=True)

    middle, branch_attn, normed_mlp = middle_part(
        after(mixed_full, out_full), out_full, out_bias[None], tokens_full, modulation
    )
    buffer, expert_act, expert_slope, hidden_act, hidden_slope, mlp_part = forward_part(
        normed_mlp, marks, share, columns, fc1_weight, fc1_bias[None], fc2_weight, first, second
    )
    mlp_sum = lax.psum_scatter(mlp_part, "tensor", scatter_dimension=1, tiled=True)

    quick = rows % 16 == 0 and dp_size == 8
    halfway = E // 2

    def start_sum(keep, send):
        return keep, dp_exchange(send, 0)

    def second_step(pair, order, weight=4_000_000):
        keep, other = pair
        if not quick:
            return keep, other
        kept, sent = halve(keep, other, 0 if order[0] == 2 else 1, weight)
        return kept, sent

    def third_step(pair, order, weight=4_000_000):
        if not quick:
            return pair
        kept, sent = pair
        return halve(kept, dp_exchange(sent, order[0]), 0, weight)

    def final_step(pair, order):
        if not quick:
            keep, other = pair
            return dp_scatter((keep.astype(F32) + other.astype(F32)).astype(BF16), order, BF16)
        kept, sent = pair
        return kept[0], dp_exchange(sent, order[1])[0]

    def whole_sum(pairs):
        if quick:
            return last(pairs, halfway)
        experts = jnp.concatenate([pair[:halfway] for pair in pairs], axis=0).swapaxes(0, 1).astype(F32)
        return [experts] + [pair[halfway].astype(F32) for pair in pairs if pair.shape[0] > halfway]

    ahead, behind = forth[1:], back[1:]
    branch_grad, branch_slot, keep, send = slots_part(
        0, halfway, marks, expert_act, dp_index, dp_size, grad=grad_full, mod=modulation, hidden=hidden_act
    )
    out_low = start_sum(keep, send)
    branch_slot, keep, send = slots_part(
        halfway, E - halfway, marks, expert_act, dp_index, dp_size, branch=branch_grad, held=branch_slot
    )
    out_high = start_sum(keep, send)
    out_low = second_step(out_low, ahead)
    out_high = second_step(out_high, behind)
    own = jnp.stack([start, start + local]).astype(I32)
    up_grad, hidden_grad, fc1_bias_part, dots, middle_grad, low_grad, mixed_parts, sums = back_part(
        branch_grad,
        after(columns, out_low[1], out_high[1]),
        fc1_weight,
        fc2_weight,
        hidden_slope,
        branch_slot,
        expert_act,
        expert_slope,
        first,
        second,
        middle,
        branch_attn,
        grad_full,
        mlp_part,
        modulation,
        out_full,
        own,
    )
    mixed_grad = lax.psum_scatter(mixed_parts, "tensor", scatter_dimension=0)

    marker = after(dp_index, mixed_parts, mlp_sum)
    out_low = third_step((after(out_low[0], marker), out_low[1]), ahead)
    out_high = third_step((after(out_high[0], marker), out_high[1]), behind)
    rank_index = rank.astype(I32).reshape(1)
    out_parts = out_grad_parts(
        low_grad, mixed_full, head_width, after(rank_index, marker, out_low[1], out_high[1])
    )
    in_low = start_sum(
        *first_part(0, halfway, buffer, up_grad, after(marker, out_parts[0]), dp_size)
    )
    out_low = final_step(out_low, ahead)
    out_high = final_step(out_high, behind)
    branch_mlp = after(mlp_sum, *out_low, *out_high).astype(F32) + fc2_row.astype(F32)[None]
    output = (own_rows(middle) + modulation[:, 5][:, None] * branch_mlp).astype(BF16)
    late_start = start
    fc2_bias_part = jnp.sum(
        lax.dynamic_slice_in_dim(branch_grad, late_start, local, 1).astype(F32), axis=(0, 1)
    )[None]
    in_high = start_sum(
        *first_part(
            halfway,
            E - halfway,
            buffer,
            up_grad,
            after(marker, in_low[0], output),
            dp_size,
            dense=(normed_mlp, hidden_grad),
        )
    )
    in_low = second_step((after(in_low[0], in_high[0], mixed_grad), in_low[1]), ahead)
    in_high = second_step((after(in_high[0], in_low[1]), in_high[1]), behind)
    out_parts = after(tuple(out_parts), mixed_grad)
    out_parts = [out_parts[0]] + [to_rank(out_parts[step], step) for step in range(1, ranks)]

    gate = after(modulation, in_low[1], in_high[1])
    tokens_part, attn_sums, qkv_grad = attention_back(
        tokens_full, gate, qkv, valid_column, projected, mixed_grad, middle_grad
    )
    tokens_grad = lax.psum_scatter(tokens_part, "tensor", scatter_dimension=1, tiled=True)
    packed = tail_part(ranks, rank_index, dots, marks, sums, attn_sums, fc2_row, out_grad, fc2_bias_part)
    late = start_sum(*late_part(qkv_grad, out_parts, after(dp_index, packed), dp_size))
    late = second_step(late, ahead, 0)
    in_low_other = dp_exchange(in_low[1], ahead[0]) if quick else in_low[1]
    in_high_other = dp_exchange(in_high[1], behind[0]) if quick else in_high[1]
    small = scatter_sum(list(after(tuple(packed[step] for step in range(ranks)), in_low_other, in_high_other)))
    if quick:
        in_high = halve(after(in_high[0], late[1]), in_high_other, 0, 0)
        in_low = halve(after(in_low[0], late[1], small), in_low_other, 0, 0)
    late = third_step((after(late[0], in_low[1], in_high[1]), late[1]), ahead)

    six, two = 6 * items, 2 * items
    modulation_grad = small[:six, :cols].reshape(items, 6, cols).astype(BF16)
    gate_grad = small[six : six + two, :local].reshape(items, 2, local).transpose(0, 2, 1)
    gate_logits_grad = gate_grad - own_rows(gate_soft) * jnp.sum(gate_grad, axis=-1, keepdims=True)
    cond_act_grad = dot("isk,dsk->id", modulation_grad, ada_weight)
    condition_part = silu_pull(cond_act_grad)[0]
    condition_part = swing(condition_part, rank * cols, 1)
    condition_grad = scatter_sum(
        [condition_part[:, step * cols : (step + 1) * cols] for step in range(ranks)]
    )

    biases = small[six + two :].reshape(width // 256, 2, 256).swapaxes(0, 1)
    payload = jnp.concatenate(
        [modulation_grad.astype(F32).reshape(-1), biases.reshape(-1), fc1_bias_part[0]]
    )
    payload = dp_gather(payload, tokens_grad, 1)
    middle_cut = items * 6 * cols
    modulation_every = payload[:, :middle_cut].astype(BF16).reshape(dp_size * items, 6, cols)
    cond_every = cond_every.reshape(dp_size * items, width)
    cond_rows = lax.dynamic_slice_in_dim(cond_every, dp_rank * rows, rows, 1)
    ada_weight_sum = dot("id,isk->dsk", cond_rows, after(modulation_every, tokens_grad))
    ada_bias_sum = jnp.sum(modulation_every.astype(F32), axis=0)
    ada_bias_sum = lax.dynamic_slice_in_dim(
        ada_bias_sum, dp_rank * (cols // dp_size), cols // dp_size, 1
    )
    fine = rows // ranks
    bias_every = jnp.sum(payload[:, middle_cut:], axis=0).reshape(-1, width)
    bias_pair = lax.dynamic_slice_in_dim(bias_every[:2], dp_rank * rows + rank * fine, fine, 1)
    fc1_bias_sum = lax.dynamic_slice_in_dim(bias_every[2], dp_rank * rows, rows, 0)

    out_low, out_high = lax.optimization_barrier((out_low, out_high, in_low[1], in_high[1]))[:2]
    expert_out_sum, fc2_sum = whole_sum([out_low, out_high])

    in_low = final_step(in_low, ahead)
    in_high = final_step(in_high, behind)
    expert_in_sum, fc1_sum = whole_sum([after(in_low, tokens_grad), in_high])
    late = final_step(late, ahead)
    late_sum = (late[0].astype(F32) + late[1].astype(F32))[0] if quick else late[0].astype(F32)
    out_sum = late_sum[:, 3 * head_width :]
    qkv_sum = late_sum[:, : 3 * head_width].reshape(rows, 3, head_width)

    return (
        output,
        tokens_grad,
        condition_grad,
        gate_logits_grad,
        ada_weight_sum,
        ada_bias_sum,
        qkv_sum,
        out_sum,
        bias_pair[1],
        fc1_sum,
        fc1_bias_sum,
        fc2_sum,
        bias_pair[0],
        expert_in_sum,
        expert_out_sum,
    )


def solution(mesh):
    in_specs = (
        P("dp", "tensor", None),
        P("dp", None),
        P("dp", None),
        P("dp", None),
        P("dp", None, None),
        P("dp", None, None),
        P(None, None, "tensor"),
        P(),
        P(None, None, "tensor"),
        P(None, "tensor"),
        P(),
        P(None, "tensor"),
        P("tensor"),
        P(None, "tensor"),
        P(),
        P(None, None, "tensor"),
        P(None, None, "tensor"),
        P("dp", "tensor", None),
    )
    out_specs = (
        P("dp", "tensor", None),
        P("dp", "tensor", None),
        P("dp", "tensor"),
        P("dp", "tensor", None),
        P("dp", None, "tensor"),
        P(None, ("tensor", "dp")),
        P("dp", None, "tensor"),
        P("dp", "tensor"),
        P(("dp", "tensor")),
        P("dp", "tensor"),
        P(("tensor", "dp")),
        P("dp", "tensor"),
        P(("dp", "tensor")),
        P("dp", None, "tensor"),
        P("dp", None, "tensor"),
    )
    return jax.shard_map(body, mesh=mesh, in_specs=in_specs, out_specs=out_specs, check_vma=False)
```

```python
import functools

import jax
import jax.numpy as jnp
from jax import lax
from jax.experimental import pallas as pl
from jax.experimental.pallas import tpu as pltpu
from jax.sharding import PartitionSpec as P

HD = 64
E = 8
CAP = 192
F32 = jnp.float32
BF16 = jnp.bfloat16
I32 = jnp.int32
VMEM_BYTES = 56 * 1024 * 1024


def dot(spec, left, right):
    return jnp.einsum(spec, left, right, preferred_element_type=F32)


def mm(left, right):
    return jnp.dot(left, right, preferred_element_type=F32)


def mm_nt(left, right):
    return lax.dot_general(left, right, (((1,), (1,)), ((), ())), preferred_element_type=F32)


def mm_tn(left, right):
    return lax.dot_general(left, right, (((0,), (0,)), ((), ())), preferred_element_type=F32)


def after(values, *others):
    return lax.optimization_barrier((values,) + others)[0]


def from_rank(values, step):
    size = lax.axis_size("tensor")
    return lax.ppermute(values, "tensor", [(i, (i - step) % size) for i in range(size)])


def to_rank(values, step):
    size = lax.axis_size("tensor")
    return lax.ppermute(values, "tensor", [(i, (i + step) % size) for i in range(size)])


def gather_parts(values):
    size = lax.axis_size("tensor")
    return [values] + [from_rank(values, step) for step in range(1, size)]


def scatter_sum(parts):
    total = parts[0].astype(F32)
    for step in range(1, len(parts)):
        total = total + to_rank(parts[step], step).astype(F32)
    return total


def swing(values, amount, axis):
    twice = jnp.concatenate([values, values], axis=axis)
    return lax.dynamic_slice_in_dim(twice, amount, values.shape[axis], axis)


def dp_exchange(values, bit):
    size = lax.axis_size("dp")
    return lax.ppermute(values, "dp", [(i, i ^ (1 << bit)) for i in range(size)])


def to_relative(blocks):
    size = lax.axis_size("dp")
    rank = lax.axis_index("dp")
    for bit in range(size.bit_length() - 1):
        paired = blocks.reshape((size >> (bit + 1), 2, 1 << bit) + blocks.shape[1:])
        swapped = jnp.where(((rank >> bit) & 1) == 0, paired, paired[:, ::-1])
        blocks = swapped.reshape(blocks.shape)
    return blocks


def dp_scatter(blocks, order, kind):
    current = blocks.reshape((2,) * len(order) + blocks.shape[1:])
    left = sorted(order, reverse=True)
    for bit in order:
        axis = left.index(bit)
        keep = lax.index_in_dim(current, 0, axis, keepdims=False)
        send = lax.index_in_dim(current, 1, axis, keepdims=False)
        other = dp_exchange(send, bit)
        current = (keep.astype(F32) + other.astype(F32)).astype(kind)
        left.pop(axis)
    return current


def dp_gather(values, held=None, stage=-1):
    size = lax.axis_size("dp")
    rank = lax.axis_index("dp")
    current = values[None]
    for bit in range(size.bit_length() - 1):
        if bit == stage:
            current = after(current, held)
        other = dp_exchange(current, bit)
        mine = (rank >> bit) & 1
        low = jnp.where(mine == 0, current, other)
        high = jnp.where(mine == 0, other, current)
        current = jnp.concatenate([low, high], axis=0)
    return current


def norm_parts(values):
    center = values - jnp.mean(values, axis=-1, keepdims=True)
    spread = jnp.mean(center * center, axis=-1, keepdims=True)
    scale = lax.rsqrt(spread + 1e-06)
    return center * scale, scale


def norm_pull(normed, scale, grad):
    return scale * (
        grad
        - jnp.mean(grad, axis=-1, keepdims=True)
        - normed * jnp.mean(grad * normed, axis=-1, keepdims=True)
    )


def gelu_both(values):
    factor = 0.7978845608028654
    square = values * values
    inner = jnp.tanh(values * (factor + (factor * 0.044715) * square))
    half = 0.5 + 0.5 * inner
    slope = half + values * (half * (1.0 - inner)) * (factor + (factor * 0.134145) * square)
    return values * half, slope


def call(kernel, out_shape, in_specs, out_specs, args, grid=(), scratch=(), flops=0, moved=0, name=None, alias=None):
    return pl.pallas_call(
        kernel,
        out_shape=out_shape,
        grid=grid,
        in_specs=in_specs,
        out_specs=out_specs,
        scratch_shapes=scratch,
        input_output_aliases=alias or {},
        compiler_params=pltpu.CompilerParams(
            vmem_limit_bytes=VMEM_BYTES, dimension_semantics=("arbitrary",) * len(grid)
        ),
        cost_estimate=pl.CostEstimate(flops=flops, bytes_accessed=moved, transcendentals=0),
        name=name,
    )(*args)


def whole(shape):
    zeros = (0,) * len(shape)
    return pl.BlockSpec(shape, lambda *_: zeros)


def once(shape):
    zeros = (0,) * len(shape)
    return pl.BlockSpec(shape, lambda *_: zeros, pipeline_mode=pl.Buffered(1))


def shaped(shape, kind):
    return jax.ShapeDtypeStruct(shape, kind)


def pack_heads(values):
    half = values.shape[0] // 2
    rest = jnp.concatenate([values[:half, 128:], values[half:, 128:]], axis=1)
    return jnp.concatenate([values[:, :128], rest], axis=0)


def unpack_heads(values):
    half = values.shape[0] // 3
    rest = values[2 * half :]
    upper = jnp.concatenate([values[:half], rest[:, :64]], axis=1)
    lower = jnp.concatenate([values[half : 2 * half], rest[:, 64:]], axis=1)
    return jnp.concatenate([upper, lower], axis=0)


def attention_kernel(heads, tokens_ref, mod_ref, weight_ref, valid_ref, projected_ref, mixed_ref):
    width = heads * HD
    normed, _ = norm_parts(tokens_ref[0].astype(F32))
    normed = normed * (1.0 + mod_ref[0, 1:2]) + mod_ref[0, 0:1]
    projected = mm(normed.astype(BF16), weight_ref[...]).astype(BF16)
    projected_ref[0] = projected
    live = valid_ref[0] > 0
    mixed = []
    for head in range(heads):
        low = head * HD
        query = projected[:, low : low + HD] * jnp.asarray(0.125, BF16)
        key = projected[:, width + low : width + low + HD]
        value = projected[:, 2 * width + low : 2 * width + low + HD]
        scores = jnp.where(live, mm_nt(query, key), -1e30)
        exponent = jnp.exp(scores - jnp.max(scores, axis=1, keepdims=True))
        probs = exponent * (1.0 / jnp.sum(exponent, axis=1, keepdims=True))
        mixed.append(mm(probs.astype(BF16), value))
    mixed_ref[0] = pack_heads(jnp.concatenate(mixed, axis=1).astype(BF16))


def attention(tokens, mod, weight, valid):
    items, length, width = tokens.shape
    head_width = weight.shape[1] // 3
    return call(
        functools.partial(attention_kernel, head_width // HD),
        (shaped((items, length, 3 * head_width), BF16), shaped((items, 3 * length // 2, 128), BF16)),
        [
            pl.BlockSpec((1, length, width), lambda i: (i, 0, 0)),
            pl.BlockSpec((1, 6, width), lambda i: (i, 0, 0)),
            whole(weight.shape),
            pl.BlockSpec((1, 1, length), lambda i: (i, 0, 0)),
        ],
        (
            pl.BlockSpec((1, length, 3 * head_width), lambda i: (i, 0, 0)),
            pl.BlockSpec((1, 3 * length // 2, 128), lambda i: (i, 0, 0)),
        ),
        (tokens, mod, weight, valid),
        grid=(items,),
        flops=8_000_000_000,
        moved=6_000_000,
        name="attention_forward",
    )


def middle_kernel(ranks, mixed_ref, rest_ref, weight_ref, bias_ref, tokens_ref, mod_ref, middle_ref, branch_ref, normed_ref):
    upper = pl.program_id(1) == 0
    branch = bias_ref[...].astype(F32)
    for rank in range(ranks):
        rest = jnp.where(upper, rest_ref[rank, 0, :, :64], rest_ref[rank, 0, :, 64:])
        branch = branch + mm(jnp.concatenate([mixed_ref[rank, 0], rest], axis=1), weight_ref[rank])
    middle = tokens_ref[0].astype(F32) + mod_ref[0, 2:3] * branch
    middle_ref[0] = middle
    branch_ref[0] = branch.astype(BF16)
    normed, _ = norm_parts(middle)
    normed_ref[0] = (normed * (1.0 + mod_ref[0, 4:5]) + mod_ref[0, 3:4]).astype(BF16)


def middle_part(mixed, weight, bias, tokens, mod):
    items, length, width = tokens.shape
    ranks = mixed.shape[0]
    block = length // 2
    rows = pl.BlockSpec((1, block, width), lambda i, r: (i, r, 0))
    return call(
        functools.partial(middle_kernel, ranks),
        (
            shaped(tokens.shape, F32),
            shaped(tokens.shape, BF16),
            shaped(tokens.shape, BF16),
        ),
        [
            pl.BlockSpec((ranks, 1, block, 128), lambda i, r: (0, i, r, 0)),
            pl.BlockSpec((ranks, 1, block, 128), lambda i, r: (0, i, 2, 0)),
            whole(weight.shape),
            whole(bias.shape),
            rows,
            pl.BlockSpec((1, 6, width), lambda i, r: (i, 0, 0)),
        ],
        (rows, rows, rows),
        (mixed, mixed, weight, bias, tokens, mod),
        grid=(items, 2),
        flops=3_000_000_000,
        moved=12_000_000,
        name="middle",
    )


def hot_rows(expert, marks):
    slots = lax.broadcasted_iota(I32, (CAP, marks.shape[1]), 0) + expert * CAP
    return slots == marks[0:1], slots == marks[1:2]


def as_hot(mask):
    return jnp.where(mask, 1.0, 0.0).astype(BF16)


def forward_kernel(
    items,
    normed_ref,
    marks_ref,
    share_ref,
    columns_ref,
    fc1_ref,
    bias_ref,
    fc2_ref,
    first_ref,
    second_ref,
    buffer_ref,
    act_ref,
    slope_ref,
    hidden_ref,
    hidden_slope_ref,
    out_ref,
    slots_ref,
):
    expert = pl.program_id(0)
    length = normed_ref.shape[1]

    @pl.when(expert == 0)
    def _():
        for item in range(items):
            hidden = mm(normed_ref[item], fc1_ref[...]) + bias_ref[...].astype(F32)
            value, slope = gelu_both(hidden)
            hidden_ref[item] = value.astype(BF16)
            hidden_slope_ref[item] = slope.astype(BF16)

    shares = []
    for item in range(items):
        one, two = hot_rows(expert, marks_ref[item])
        buffer_ref[0, item * CAP : (item + 1) * CAP] = mm(as_hot(one | two), normed_ref[item]).astype(BF16)
        held = jnp.where(one, share_ref[item, 0:1], 0.0) + jnp.where(two, share_ref[item, 1:2], 0.0)
        shares.append(jnp.sum(held, axis=1, keepdims=True))
    share = jnp.concatenate(shares, axis=0)
    value, slope = gelu_both(mm(buffer_ref[0], first_ref[0]))
    act_ref[0] = (share * value).astype(BF16)
    slope_ref[0] = (share * slope).astype(BF16)
    returned = mm_nt(act_ref[0], second_ref[0]).astype(BF16)
    place = pl.ds(pl.multiple_of(expert * CAP, 64), CAP)
    for item in range(items):
        slots_ref[item, place] = returned[item * CAP : (item + 1) * CAP]

    @pl.when(expert == E - 1)
    def _():
        lanes = lax.broadcasted_iota(I32, (length, E * CAP), 1)
        for item in range(items):
            marks = columns_ref[item]
            hot = as_hot((lanes == marks[:, 0:1]) | (lanes == marks[:, 1:2]))
            total = mm(hot, slots_ref[item]) + mm_nt(hidden_ref[item], fc2_ref[...])
            out_ref[item] = total.astype(BF16)


def forward_part(normed, marks, share, columns, fc1, bias, fc2, first, second):
    items, length, width = normed.shape
    units = fc1.shape[1]
    slots = items * CAP
    inner = pl.BlockSpec((1, slots, units), lambda e: (e, 0, 0))
    weight = pl.BlockSpec((1, width, units), lambda e: (e, 0, 0))
    hidden = (items, length, units)
    return call(
        functools.partial(forward_kernel, items),
        (
            shaped((E, slots, width), BF16),
            shaped((E, slots, units), BF16),
            shaped((E, slots, units), BF16),
            shaped(hidden, BF16),
            shaped(hidden, BF16),
            shaped(normed.shape, BF16),
        ),
        [
            whole(normed.shape),
            whole(marks.shape),
            whole(share.shape),
            whole(columns.shape),
            whole(fc1.shape),
            whole(bias.shape),
            whole(fc2.shape),
            weight,
            weight,
        ],
        (
            pl.BlockSpec((1, slots, width), lambda e: (e, 0, 0)),
            inner,
            inner,
            whole(hidden),
            whole(hidden),
            whole(normed.shape),
        ),
        (normed, marks, share, columns, fc1, bias, fc2, first, second),
        grid=(E,),
        scratch=[pltpu.VMEM((items, E * CAP, width), BF16)],
        flops=14_000_000_000,
        moved=40_000_000,
        name="mlp_forward",
    )


def store_blocks(keep_ref, send_ref, rank, index, grad):
    blocks, rows = 2 * keep_ref.shape[0], keep_ref.shape[2]
    for pair in range(blocks // 2):
        place = lax.bitwise_xor(rank // 2, pair)
        low = grad[2 * pair * rows : (2 * pair + 1) * rows]
        high = grad[(2 * pair + 1) * rows : (2 * pair + 2) * rows]
        odd = rank % 2 == 1

        @pl.when(odd)
        def _():
            keep_ref[place, index] = high
            send_ref[place, index] = low

        @pl.when(jnp.logical_not(odd))
        def _():
            keep_ref[place, index] = low
            send_ref[place, index] = high


def split_blocks(grads, dp_size):
    count, width, units = grads.shape
    blocks = to_relative(grads.reshape(count, dp_size, width // dp_size, units).swapaxes(0, 1))
    pairs = blocks.reshape((dp_size // 2, 2) + blocks.shape[1:])
    return pairs[:, 0], pairs[:, 1]


def call_grads(kernel, steps, rank, dp_size, shape, outs, out_specs, specs, args, alias=None, weight=20_000_000):
    width, units = shape
    rows = width // dp_size
    smooth = rows % 16 == 0
    block = pl.BlockSpec((dp_size // 2, 1, rows, units), lambda e: (0, e, 0, 0))
    part = shaped((dp_size // 2, steps, rows, units), BF16)
    return call(
        kernel,
        outs + ((part, part) if smooth else ()),
        [pl.BlockSpec(memory_space=pltpu.SMEM)] + specs,
        out_specs + ((block, block) if smooth else ()),
        (rank,) + args,
        grid=(steps,),
        flops=0,
        moved=weight,
        name="weight_grads",
        alias=alias,
    )


def expert_block(start, count, shape):
    return pl.BlockSpec((1,) + shape, lambda e: (jnp.minimum(e, count - 1) + start, 0, 0))


def slots_kernel(items, start, count, rank_ref, marks_ref, act_ref, *refs):
    expert = pl.program_id(0)
    if start == 0:
        grad_ref, mod_ref, hidden_ref, branch_ref, slots_ref, *grad_refs = refs

        @pl.when(expert == 0)
        def _():
            for item in range(items):
                branch_ref[item] = (grad_ref[item].astype(F32) * mod_ref[item, 5:6]).astype(BF16)

    else:
        branch_ref, _, slots_ref, *grad_refs = refs

    @pl.when(expert < count)
    def _():
        for item in range(items):
            one, two = hot_rows(expert + start, marks_ref[item])
            slots_ref[0, item * CAP : (item + 1) * CAP] = mm(as_hot(one | two), branch_ref[item]).astype(BF16)
        if grad_refs:
            store_blocks(*grad_refs, rank_ref[0], 0, mm_tn(slots_ref[0], act_ref[0]).astype(BF16))

    if start == 0 and grad_refs:

        @pl.when(expert == count)
        def _():
            total = mm_tn(branch_ref[0], hidden_ref[0])
            for item in range(1, items):
                total = total + mm_tn(branch_ref[item], hidden_ref[item])
            store_blocks(*grad_refs, rank_ref[0], 0, total.astype(BF16))


def slots_part(start, count, marks, act, rank, dp_size, grad=None, mod=None, hidden=None, branch=None, held=None):
    items, length, width = (branch if grad is None else grad).shape
    units = act.shape[2]
    slots = items * CAP
    all_rows = whole((items, length, width))
    each = expert_block(start, count, (slots, width))
    filled = shaped((E, slots, width), BF16)
    if start == 0:
        specs, more = [all_rows, whole(mod.shape), whole(hidden.shape)], (grad, mod, hidden)
        outs, out_specs, alias = (shaped(grad.shape, BF16), filled), (all_rows, each), {}
    else:
        specs, more = [all_rows, pl.BlockSpec(memory_space=pl.ANY)], (branch, held)
        outs, out_specs, alias = (filled,), (each,), {4: 0}
    result = call_grads(
        functools.partial(slots_kernel, items, start, count),
        count + (start == 0),
        rank,
        dp_size,
        (width, units),
        outs,
        out_specs,
        [whole(marks.shape), expert_block(start, count, (slots, units))] + specs,
        (marks, act) + more,
        alias,
    )
    if (width // dp_size) % 16:
        picked = slice(start, start + count)
        grads = dot("ecd,ecf->edf", result[-1][picked], act[picked])
        if start == 0:
            grads = jnp.concatenate([grads, dot("isd,isf->df", result[0], hidden)[None]], axis=0)
        result = tuple(result) + split_blocks(grads.astype(BF16), dp_size)
    return result


def out_grad_kernel(rank_ref, low_ref, mixed_ref, *out_refs):
    ranks = mixed_ref.shape[0]
    for rank in range(ranks):
        total = mm_tn(unpack_heads(mixed_ref[rank, 0]), low_ref[0])
        for item in range(1, low_ref.shape[0]):
            total = total + mm_tn(unpack_heads(mixed_ref[rank, item]), low_ref[item])
        total = total.astype(BF16)
        for step, out_ref in enumerate(out_refs):

            @pl.when(lax.rem(rank - rank_ref[0] + ranks, ranks) == step)
            def _():
                out_ref[...] = total


def out_grad_parts(low, mixed, head_width, rank):
    ranks, width = mixed.shape[0], low.shape[2]
    vmem = pl.BlockSpec(memory_space=pltpu.VMEM)
    return call(
        out_grad_kernel,
        (shaped((head_width, width), BF16),) * ranks,
        [pl.BlockSpec(memory_space=pltpu.SMEM), vmem, vmem],
        (vmem,) * ranks,
        (rank, low, mixed),
        flops=0,
        moved=4_000_000,
        name="out_weight_grad",
    )


def late_kernel(rank_ref, qkv_ref, *refs):
    *out_refs, keep_ref, send_ref = refs
    total = sum(out_ref[...].astype(F32) for out_ref in out_refs)
    grad = jnp.concatenate([qkv_ref[...], total.T], axis=1)
    store_blocks(keep_ref, send_ref, rank_ref[0], 0, grad.astype(BF16))


def late_part(qkv_grad, out_parts, rank, dp_size):
    width = qkv_grad.shape[0]
    columns = qkv_grad.shape[1] + out_parts[0].shape[0]
    rows = width // dp_size
    if rows % 16:
        total = sum(part.astype(F32) for part in out_parts)
        grads = jnp.concatenate([qkv_grad, total.T], axis=1).astype(BF16)
        return split_blocks(grads[None], dp_size)
    part = shaped((dp_size // 2, 1, rows, columns), BF16)
    vmem = pl.BlockSpec(memory_space=pltpu.VMEM)
    return call(
        late_kernel,
        (part, part),
        [pl.BlockSpec(memory_space=pltpu.SMEM), vmem] + [vmem] * len(out_parts),
        (vmem, vmem),
        (rank, qkv_grad, *out_parts),
        flops=0,
        moved=0,
        name="late_blocks",
    )


def first_kernel(count, rank_ref, left_ref, right_ref, *refs):
    expert = pl.program_id(0)
    grad_refs = refs[-2:]

    @pl.when(expert < count)
    def _():
        store_blocks(*grad_refs, rank_ref[0], 0, mm_tn(left_ref[0], right_ref[0]).astype(BF16))

    if len(refs) > 2:
        dense_left_ref, dense_right_ref = refs[:2]

        @pl.when(expert == count)
        def _():
            total = mm_tn(dense_left_ref[0], dense_right_ref[0])
            for item in range(1, dense_left_ref.shape[0]):
                total = total + mm_tn(dense_left_ref[item], dense_right_ref[item])
            store_blocks(*grad_refs, rank_ref[0], 0, total.astype(BF16))


def first_part(start, count, left, right, rank, dp_size, dense=()):
    _, slots, width = left.shape
    units = right.shape[2]
    rows = width // dp_size
    if rows % 16:
        picked = slice(start, start + count)
        grads = dot("ecd,ecf->edf", left[picked], right[picked])
        if dense:
            grads = jnp.concatenate([grads, dot("isd,isf->df", *dense)[None]], axis=0)
        return split_blocks(grads.astype(BF16), dp_size)
    return call_grads(
        functools.partial(first_kernel, count),
        count + (1 if dense else 0),
        rank,
        dp_size,
        (width, units),
        (),
        (),
        [expert_block(start, count, (slots, width)), expert_block(start, count, (slots, units))]
        + [whole(value.shape) for value in dense],
        (left, right) + tuple(dense),
        weight=20_000_000 if dense else 4_000_000,
    )


def halve_kernel(first, keep_ref, other_ref, kept_ref, sent_ref):
    total = (keep_ref[...].astype(F32) + other_ref[...].astype(F32)).astype(BF16)
    kept_ref[...] = total[0:1] if first else total[:, 0:1]
    sent_ref[...] = total[1:2] if first else total[:, 1:2]


def halve(keep, other, axis, weight):
    lead = keep.shape[0]
    rest = keep.shape[1:]
    zeros = (0,) * len(rest)
    if lead == 2:
        shape, outer, axis = (2, 1) + rest, 1, 0
    else:
        shape, outer = (2, lead // 2) + rest, lead // 2
    if axis == 0:
        block, result = (2, 1) + rest, (1, outer) + rest
        spec = pl.BlockSpec(block, lambda i: (0, i) + zeros)
        out = pl.BlockSpec((1, 1) + rest, lambda i: (0, i) + zeros)
        steps = outer
    else:
        block, result = (1, 2) + rest, (2, 1) + rest
        spec = pl.BlockSpec(block, lambda i: (i, 0) + zeros)
        out = pl.BlockSpec((1, 1) + rest, lambda i: (i, 0) + zeros)
        steps = 2
    kept, sent = call(
        functools.partial(halve_kernel, axis == 0),
        (shaped(result, BF16),) * 2,
        [spec, spec],
        (out, out),
        (keep.reshape(shape), other.reshape(shape)),
        grid=(steps,),
        flops=0,
        moved=weight,
        name="halve",
    )
    return kept.reshape((lead // 2,) + rest), sent.reshape((lead // 2,) + rest)


def last_kernel(halfway, counts, *refs):
    inputs, (out_ref, *dense_refs) = refs[: 2 * len(counts)], refs[2 * len(counts) :]
    dense = iter(dense_refs)
    place = 0
    for group, size in enumerate(counts):
        keep_ref, other_ref = inputs[2 * group], inputs[2 * group + 1]
        for index in range(size):
            total = keep_ref[index].astype(F32) + other_ref[index].astype(F32)
            if index < halfway:
                out_ref[:, place] = total
                place += 1
            else:
                next(dense)[...] = total


def last(pairs, halfway):
    counts = [keep.shape[0] for keep, _ in pairs]
    rows, units = pairs[0][0].shape[1:]
    args = [value for pair in pairs for value in pair]
    vmem = pl.BlockSpec(memory_space=pltpu.VMEM)
    extra = sum(size > halfway for size in counts)
    return call(
        functools.partial(last_kernel, halfway, counts),
        (shaped((rows, halfway * len(counts), units), F32),) + (shaped((rows, units), F32),) * extra,
        [vmem] * len(args),
        (vmem,) * (1 + extra),
        tuple(args),
        flops=sum(counts) * rows * units,
        moved=8 * sum(counts) * rows * units,
        name="last_sum",
    )


def back_kernel(
    items,
    ranks,
    own_ref,
    branch_ref,
    columns_ref,
    fc1_ref,
    fc2_ref,
    hidden_slope_ref,
    mod_ref,
    weight_ref,
    slots_ref,
    act_ref,
    slope_ref,
    first_ref,
    second_ref,
    middle_hbm,
    attn_hbm,
    cotangent_hbm,
    mlp_hbm,
    up_grad_ref,
    hidden_grad_ref,
    bias_grad_ref,
    dots_ref,
    middle_grad_ref,
    low_ref,
    mixed_ref,
    sums_ref,
    grad_ref,
    held_ref,
    middle_ref,
    attn_ref,
    cotangent_ref,
    mlp_ref,
    sems,
):
    expert = pl.program_id(0)
    length = branch_ref.shape[1]
    pairs = [(middle_hbm, middle_ref), (attn_hbm, attn_ref), (cotangent_hbm, cotangent_ref), (mlp_hbm, mlp_ref)]
    copies = [pltpu.make_async_copy(far, near, sems.at[index]) for index, (far, near) in enumerate(pairs)]

    @pl.when(expert == 0)
    def _():
        for copy in copies:
            copy.start()
        total = jnp.zeros(bias_grad_ref.shape, F32)
        for item in range(items):
            grad = mm(branch_ref[item], fc2_ref[...]) * hidden_slope_ref[item].astype(F32)
            grad = grad.astype(BF16)
            hidden_grad_ref[item] = grad
            total = total + jnp.sum(grad.astype(F32), axis=0, keepdims=True)
            grad_ref[item] = mm_nt(grad, fc1_ref[...])
        bias_grad_ref[...] = total

    pulled = mm(slots_ref[0], second_ref[0])
    up_grad = (pulled * slope_ref[0].astype(F32)).astype(BF16)
    up_grad_ref[0] = up_grad
    total = jnp.sum(act_ref[0].astype(F32) * pulled, axis=1, keepdims=True)
    high = total.astype(BF16).astype(F32)
    lane = lax.broadcasted_iota(I32, (items * CAP, 128), 1)
    split = jnp.where(lane == 0, high, jnp.where(lane == 1, total - high, 0.0)).astype(BF16)
    back = mm_nt(up_grad, first_ref[0]).astype(BF16)
    place = pl.ds(pl.multiple_of(expert * CAP, 64), CAP)
    for item in range(items):
        held_ref[item, place] = back[item * CAP : (item + 1) * CAP]
        dots_ref[item, place] = split[item * CAP : (item + 1) * CAP]

    @pl.when(expert == E - 1)
    def _():
        for copy in copies:
            copy.wait()
        block = length // 2
        lanes = lax.broadcasted_iota(I32, (block, E * CAP), 1)
        for item in range(items):
            sums = []
            for step in range(2):
                part = slice(step * block, (step + 1) * block)
                marks = columns_ref[item, part]
                hot = as_hot((lanes == marks[:, 0:1]) | (lanes == marks[:, 1:2]))
                grad = grad_ref[item, part] + mm(hot, held_ref[item])
                normed, scale = norm_parts(middle_ref[item, part])
                pulled = norm_pull(normed, scale, grad * (1.0 + mod_ref[item, 4:5]))
                at = lax.broadcasted_iota(I32, (block, 1), 0) + step * block
                own = (at >= own_ref[0]) & (at < own_ref[1])
                cotangent = cotangent_ref[item, part].astype(F32)
                pulled = pulled + jnp.where(own, cotangent, 0.0)
                middle_grad_ref[item, part] = pulled.astype(BF16)
                low = (pulled * mod_ref[item, 2:3]).astype(BF16)
                low_ref[item, part] = low
                for rank in range(ranks):
                    mixed = mm_nt(low, weight_ref[rank]).astype(BF16)
                    mixed_ref[rank, item, part] = mixed[:, :128]
                    mixed_ref[rank, item, 2 * block :, step * 64 : (step + 1) * 64] = mixed[:, 128:]
                terms = [
                    grad,
                    grad * normed,
                    pulled * attn_ref[item, part].astype(F32),
                    low.astype(F32),
                    cotangent * mlp_ref[item, part].astype(F32),
                ]
                sums.append(jnp.concatenate([jnp.sum(term, axis=0, keepdims=True) for term in terms], axis=0))
            sums_ref[item] = sums[0] + sums[1]


def back_part(
    branch, columns, fc1, fc2, hidden_slope, branch_slot, act, slope, first, second, middle, attn, cotangent, mlp, mod, weight, own
):
    items, length, width = branch.shape
    ranks = weight.shape[0]
    units = fc1.shape[1]
    slots = items * CAP
    inner = pl.BlockSpec((1, slots, units), lambda e: (e, 0, 0))
    expert_weight = pl.BlockSpec((1, width, units), lambda e: (e, 0, 0))
    hidden = (items, length, units)
    packed = (ranks, items, 3 * length // 2, 128)
    far = pl.BlockSpec(memory_space=pl.ANY)
    return call(
        functools.partial(back_kernel, items, ranks),
        (
            shaped((E, slots, units), BF16),
            shaped(hidden, BF16),
            shaped((1, units), F32),
            shaped((items, E * CAP, 128), BF16),
            shaped(branch.shape, BF16),
            shaped(branch.shape, BF16),
            shaped(packed, BF16),
            shaped((items, 5, width), F32),
        ),
        [
            pl.BlockSpec(memory_space=pltpu.SMEM),
            once(branch.shape),
            once(columns.shape),
            once(fc1.shape),
            once(fc2.shape),
            once(hidden),
            once(mod.shape),
            once(weight.shape),
            pl.BlockSpec((1, slots, width), lambda e: (e, 0, 0)),
            inner,
            inner,
            expert_weight,
            expert_weight,
            far,
            far,
            far,
            far,
        ],
        (
            inner,
            whole(hidden),
            whole((1, units)),
            whole((items, E * CAP, 128)),
            whole(branch.shape),
            whole(branch.shape),
            whole(packed),
            whole((items, 5, width)),
        ),
        (own, branch, columns, fc1, fc2, hidden_slope, mod, weight, branch_slot, act, slope, first, second, middle, attn, cotangent, mlp),
        grid=(E,),
        scratch=[
            pltpu.VMEM(branch.shape, F32),
            pltpu.VMEM((items, E * CAP, width), BF16),
            pltpu.VMEM(middle.shape, F32),
            pltpu.VMEM(attn.shape, BF16),
            pltpu.VMEM(cotangent.shape, BF16),
            pltpu.VMEM(mlp.shape, BF16),
            pltpu.SemaphoreType.DMA((4,)),
        ],
        flops=14_000_000_000,
        moved=50_000_000,
        name="mlp_back",
    )


def tail_kernel(
    ranks,
    rank_ref,
    dots_ref,
    marks_ref,
    sums_ref,
    attn_ref,
    bias_ref,
    grad_ref,
    bias_grad_ref,
    packed_ref,
):
    items, local, width = grad_ref.shape
    cols = width // ranks
    packed_ref[...] = jnp.zeros(packed_ref.shape, F32)
    bias = bias_ref[...].astype(F32)
    slots = lax.broadcasted_iota(I32, (dots_ref.shape[1], marks_ref.shape[2]), 0)
    gates, mods = [], []
    for item in range(items):
        for choice in range(2):
            both = mm_tn(dots_ref[item], as_hot(slots == marks_ref[item, choice : choice + 1]))
            gates.append(both[0:1] + both[1:2])
        sums = sums_ref[item]
        local_sum = jnp.sum(grad_ref[item].astype(F32), axis=0, keepdims=True)
        mods += [attn_ref[item], sums[2:3], sums[0:2], sums[4:5] + local_sum * bias]
    bias_grad = bias_grad_ref[...]
    out_bias_grad = jnp.zeros((1, width), F32)
    for item in range(items):
        out_bias_grad = out_bias_grad + sums_ref[item, 3:4]
    mod_grads = jnp.concatenate(mods, axis=0)
    gates = jnp.concatenate(gates, axis=0)
    six, two = 6 * items, 2 * items
    for rank in range(ranks):
        place = lax.rem(rank - rank_ref[0] + ranks, ranks)
        packed_ref[place, 0:six, 0:cols] = mod_grads[:, rank * cols : (rank + 1) * cols]
        packed_ref[place, six : six + two, 0:local] = gates[:, rank * local : (rank + 1) * local]
        for cut in range(width // 256):
            part = slice(cut * 256, (cut + 1) * 256)
            row = six + two + 2 * cut
            packed_ref[place, row : row + 1] = bias_grad[:, part]
            packed_ref[place, row + 1 : row + 2] = out_bias_grad[:, part]


def tail_part(ranks, rank, dots, marks, sums, attn_sums, bias, grad, bias_grad):
    items, local, width = grad.shape
    packed_rows = 8 * items + 2 * (width // 256)
    vmem = pl.BlockSpec(memory_space=pltpu.VMEM)
    return call(
        functools.partial(tail_kernel, ranks),
        shaped((ranks, packed_rows, 256), F32),
        [pl.BlockSpec(memory_space=pltpu.SMEM)] + [vmem] * 7,
        vmem,
        (rank, dots, marks, sums, attn_sums, bias, grad, bias_grad),
        flops=0,
        moved=0,
        name="tail",
    )


def attention_back_kernel(
    heads, tokens_ref, mod_ref, weight_ref, valid_ref, projected_ref, mixed_ref, middle_ref, part_ref, sums_ref, total_ref
):
    item = pl.program_id(0)
    width = heads * HD
    base, scale = norm_parts(tokens_ref[0].astype(F32))
    normed = (base * (1.0 + mod_ref[0, 1:2]) + mod_ref[0, 0:1]).astype(BF16)
    projected = projected_ref[0]
    grads = [[], [], []]
    count = jnp.sum(valid_ref[0], axis=1, keepdims=True)
    live = lax.broadcasted_iota(I32, (tokens_ref.shape[1], 1), 0) < count
    mixed_grad = unpack_heads(mixed_ref[0])
    for head in range(heads):
        low = head * HD
        query = projected[:, low : low + HD] * jnp.asarray(0.125, BF16)
        key = projected[:, width + low : width + low + HD]
        value = projected[:, 2 * width + low : 2 * width + low + HD]
        mixed = mixed_grad[:, low : low + HD]
        scores = jnp.where(live, mm_nt(key, query), -1e30)
        exponent = jnp.exp(scores - jnp.max(scores, axis=0, keepdims=True))
        probs = exponent * (1.0 / jnp.sum(exponent, axis=0, keepdims=True))
        value_grad = mm(probs.astype(BF16), mixed)
        prob_grad = mm_nt(value, mixed)
        held = probs * prob_grad
        score_grad = (held - probs * jnp.sum(held, axis=0, keepdims=True)).astype(BF16)
        grads[0].append(mm_tn(score_grad, key) * 0.125)
        grads[1].append(mm(score_grad, query))
        grads[2].append(value_grad)
    project_grad = jnp.concatenate(grads[0] + grads[1] + grads[2], axis=1).astype(BF16)
    grad = mm_nt(project_grad, weight_ref[...])
    sums_ref[0] = jnp.concatenate(
        [jnp.sum(grad, axis=0, keepdims=True), jnp.sum(grad * base, axis=0, keepdims=True)], axis=0
    )
    part_ref[0] = (middle_ref[0].astype(F32) + norm_pull(base, scale, grad * (1.0 + mod_ref[0, 1:2]))).astype(BF16)
    weight_grad = mm_tn(normed, project_grad)

    @pl.when(item == 0)
    def _():
        total_ref[...] = weight_grad

    @pl.when(item > 0)
    def _():
        total_ref[...] += weight_grad


def attention_back(tokens, mod, weight, valid, projected, mixed, middle):
    items, length, width = tokens.shape
    columns = weight.shape[1]
    each = pl.BlockSpec((1, length, width), lambda i: (i, 0, 0))
    return call(
        functools.partial(attention_back_kernel, columns // (3 * HD)),
        (shaped(tokens.shape, BF16), shaped((items, 2, width), F32), shaped(weight.shape, F32)),
        [
            each,
            pl.BlockSpec((1, 6, width), lambda i: (i, 0, 0)),
            whole(weight.shape),
            pl.BlockSpec((1, 1, length), lambda i: (i, 0, 0)),
            pl.BlockSpec((1, length, columns), lambda i: (i, 0, 0)),
            pl.BlockSpec((1, 3 * length // 2, 128), lambda i: (i, 0, 0)),
            each,
        ],
        (each, pl.BlockSpec((1, 2, width), lambda i: (i, 0, 0)), whole(weight.shape)),
        (tokens, mod, weight, valid, projected, mixed, middle),
        grid=(items,),
        flops=0,
        moved=0,
        name="attention_back",
    )


def body(
    tokens,
    time_embed,
    class_embed,
    valid_mask,
    routes,
    gate_logits,
    ada_weight,
    ada_bias,
    qkv_weight,
    out_weight,
    out_bias,
    fc1_weight,
    fc1_bias,
    fc2_weight,
    fc2_bias,
    expert_in,
    expert_out,
    out_grad,
):
    items, local, width = tokens.shape
    ranks = lax.axis_size("tensor")
    rank = lax.axis_index("tensor")
    dp_size = lax.axis_size("dp")
    dp_rank = lax.axis_index("dp")
    length = local * ranks
    head_width = qkv_weight.shape[2]
    cols = ada_weight.shape[2]
    rows = width // dp_size
    start = rank * local
    bits = dp_size.bit_length() - 1
    forth = list(range(bits))
    back = [0] + list(range(bits - 1, 0, -1))
    dp_index = dp_rank.astype(I32).reshape(1)

    def own_rows(values):
        return lax.dynamic_slice_in_dim(values, start, local, 1)

    tokens_full = lax.all_gather(tokens, "tensor", axis=1, tiled=True)
    out_turned = out_weight.T
    share_rows = head_width // dp_size
    piece = lax.dynamic_slice_in_dim(out_turned, dp_rank * share_rows, share_rows, 0)
    pieces = jnp.concatenate(gather_parts(piece), axis=0)
    condition = time_embed + class_embed
    cond_wide, silu_pull = jax.vjp(jax.nn.silu, condition)
    cond_low = cond_wide.astype(BF16)
    bias_cols = lax.dynamic_slice_in_dim(ada_bias, rank * cols, cols, 1)
    modulation_local = dot("id,dsk->isk", cond_low, ada_weight) + bias_cols.astype(F32)[None]
    modulation = jnp.concatenate(gather_parts(modulation_local), axis=2)
    modulation = swing(modulation, width - rank * cols, 2)

    first = after(expert_in, modulation).transpose(1, 0, 2)
    second = after(expert_out, modulation).transpose(1, 0, 2)
    qkv = qkv_weight.reshape(width, 3 * head_width)
    chosen = routes.transpose(0, 2, 1)
    live = valid_mask[:, None, :] > 0
    expert_ids = jnp.arange(E, dtype=I32)
    named = (chosen[:, :, None, :] == expert_ids[None, None, :, None]) & live[:, :, None, :]
    choose = jnp.any(named, axis=1)
    place = jnp.arange(length, dtype=I32)
    earlier = (place[:, None] < place[None, :]).astype(BF16)
    before = dot("iet,ts->ies", choose.astype(BF16), earlier).astype(I32)
    position = jnp.sum(jnp.where(named, before[:, None], 0), axis=2)
    marks = jnp.where(live, chosen * CAP + position, -1)
    columns = marks.transpose(0, 2, 1)
    gate_soft = jax.nn.softmax(gate_logits, axis=-1)
    share = gate_soft.transpose(0, 2, 1) * live

    every = dp_gather(jnp.concatenate([pieces, cond_low], axis=0))
    cond_every = every[:, ranks * share_rows :]
    out_full = every[:, : ranks * share_rows].reshape(dp_size, ranks, share_rows, width)
    out_full = out_full.swapaxes(0, 1).reshape(ranks, head_width, width)
    out_full = swing(out_full, ranks - rank, 0)
    fc2_row = fc2_bias[None] * 1
    modulation = after(modulation, first, second, marks, columns, share, fc2_row)
    projected, mixed = attention(tokens_full, modulation, qkv, valid_mask[:, None, :])
    mixed_full = lax.all_gather(mixed, "tensor", axis=0)
    grad_full = lax.all_gather(after(out_grad, mixed_full, out_full), "tensor", axis=1, tiled=True)

    middle, branch_attn, normed_mlp = middle_part(
        after(mixed_full, out_full), out_full, out_bias[None], tokens_full, modulation
    )
    buffer, expert_act, expert_slope, hidden_act, hidden_slope, mlp_part = forward_part(
        normed_mlp, marks, share, columns, fc1_weight, fc1_bias[None], fc2_weight, first, second
    )
    mlp_sum = lax.psum_scatter(mlp_part, "tensor", scatter_dimension=1, tiled=True)

    quick = rows % 16 == 0 and dp_size == 8
    halfway = E // 2

    def start_sum(keep, send):
        return keep, dp_exchange(send, 0)

    def second_step(pair, order, weight=4_000_000):
        keep, other = pair
        if not quick:
            return keep, other
        kept, sent = halve(keep, other, 0 if order[0] == 2 else 1, weight)
        return kept, sent

    def third_step(pair, order, weight=4_000_000):
        if not quick:
            return pair
        kept, sent = pair
        return halve(kept, dp_exchange(sent, order[0]), 0, weight)

    def final_step(pair, order):
        if not quick:
            keep, other = pair
            return dp_scatter((keep.astype(F32) + other.astype(F32)).astype(BF16), order, BF16)
        kept, sent = pair
        return kept[0], dp_exchange(sent, order[1])[0]

    def whole_sum(pairs):
        if quick:
            return last(pairs, halfway)
        experts = jnp.concatenate([pair[:halfway] for pair in pairs], axis=0).swapaxes(0, 1).astype(F32)
        return [experts] + [pair[halfway].astype(F32) for pair in pairs if pair.shape[0] > halfway]

    ahead, behind = forth[1:], back[1:]
    branch_grad, branch_slot, keep, send = slots_part(
        0, halfway, marks, expert_act, dp_index, dp_size, grad=grad_full, mod=modulation, hidden=hidden_act
    )
    out_low = start_sum(keep, send)
    branch_slot, keep, send = slots_part(
        halfway, E - halfway, marks, expert_act, dp_index, dp_size, branch=branch_grad, held=branch_slot
    )
    out_high = start_sum(keep, send)
    out_low = second_step(out_low, ahead)
    out_high = second_step(out_high, behind)
    own = jnp.stack([start, start + local]).astype(I32)
    up_grad, hidden_grad, fc1_bias_part, dots, middle_grad, low_grad, mixed_parts, sums = back_part(
        branch_grad,
        after(columns, out_low[1], out_high[1]),
        fc1_weight,
        fc2_weight,
        hidden_slope,
        branch_slot,
        expert_act,
        expert_slope,
        first,
        second,
        middle,
        branch_attn,
        grad_full,
        mlp_part,
        modulation,
        out_full,
        own,
    )
    mixed_grad = lax.psum_scatter(mixed_parts, "tensor", scatter_dimension=0)

    marker = after(dp_index, mixed_parts, mlp_sum)
    out_low = third_step((after(out_low[0], marker), out_low[1]), ahead)
    out_high = third_step((after(out_high[0], marker), out_high[1]), behind)
    rank_index = rank.astype(I32).reshape(1)
    out_parts = out_grad_parts(
        low_grad, mixed_full, head_width, after(rank_index, marker, out_low[1], out_high[1])
    )
    in_low = start_sum(
        *first_part(0, halfway, buffer, up_grad, after(marker, out_parts[0]), dp_size)
    )
    out_low = final_step(out_low, ahead)
    out_high = final_step(out_high, behind)
    branch_mlp = after(mlp_sum, *out_low, *out_high).astype(F32) + fc2_row.astype(F32)[None]
    output = (own_rows(middle) + modulation[:, 5][:, None] * branch_mlp).astype(BF16)
    late_start = start
    fc2_bias_part = jnp.sum(
        lax.dynamic_slice_in_dim(branch_grad, late_start, local, 1).astype(F32), axis=(0, 1)
    )[None]
    in_high = start_sum(
        *first_part(
            halfway,
            E - halfway,
            buffer,
            up_grad,
            after(marker, in_low[0], output),
            dp_size,
            dense=(normed_mlp, hidden_grad),
        )
    )
    in_low = second_step((after(in_low[0], in_high[0]), in_low[1]), ahead)
    in_high = second_step((after(in_high[0], in_low[1], mixed_grad), in_high[1]), behind)
    out_parts = after(tuple(out_parts), mixed_grad)
    out_parts = [out_parts[0]] + [to_rank(out_parts[step], step) for step in range(1, ranks)]

    gate = after(modulation, in_low[1], in_high[1])
    tokens_part, attn_sums, qkv_grad = attention_back(
        tokens_full, gate, qkv, valid_mask[:, None, :], projected, mixed_grad, middle_grad
    )
    tokens_grad = lax.psum_scatter(tokens_part, "tensor", scatter_dimension=1, tiled=True)
    packed = tail_part(ranks, rank_index, dots, marks, sums, attn_sums, fc2_row, out_grad, fc2_bias_part)
    late = start_sum(*late_part(qkv_grad, out_parts, after(dp_index, packed), dp_size))
    late = second_step(late, ahead, 0)
    in_low_other = dp_exchange(in_low[1], ahead[0]) if quick else in_low[1]
    in_high_other = dp_exchange(in_high[1], behind[0]) if quick else in_high[1]
    small = scatter_sum(list(after(tuple(packed[step] for step in range(ranks)), in_low_other, in_high_other)))
    if quick:
        in_high = halve(after(in_high[0], late[1]), in_high_other, 0, 0)
        in_low = halve(after(in_low[0], late[1], small), in_low_other, 0, 0)
    late = third_step((after(late[0], in_low[1], in_high[1]), late[1]), ahead)

    six, two = 6 * items, 2 * items
    modulation_grad = small[:six, :cols].reshape(items, 6, cols).astype(BF16)
    gate_grad = small[six : six + two, :local].reshape(items, 2, local).transpose(0, 2, 1)
    gate_logits_grad = gate_grad - own_rows(gate_soft) * jnp.sum(gate_grad, axis=-1, keepdims=True)
    cond_act_grad = dot("isk,dsk->id", modulation_grad, ada_weight)
    condition_part = silu_pull(cond_act_grad)[0]
    condition_part = swing(condition_part, rank * cols, 1)
    condition_grad = scatter_sum(
        [condition_part[:, step * cols : (step + 1) * cols] for step in range(ranks)]
    )

    biases = small[six + two :].reshape(width // 256, 2, 256).swapaxes(0, 1)
    payload = jnp.concatenate(
        [modulation_grad.astype(F32).reshape(-1), biases.reshape(-1), fc1_bias_part[0]]
    )
    payload = dp_gather(payload, tokens_grad, 1)
    middle_cut = items * 6 * cols
    modulation_every = payload[:, :middle_cut].astype(BF16).reshape(dp_size * items, 6, cols)
    cond_every = cond_every.reshape(dp_size * items, width)
    cond_rows = lax.dynamic_slice_in_dim(cond_every, dp_rank * rows, rows, 1)
    ada_weight_sum = dot("id,isk->dsk", cond_rows, after(modulation_every, tokens_grad))
    ada_bias_sum = jnp.sum(modulation_every.astype(F32), axis=0)
    ada_bias_sum = lax.dynamic_slice_in_dim(
        ada_bias_sum, dp_rank * (cols // dp_size), cols // dp_size, 1
    )
    fine = rows // ranks
    bias_every = jnp.sum(payload[:, middle_cut:], axis=0).reshape(-1, width)
    bias_pair = lax.dynamic_slice_in_dim(bias_every[:2], dp_rank * rows + rank * fine, fine, 1)
    fc1_bias_sum = lax.dynamic_slice_in_dim(bias_every[2], dp_rank * rows, rows, 0)

    out_low, out_high = lax.optimization_barrier((out_low, out_high, in_low[1], in_high[1]))[:2]
    expert_out_sum, fc2_sum = whole_sum([out_low, out_high])

    in_low = final_step(in_low, ahead)
    in_high = final_step(in_high, behind)
    expert_in_sum, fc1_sum = whole_sum([after(in_low, tokens_grad), in_high])
    late = final_step(late, ahead)
    late_sum = (late[0].astype(F32) + late[1].astype(F32))[0] if quick else late[0].astype(F32)
    out_sum = late_sum[:, 3 * head_width :]
    qkv_sum = late_sum[:, : 3 * head_width].reshape(rows, 3, head_width)

    return (
        output,
        tokens_grad,
        condition_grad,
        gate_logits_grad,
        ada_weight_sum,
        ada_bias_sum,
        qkv_sum,
        out_sum,
        bias_pair[1],
        fc1_sum,
        fc1_bias_sum,
        fc2_sum,
        bias_pair[0],
        expert_in_sum,
        expert_out_sum,
    )


def solution(mesh):
    in_specs = (
        P("dp", "tensor", None),
        P("dp", None),
        P("dp", None),
        P("dp", None),
        P("dp", None, None),
        P("dp", None, None),
        P(None, None, "tensor"),
        P(),
        P(None, None, "tensor"),
        P(None, "tensor"),
        P(),
        P(None, "tensor"),
        P("tensor"),
        P(None, "tensor"),
        P(),
        P(None, None, "tensor"),
        P(None, None, "tensor"),
        P("dp", "tensor", None),
    )
    out_specs = (
        P("dp", "tensor", None),
        P("dp", "tensor", None),
        P("dp", "tensor"),
        P("dp", "tensor", None),
        P("dp", None, "tensor"),
        P(None, ("tensor", "dp")),
        P("dp", None, "tensor"),
        P("dp", "tensor"),
        P(("dp", "tensor")),
        P("dp", "tensor"),
        P(("tensor", "dp")),
        P("dp", "tensor"),
        P(("dp", "tensor")),
        P("dp", None, "tensor"),
        P("dp", None, "tensor"),
    )
    return jax.shard_map(body, mesh=mesh, in_specs=in_specs, out_specs=out_specs, check_vma=False)
```

```python
import functools

import jax
import jax.numpy as jnp
from jax import lax
from jax.experimental import pallas as pl
from jax.experimental.pallas import tpu as pltpu
from jax.sharding import PartitionSpec as P

HD = 64
E = 8
CAP = 192
F32 = jnp.float32
BF16 = jnp.bfloat16
I32 = jnp.int32
VMEM_BYTES = 56 * 1024 * 1024


def dot(spec, left, right):
    return jnp.einsum(spec, left, right, preferred_element_type=F32)


def mm(left, right):
    return jnp.dot(left, right, preferred_element_type=F32)


def mm_nt(left, right):
    return lax.dot_general(left, right, (((1,), (1,)), ((), ())), preferred_element_type=F32)


def mm_tn(left, right):
    return lax.dot_general(left, right, (((0,), (0,)), ((), ())), preferred_element_type=F32)


def after(values, *others):
    return lax.optimization_barrier((values,) + others)[0]


def from_rank(values, step):
    size = lax.axis_size("tensor")
    return lax.ppermute(values, "tensor", [(i, (i - step) % size) for i in range(size)])


def to_rank(values, step):
    size = lax.axis_size("tensor")
    return lax.ppermute(values, "tensor", [(i, (i + step) % size) for i in range(size)])


def gather_parts(values):
    size = lax.axis_size("tensor")
    return [values] + [from_rank(values, step) for step in range(1, size)]


def scatter_sum(parts):
    total = parts[0].astype(F32)
    for step in range(1, len(parts)):
        total = total + to_rank(parts[step], step).astype(F32)
    return total


def swing(values, amount, axis):
    twice = jnp.concatenate([values, values], axis=axis)
    return lax.dynamic_slice_in_dim(twice, amount, values.shape[axis], axis)


def dp_exchange(values, bit):
    size = lax.axis_size("dp")
    return lax.ppermute(values, "dp", [(i, i ^ (1 << bit)) for i in range(size)])


def to_relative(blocks):
    size = lax.axis_size("dp")
    rank = lax.axis_index("dp")
    for bit in range(size.bit_length() - 1):
        paired = blocks.reshape((size >> (bit + 1), 2, 1 << bit) + blocks.shape[1:])
        swapped = jnp.where(((rank >> bit) & 1) == 0, paired, paired[:, ::-1])
        blocks = swapped.reshape(blocks.shape)
    return blocks


def dp_scatter(blocks, order, kind):
    current = blocks.reshape((2,) * len(order) + blocks.shape[1:])
    left = sorted(order, reverse=True)
    for bit in order:
        axis = left.index(bit)
        keep = lax.index_in_dim(current, 0, axis, keepdims=False)
        send = lax.index_in_dim(current, 1, axis, keepdims=False)
        other = dp_exchange(send, bit)
        current = (keep.astype(F32) + other.astype(F32)).astype(kind)
        left.pop(axis)
    return current


def dp_gather(values, held=None, stage=-1):
    size = lax.axis_size("dp")
    rank = lax.axis_index("dp")
    current = values[None]
    for bit in range(size.bit_length() - 1):
        if bit == stage:
            current = after(current, held)
        other = dp_exchange(current, bit)
        mine = (rank >> bit) & 1
        low = jnp.where(mine == 0, current, other)
        high = jnp.where(mine == 0, other, current)
        current = jnp.concatenate([low, high], axis=0)
    return current


def norm_parts(values):
    center = values - jnp.mean(values, axis=-1, keepdims=True)
    spread = jnp.mean(center * center, axis=-1, keepdims=True)
    scale = lax.rsqrt(spread + 1e-06)
    return center * scale, scale


def norm_pull(normed, scale, grad):
    return scale * (
        grad
        - jnp.mean(grad, axis=-1, keepdims=True)
        - normed * jnp.mean(grad * normed, axis=-1, keepdims=True)
    )


def gelu_both(values):
    factor = 0.7978845608028654
    square = values * values
    inner = jnp.tanh(values * (factor + (factor * 0.044715) * square))
    half = 0.5 + 0.5 * inner
    slope = half + values * (half * (1.0 - inner)) * (factor + (factor * 0.134145) * square)
    return values * half, slope


def call(kernel, out_shape, in_specs, out_specs, args, grid=(), scratch=(), flops=0, moved=0, name=None, alias=None):
    return pl.pallas_call(
        kernel,
        out_shape=out_shape,
        grid=grid,
        in_specs=in_specs,
        out_specs=out_specs,
        scratch_shapes=scratch,
        input_output_aliases=alias or {},
        compiler_params=pltpu.CompilerParams(
            vmem_limit_bytes=VMEM_BYTES, dimension_semantics=("arbitrary",) * len(grid)
        ),
        cost_estimate=pl.CostEstimate(flops=flops, bytes_accessed=moved, transcendentals=0),
        name=name,
    )(*args)


def whole(shape):
    zeros = (0,) * len(shape)
    return pl.BlockSpec(shape, lambda *_: zeros)


def once(shape):
    zeros = (0,) * len(shape)
    return pl.BlockSpec(shape, lambda *_: zeros, pipeline_mode=pl.Buffered(1))


def shaped(shape, kind):
    return jax.ShapeDtypeStruct(shape, kind)


def pack_heads(values):
    half = values.shape[0] // 2
    rest = jnp.concatenate([values[:half, 128:], values[half:, 128:]], axis=1)
    return jnp.concatenate([values[:, :128], rest], axis=0)


def unpack_heads(values):
    half = values.shape[0] // 3
    rest = values[2 * half :]
    upper = jnp.concatenate([values[:half], rest[:, :64]], axis=1)
    lower = jnp.concatenate([values[half : 2 * half], rest[:, 64:]], axis=1)
    return jnp.concatenate([upper, lower], axis=0)


def attention_kernel(heads, tokens_ref, mod_ref, weight_ref, valid_ref, projected_ref, mixed_ref):
    width = heads * HD
    normed, _ = norm_parts(tokens_ref[0].astype(F32))
    normed = normed * (1.0 + mod_ref[0, 1:2]) + mod_ref[0, 0:1]
    projected = mm(normed.astype(BF16), weight_ref[...]).astype(BF16)
    projected_ref[0] = projected
    live = valid_ref[0] > 0
    mixed = []
    for head in range(heads):
        low = head * HD
        query = projected[:, low : low + HD] * jnp.asarray(0.125, BF16)
        key = projected[:, width + low : width + low + HD]
        value = projected[:, 2 * width + low : 2 * width + low + HD]
        scores = jnp.where(live, mm_nt(query, key), -1e30)
        exponent = jnp.exp(scores - jnp.max(scores, axis=1, keepdims=True))
        probs = exponent * (1.0 / jnp.sum(exponent, axis=1, keepdims=True))
        mixed.append(mm(probs.astype(BF16), value))
    mixed_ref[0] = pack_heads(jnp.concatenate(mixed, axis=1).astype(BF16))


def attention(tokens, mod, weight, valid):
    items, length, width = tokens.shape
    head_width = weight.shape[1] // 3
    return call(
        functools.partial(attention_kernel, head_width // HD),
        (shaped((items, length, 3 * head_width), BF16), shaped((items, 3 * length // 2, 128), BF16)),
        [
            pl.BlockSpec((1, length, width), lambda i: (i, 0, 0)),
            pl.BlockSpec((1, 6, width), lambda i: (i, 0, 0)),
            whole(weight.shape),
            pl.BlockSpec((1, 1, length), lambda i: (i, 0, 0)),
        ],
        (
            pl.BlockSpec((1, length, 3 * head_width), lambda i: (i, 0, 0)),
            pl.BlockSpec((1, 3 * length // 2, 128), lambda i: (i, 0, 0)),
        ),
        (tokens, mod, weight, valid),
        grid=(items,),
        flops=8_000_000_000,
        moved=6_000_000,
        name="attention_forward",
    )


def middle_kernel(ranks, mixed_ref, rest_ref, weight_ref, bias_ref, tokens_ref, mod_ref, middle_ref, branch_ref, normed_ref):
    upper = pl.program_id(1) == 0
    branch = bias_ref[...].astype(F32)
    for rank in range(ranks):
        rest = jnp.where(upper, rest_ref[rank, 0, :, :64], rest_ref[rank, 0, :, 64:])
        branch = branch + mm(jnp.concatenate([mixed_ref[rank, 0], rest], axis=1), weight_ref[rank])
    middle = tokens_ref[0].astype(F32) + mod_ref[0, 2:3] * branch
    middle_ref[0] = middle
    branch_ref[0] = branch.astype(BF16)
    normed, _ = norm_parts(middle)
    normed_ref[0] = (normed * (1.0 + mod_ref[0, 4:5]) + mod_ref[0, 3:4]).astype(BF16)


def middle_part(mixed, weight, bias, tokens, mod):
    items, length, width = tokens.shape
    ranks = mixed.shape[0]
    block = length // 2
    rows = pl.BlockSpec((1, block, width), lambda i, r: (i, r, 0))
    return call(
        functools.partial(middle_kernel, ranks),
        (
            shaped(tokens.shape, F32),
            shaped(tokens.shape, BF16),
            shaped(tokens.shape, BF16),
        ),
        [
            pl.BlockSpec((ranks, 1, block, 128), lambda i, r: (0, i, r, 0)),
            pl.BlockSpec((ranks, 1, block, 128), lambda i, r: (0, i, 2, 0)),
            whole(weight.shape),
            whole(bias.shape),
            rows,
            pl.BlockSpec((1, 6, width), lambda i, r: (i, 0, 0)),
        ],
        (rows, rows, rows),
        (mixed, mixed, weight, bias, tokens, mod),
        grid=(items, 2),
        flops=3_000_000_000,
        moved=12_000_000,
        name="middle",
    )


def hot_rows(expert, marks):
    slots = lax.broadcasted_iota(I32, (CAP, marks.shape[1]), 0) + expert * CAP
    return slots == marks[0:1], slots == marks[1:2]


def as_hot(mask):
    return jnp.where(mask, 1.0, 0.0).astype(BF16)


def forward_kernel(
    items,
    normed_ref,
    marks_ref,
    share_ref,
    columns_ref,
    fc1_ref,
    bias_ref,
    fc2_ref,
    first_ref,
    second_ref,
    buffer_ref,
    act_ref,
    slope_ref,
    hidden_ref,
    hidden_slope_ref,
    out_ref,
    slots_ref,
):
    expert = pl.program_id(0)
    length = normed_ref.shape[1]

    @pl.when(expert == 0)
    def _():
        for item in range(items):
            hidden = mm(normed_ref[item], fc1_ref[...]) + bias_ref[...].astype(F32)
            value, slope = gelu_both(hidden)
            hidden_ref[item] = value.astype(BF16)
            hidden_slope_ref[item] = slope.astype(BF16)

    shares = []
    for item in range(items):
        one, two = hot_rows(expert, marks_ref[item])
        buffer_ref[0, item * CAP : (item + 1) * CAP] = mm(as_hot(one | two), normed_ref[item]).astype(BF16)
        held = jnp.where(one, share_ref[item, 0:1], 0.0) + jnp.where(two, share_ref[item, 1:2], 0.0)
        shares.append(jnp.sum(held, axis=1, keepdims=True))
    share = jnp.concatenate(shares, axis=0)
    value, slope = gelu_both(mm(buffer_ref[0], first_ref[0]))
    act_ref[0] = (share * value).astype(BF16)
    slope_ref[0] = (share * slope).astype(BF16)
    returned = mm_nt(act_ref[0], second_ref[0]).astype(BF16)
    place = pl.ds(pl.multiple_of(expert * CAP, 64), CAP)
    for item in range(items):
        slots_ref[item, place] = returned[item * CAP : (item + 1) * CAP]

    @pl.when(expert == E - 1)
    def _():
        lanes = lax.broadcasted_iota(I32, (length, E * CAP), 1)
        for item in range(items):
            marks = columns_ref[item]
            hot = as_hot((lanes == marks[:, 0:1]) | (lanes == marks[:, 1:2]))
            total = mm(hot, slots_ref[item]) + mm_nt(hidden_ref[item], fc2_ref[...])
            out_ref[item] = total.astype(BF16)


def forward_part(normed, marks, share, columns, fc1, bias, fc2, first, second):
    items, length, width = normed.shape
    units = fc1.shape[1]
    slots = items * CAP
    inner = pl.BlockSpec((1, slots, units), lambda e: (e, 0, 0))
    weight = pl.BlockSpec((1, width, units), lambda e: (e, 0, 0))
    hidden = (items, length, units)
    return call(
        functools.partial(forward_kernel, items),
        (
            shaped((E, slots, width), BF16),
            shaped((E, slots, units), BF16),
            shaped((E, slots, units), BF16),
            shaped(hidden, BF16),
            shaped(hidden, BF16),
            shaped(normed.shape, BF16),
        ),
        [
            whole(normed.shape),
            whole(marks.shape),
            whole(share.shape),
            whole(columns.shape),
            whole(fc1.shape),
            whole(bias.shape),
            whole(fc2.shape),
            weight,
            weight,
        ],
        (
            pl.BlockSpec((1, slots, width), lambda e: (e, 0, 0)),
            inner,
            inner,
            whole(hidden),
            whole(hidden),
            whole(normed.shape),
        ),
        (normed, marks, share, columns, fc1, bias, fc2, first, second),
        grid=(E,),
        scratch=[pltpu.VMEM((items, E * CAP, width), BF16)],
        flops=14_000_000_000,
        moved=40_000_000,
        name="mlp_forward",
    )


def store_blocks(keep_ref, send_ref, rank, index, grad):
    blocks, rows = 2 * keep_ref.shape[0], keep_ref.shape[2]
    for pair in range(blocks // 2):
        place = lax.bitwise_xor(rank // 2, pair)
        low = grad[2 * pair * rows : (2 * pair + 1) * rows]
        high = grad[(2 * pair + 1) * rows : (2 * pair + 2) * rows]
        odd = rank % 2 == 1

        @pl.when(odd)
        def _():
            keep_ref[place, index] = high
            send_ref[place, index] = low

        @pl.when(jnp.logical_not(odd))
        def _():
            keep_ref[place, index] = low
            send_ref[place, index] = high


def split_blocks(grads, dp_size):
    count, width, units = grads.shape
    blocks = to_relative(grads.reshape(count, dp_size, width // dp_size, units).swapaxes(0, 1))
    pairs = blocks.reshape((dp_size // 2, 2) + blocks.shape[1:])
    return pairs[:, 0], pairs[:, 1]


def call_grads(kernel, steps, rank, dp_size, shape, outs, out_specs, specs, args, alias=None, weight=20_000_000):
    width, units = shape
    rows = width // dp_size
    smooth = rows % 16 == 0
    block = pl.BlockSpec((dp_size // 2, 1, rows, units), lambda e: (0, e, 0, 0))
    part = shaped((dp_size // 2, steps, rows, units), BF16)
    return call(
        kernel,
        outs + ((part, part) if smooth else ()),
        [pl.BlockSpec(memory_space=pltpu.SMEM)] + specs,
        out_specs + ((block, block) if smooth else ()),
        (rank,) + args,
        grid=(steps,),
        flops=0,
        moved=weight,
        name="weight_grads",
        alias=alias,
    )


def expert_block(start, count, shape):
    return pl.BlockSpec((1,) + shape, lambda e: (jnp.minimum(e, count - 1) + start, 0, 0))


def slots_kernel(items, start, count, rank_ref, marks_ref, act_ref, *refs):
    expert = pl.program_id(0)
    if start == 0:
        grad_ref, mod_ref, hidden_ref, branch_ref, slots_ref, *grad_refs = refs

        @pl.when(expert == 0)
        def _():
            for item in range(items):
                branch_ref[item] = (grad_ref[item].astype(F32) * mod_ref[item, 5:6]).astype(BF16)

    else:
        branch_ref, _, slots_ref, *grad_refs = refs

    @pl.when(expert < count)
    def _():
        for item in range(items):
            one, two = hot_rows(expert + start, marks_ref[item])
            slots_ref[0, item * CAP : (item + 1) * CAP] = mm(as_hot(one | two), branch_ref[item]).astype(BF16)
        if grad_refs:
            store_blocks(*grad_refs, rank_ref[0], 0, mm_tn(slots_ref[0], act_ref[0]).astype(BF16))

    if start == 0 and grad_refs:

        @pl.when(expert == count)
        def _():
            total = mm_tn(branch_ref[0], hidden_ref[0])
            for item in range(1, items):
                total = total + mm_tn(branch_ref[item], hidden_ref[item])
            store_blocks(*grad_refs, rank_ref[0], 0, total.astype(BF16))


def slots_part(start, count, marks, act, rank, dp_size, grad=None, mod=None, hidden=None, branch=None, held=None):
    items, length, width = (branch if grad is None else grad).shape
    units = act.shape[2]
    slots = items * CAP
    all_rows = whole((items, length, width))
    each = expert_block(start, count, (slots, width))
    filled = shaped((E, slots, width), BF16)
    if start == 0:
        specs, more = [all_rows, whole(mod.shape), whole(hidden.shape)], (grad, mod, hidden)
        outs, out_specs, alias = (shaped(grad.shape, BF16), filled), (all_rows, each), {}
    else:
        specs, more = [all_rows, pl.BlockSpec(memory_space=pl.ANY)], (branch, held)
        outs, out_specs, alias = (filled,), (each,), {4: 0}
    result = call_grads(
        functools.partial(slots_kernel, items, start, count),
        count + (start == 0),
        rank,
        dp_size,
        (width, units),
        outs,
        out_specs,
        [whole(marks.shape), expert_block(start, count, (slots, units))] + specs,
        (marks, act) + more,
        alias,
    )
    if (width // dp_size) % 16:
        picked = slice(start, start + count)
        grads = dot("ecd,ecf->edf", result[-1][picked], act[picked])
        if start == 0:
            grads = jnp.concatenate([grads, dot("isd,isf->df", result[0], hidden)[None]], axis=0)
        result = tuple(result) + split_blocks(grads.astype(BF16), dp_size)
    return result


def out_grad_kernel(rank_ref, low_ref, mixed_ref, *out_refs):
    ranks = mixed_ref.shape[0]
    for rank in range(ranks):
        total = mm_tn(unpack_heads(mixed_ref[rank, 0]), low_ref[0])
        for item in range(1, low_ref.shape[0]):
            total = total + mm_tn(unpack_heads(mixed_ref[rank, item]), low_ref[item])
        total = total.astype(BF16)
        for step, out_ref in enumerate(out_refs):

            @pl.when(lax.rem(rank - rank_ref[0] + ranks, ranks) == step)
            def _():
                out_ref[...] = total


def out_grad_parts(low, mixed, head_width, rank):
    ranks, width = mixed.shape[0], low.shape[2]
    vmem = pl.BlockSpec(memory_space=pltpu.VMEM)
    return call(
        out_grad_kernel,
        (shaped((head_width, width), BF16),) * ranks,
        [pl.BlockSpec(memory_space=pltpu.SMEM), vmem, vmem],
        (vmem,) * ranks,
        (rank, low, mixed),
        flops=0,
        moved=4_000_000,
        name="out_weight_grad",
    )


def late_kernel(rank_ref, qkv_ref, *refs):
    *out_refs, keep_ref, send_ref = refs
    total = sum(out_ref[...].astype(F32) for out_ref in out_refs)
    grad = jnp.concatenate([qkv_ref[...], total.T], axis=1)
    store_blocks(keep_ref, send_ref, rank_ref[0], 0, grad.astype(BF16))


def late_part(qkv_grad, out_parts, rank, dp_size):
    width = qkv_grad.shape[0]
    columns = qkv_grad.shape[1] + out_parts[0].shape[0]
    rows = width // dp_size
    if rows % 16:
        total = sum(part.astype(F32) for part in out_parts)
        grads = jnp.concatenate([qkv_grad, total.T], axis=1).astype(BF16)
        return split_blocks(grads[None], dp_size)
    part = shaped((dp_size // 2, 1, rows, columns), BF16)
    vmem = pl.BlockSpec(memory_space=pltpu.VMEM)
    return call(
        late_kernel,
        (part, part),
        [pl.BlockSpec(memory_space=pltpu.SMEM), vmem] + [vmem] * len(out_parts),
        (vmem, vmem),
        (rank, qkv_grad, *out_parts),
        flops=0,
        moved=0,
        name="late_blocks",
    )


def first_kernel(count, rank_ref, left_ref, right_ref, *refs):
    expert = pl.program_id(0)
    grad_refs = refs[-2:]

    @pl.when(expert < count)
    def _():
        store_blocks(*grad_refs, rank_ref[0], 0, mm_tn(left_ref[0], right_ref[0]).astype(BF16))

    if len(refs) > 2:
        dense_left_ref, dense_right_ref = refs[:2]

        @pl.when(expert == count)
        def _():
            total = mm_tn(dense_left_ref[0], dense_right_ref[0])
            for item in range(1, dense_left_ref.shape[0]):
                total = total + mm_tn(dense_left_ref[item], dense_right_ref[item])
            store_blocks(*grad_refs, rank_ref[0], 0, total.astype(BF16))


def first_part(start, count, left, right, rank, dp_size, dense=()):
    _, slots, width = left.shape
    units = right.shape[2]
    rows = width // dp_size
    if rows % 16:
        picked = slice(start, start + count)
        grads = dot("ecd,ecf->edf", left[picked], right[picked])
        if dense:
            grads = jnp.concatenate([grads, dot("isd,isf->df", *dense)[None]], axis=0)
        return split_blocks(grads.astype(BF16), dp_size)
    return call_grads(
        functools.partial(first_kernel, count),
        count + (1 if dense else 0),
        rank,
        dp_size,
        (width, units),
        (),
        (),
        [expert_block(start, count, (slots, width)), expert_block(start, count, (slots, units))]
        + [whole(value.shape) for value in dense],
        (left, right) + tuple(dense),
        weight=20_000_000 if dense else 4_000_000,
    )


def halve_kernel(first, keep_ref, other_ref, kept_ref, sent_ref):
    total = (keep_ref[...].astype(F32) + other_ref[...].astype(F32)).astype(BF16)
    kept_ref[...] = total[0:1] if first else total[:, 0:1]
    sent_ref[...] = total[1:2] if first else total[:, 1:2]


def halve(keep, other, axis, weight):
    lead = keep.shape[0]
    rest = keep.shape[1:]
    zeros = (0,) * len(rest)
    if lead == 2:
        shape, outer, axis = (2, 1) + rest, 1, 0
    else:
        shape, outer = (2, lead // 2) + rest, lead // 2
    if axis == 0:
        block, result = (2, 1) + rest, (1, outer) + rest
        spec = pl.BlockSpec(block, lambda i: (0, i) + zeros)
        out = pl.BlockSpec((1, 1) + rest, lambda i: (0, i) + zeros)
        steps = outer
    else:
        block, result = (1, 2) + rest, (2, 1) + rest
        spec = pl.BlockSpec(block, lambda i: (i, 0) + zeros)
        out = pl.BlockSpec((1, 1) + rest, lambda i: (i, 0) + zeros)
        steps = 2
    kept, sent = call(
        functools.partial(halve_kernel, axis == 0),
        (shaped(result, BF16),) * 2,
        [spec, spec],
        (out, out),
        (keep.reshape(shape), other.reshape(shape)),
        grid=(steps,),
        flops=0,
        moved=weight,
        name="halve",
    )
    return kept.reshape((lead // 2,) + rest), sent.reshape((lead // 2,) + rest)


def last_kernel(halfway, counts, *refs):
    inputs, (out_ref, *dense_refs) = refs[: 2 * len(counts)], refs[2 * len(counts) :]
    dense = iter(dense_refs)
    place = 0
    for group, size in enumerate(counts):
        keep_ref, other_ref = inputs[2 * group], inputs[2 * group + 1]
        for index in range(size):
            total = keep_ref[index].astype(F32) + other_ref[index].astype(F32)
            if index < halfway:
                out_ref[:, place] = total
                place += 1
            else:
                next(dense)[...] = total


def last(pairs, halfway):
    counts = [keep.shape[0] for keep, _ in pairs]
    rows, units = pairs[0][0].shape[1:]
    args = [value for pair in pairs for value in pair]
    vmem = pl.BlockSpec(memory_space=pltpu.VMEM)
    extra = sum(size > halfway for size in counts)
    return call(
        functools.partial(last_kernel, halfway, counts),
        (shaped((rows, halfway * len(counts), units), F32),) + (shaped((rows, units), F32),) * extra,
        [vmem] * len(args),
        (vmem,) * (1 + extra),
        tuple(args),
        flops=sum(counts) * rows * units,
        moved=8 * sum(counts) * rows * units,
        name="last_sum",
    )


def back_kernel(
    items,
    ranks,
    own_ref,
    branch_ref,
    columns_ref,
    fc1_ref,
    fc2_ref,
    hidden_slope_ref,
    mod_ref,
    weight_ref,
    slots_ref,
    act_ref,
    slope_ref,
    first_ref,
    second_ref,
    middle_hbm,
    attn_hbm,
    cotangent_hbm,
    mlp_hbm,
    up_grad_ref,
    hidden_grad_ref,
    bias_grad_ref,
    dots_ref,
    middle_grad_ref,
    low_ref,
    mixed_ref,
    sums_ref,
    grad_ref,
    held_ref,
    middle_ref,
    attn_ref,
    cotangent_ref,
    mlp_ref,
    sems,
):
    expert = pl.program_id(0)
    length = branch_ref.shape[1]
    pairs = [(middle_hbm, middle_ref), (attn_hbm, attn_ref), (cotangent_hbm, cotangent_ref), (mlp_hbm, mlp_ref)]
    copies = [pltpu.make_async_copy(far, near, sems.at[index]) for index, (far, near) in enumerate(pairs)]

    @pl.when(expert == 0)
    def _():
        for copy in copies:
            copy.start()
        total = jnp.zeros(bias_grad_ref.shape, F32)
        for item in range(items):
            grad = mm(branch_ref[item], fc2_ref[...]) * hidden_slope_ref[item].astype(F32)
            grad = grad.astype(BF16)
            hidden_grad_ref[item] = grad
            total = total + jnp.sum(grad.astype(F32), axis=0, keepdims=True)
            grad_ref[item] = mm_nt(grad, fc1_ref[...])
        bias_grad_ref[...] = total

    pulled = mm(slots_ref[0], second_ref[0])
    up_grad = (pulled * slope_ref[0].astype(F32)).astype(BF16)
    up_grad_ref[0] = up_grad
    total = jnp.sum(act_ref[0].astype(F32) * pulled, axis=1, keepdims=True)
    high = total.astype(BF16).astype(F32)
    lane = lax.broadcasted_iota(I32, (items * CAP, 128), 1)
    split = jnp.where(lane == 0, high, jnp.where(lane == 1, total - high, 0.0)).astype(BF16)
    back = mm_nt(up_grad, first_ref[0]).astype(BF16)
    place = pl.ds(pl.multiple_of(expert * CAP, 64), CAP)
    for item in range(items):
        held_ref[item, place] = back[item * CAP : (item + 1) * CAP]
        dots_ref[item, place] = split[item * CAP : (item + 1) * CAP]

    @pl.when(expert == E - 1)
    def _():
        for copy in copies:
            copy.wait()
        block = length // 2
        lanes = lax.broadcasted_iota(I32, (block, E * CAP), 1)
        for item in range(items):
            sums = []
            for step in range(2):
                part = slice(step * block, (step + 1) * block)
                marks = columns_ref[item, part]
                hot = as_hot((lanes == marks[:, 0:1]) | (lanes == marks[:, 1:2]))
                grad = grad_ref[item, part] + mm(hot, held_ref[item])
                normed, scale = norm_parts(middle_ref[item, part])
                pulled = norm_pull(normed, scale, grad * (1.0 + mod_ref[item, 4:5]))
                at = lax.broadcasted_iota(I32, (block, 1), 0) + step * block
                own = (at >= own_ref[0]) & (at < own_ref[1])
                cotangent = cotangent_ref[item, part].astype(F32)
                pulled = pulled + jnp.where(own, cotangent, 0.0)
                middle_grad_ref[item, part] = pulled.astype(BF16)
                low = (pulled * mod_ref[item, 2:3]).astype(BF16)
                low_ref[item, part] = low
                for rank in range(ranks):
                    mixed = mm_nt(low, weight_ref[rank]).astype(BF16)
                    mixed_ref[rank, item, part] = mixed[:, :128]
                    mixed_ref[rank, item, 2 * block :, step * 64 : (step + 1) * 64] = mixed[:, 128:]
                terms = [
                    grad,
                    grad * normed,
                    pulled * attn_ref[item, part].astype(F32),
                    low.astype(F32),
                    cotangent * mlp_ref[item, part].astype(F32),
                ]
                sums.append(jnp.concatenate([jnp.sum(term, axis=0, keepdims=True) for term in terms], axis=0))
            sums_ref[item] = sums[0] + sums[1]


def back_part(
    branch, columns, fc1, fc2, hidden_slope, branch_slot, act, slope, first, second, middle, attn, cotangent, mlp, mod, weight, own
):
    items, length, width = branch.shape
    ranks = weight.shape[0]
    units = fc1.shape[1]
    slots = items * CAP
    inner = pl.BlockSpec((1, slots, units), lambda e: (e, 0, 0))
    expert_weight = pl.BlockSpec((1, width, units), lambda e: (e, 0, 0))
    hidden = (items, length, units)
    packed = (ranks, items, 3 * length // 2, 128)
    far = pl.BlockSpec(memory_space=pl.ANY)
    return call(
        functools.partial(back_kernel, items, ranks),
        (
            shaped((E, slots, units), BF16),
            shaped(hidden, BF16),
            shaped((1, units), F32),
            shaped((items, E * CAP, 128), BF16),
            shaped(branch.shape, BF16),
            shaped(branch.shape, BF16),
            shaped(packed, BF16),
            shaped((items, 5, width), F32),
        ),
        [
            pl.BlockSpec(memory_space=pltpu.SMEM),
            once(branch.shape),
            once(columns.shape),
            once(fc1.shape),
            once(fc2.shape),
            once(hidden),
            once(mod.shape),
            once(weight.shape),
            pl.BlockSpec((1, slots, width), lambda e: (e, 0, 0)),
            inner,
            inner,
            expert_weight,
            expert_weight,
            far,
            far,
            far,
            far,
        ],
        (
            inner,
            whole(hidden),
            whole((1, units)),
            whole((items, E * CAP, 128)),
            whole(branch.shape),
            whole(branch.shape),
            whole(packed),
            whole((items, 5, width)),
        ),
        (own, branch, columns, fc1, fc2, hidden_slope, mod, weight, branch_slot, act, slope, first, second, middle, attn, cotangent, mlp),
        grid=(E,),
        scratch=[
            pltpu.VMEM(branch.shape, F32),
            pltpu.VMEM((items, E * CAP, width), BF16),
            pltpu.VMEM(middle.shape, F32),
            pltpu.VMEM(attn.shape, BF16),
            pltpu.VMEM(cotangent.shape, BF16),
            pltpu.VMEM(mlp.shape, BF16),
            pltpu.SemaphoreType.DMA((4,)),
        ],
        flops=14_000_000_000,
        moved=50_000_000,
        name="mlp_back",
    )


def tail_kernel(
    ranks,
    rank_ref,
    dots_ref,
    marks_ref,
    sums_ref,
    attn_ref,
    bias_ref,
    grad_ref,
    bias_grad_ref,
    packed_ref,
):
    items, local, width = grad_ref.shape
    cols = width // ranks
    packed_ref[...] = jnp.zeros(packed_ref.shape, F32)
    bias = bias_ref[...].astype(F32)
    slots = lax.broadcasted_iota(I32, (dots_ref.shape[1], marks_ref.shape[2]), 0)
    gates, mods = [], []
    for item in range(items):
        for choice in range(2):
            both = mm_tn(dots_ref[item], as_hot(slots == marks_ref[item, choice : choice + 1]))
            gates.append(both[0:1] + both[1:2])
        sums = sums_ref[item]
        local_sum = jnp.sum(grad_ref[item].astype(F32), axis=0, keepdims=True)
        mods += [attn_ref[item], sums[2:3], sums[0:2], sums[4:5] + local_sum * bias]
    bias_grad = bias_grad_ref[...]
    out_bias_grad = jnp.zeros((1, width), F32)
    for item in range(items):
        out_bias_grad = out_bias_grad + sums_ref[item, 3:4]
    mod_grads = jnp.concatenate(mods, axis=0)
    gates = jnp.concatenate(gates, axis=0)
    six, two = 6 * items, 2 * items
    for rank in range(ranks):
        place = lax.rem(rank - rank_ref[0] + ranks, ranks)
        packed_ref[place, 0:six, 0:cols] = mod_grads[:, rank * cols : (rank + 1) * cols]
        packed_ref[place, six : six + two, 0:local] = gates[:, rank * local : (rank + 1) * local]
        for cut in range(width // 256):
            part = slice(cut * 256, (cut + 1) * 256)
            row = six + two + 2 * cut
            packed_ref[place, row : row + 1] = bias_grad[:, part]
            packed_ref[place, row + 1 : row + 2] = out_bias_grad[:, part]


def tail_part(ranks, rank, dots, marks, sums, attn_sums, bias, grad, bias_grad):
    items, local, width = grad.shape
    packed_rows = 8 * items + 2 * (width // 256)
    vmem = pl.BlockSpec(memory_space=pltpu.VMEM)
    return call(
        functools.partial(tail_kernel, ranks),
        shaped((ranks, packed_rows, 256), F32),
        [pl.BlockSpec(memory_space=pltpu.SMEM)] + [vmem] * 7,
        vmem,
        (rank, dots, marks, sums, attn_sums, bias, grad, bias_grad),
        flops=0,
        moved=0,
        name="tail",
    )


def attention_back_kernel(
    heads, tokens_ref, mod_ref, weight_ref, valid_ref, projected_ref, mixed_ref, middle_ref, part_ref, sums_ref, total_ref
):
    item = pl.program_id(0)
    width = heads * HD
    base, scale = norm_parts(tokens_ref[0].astype(F32))
    normed = (base * (1.0 + mod_ref[0, 1:2]) + mod_ref[0, 0:1]).astype(BF16)
    projected = projected_ref[0]
    grads = [[], [], []]
    count = jnp.sum(valid_ref[0], axis=1, keepdims=True)
    live = lax.broadcasted_iota(I32, (tokens_ref.shape[1], 1), 0) < count
    mixed_grad = unpack_heads(mixed_ref[0])
    for head in range(heads):
        low = head * HD
        query = projected[:, low : low + HD] * jnp.asarray(0.125, BF16)
        key = projected[:, width + low : width + low + HD]
        value = projected[:, 2 * width + low : 2 * width + low + HD]
        mixed = mixed_grad[:, low : low + HD]
        scores = jnp.where(live, mm_nt(key, query), -1e30)
        exponent = jnp.exp(scores - jnp.max(scores, axis=0, keepdims=True))
        probs = exponent * (1.0 / jnp.sum(exponent, axis=0, keepdims=True))
        value_grad = mm(probs.astype(BF16), mixed)
        prob_grad = mm_nt(value, mixed)
        held = probs * prob_grad
        score_grad = (held - probs * jnp.sum(held, axis=0, keepdims=True)).astype(BF16)
        grads[0].append(mm_tn(score_grad, key) * 0.125)
        grads[1].append(mm(score_grad, query))
        grads[2].append(value_grad)
    project_grad = jnp.concatenate(grads[0] + grads[1] + grads[2], axis=1).astype(BF16)
    grad = mm_nt(project_grad, weight_ref[...])
    sums_ref[0] = jnp.concatenate(
        [jnp.sum(grad, axis=0, keepdims=True), jnp.sum(grad * base, axis=0, keepdims=True)], axis=0
    )
    part_ref[0] = (middle_ref[0].astype(F32) + norm_pull(base, scale, grad * (1.0 + mod_ref[0, 1:2]))).astype(BF16)
    weight_grad = mm_tn(normed, project_grad)

    @pl.when(item == 0)
    def _():
        total_ref[...] = weight_grad

    @pl.when(item > 0)
    def _():
        total_ref[...] += weight_grad


def attention_back(tokens, mod, weight, valid, projected, mixed, middle):
    items, length, width = tokens.shape
    columns = weight.shape[1]
    each = pl.BlockSpec((1, length, width), lambda i: (i, 0, 0))
    return call(
        functools.partial(attention_back_kernel, columns // (3 * HD)),
        (shaped(tokens.shape, BF16), shaped((items, 2, width), F32), shaped(weight.shape, F32)),
        [
            each,
            pl.BlockSpec((1, 6, width), lambda i: (i, 0, 0)),
            whole(weight.shape),
            pl.BlockSpec((1, 1, length), lambda i: (i, 0, 0)),
            pl.BlockSpec((1, length, columns), lambda i: (i, 0, 0)),
            pl.BlockSpec((1, 3 * length // 2, 128), lambda i: (i, 0, 0)),
            each,
        ],
        (each, pl.BlockSpec((1, 2, width), lambda i: (i, 0, 0)), whole(weight.shape)),
        (tokens, mod, weight, valid, projected, mixed, middle),
        grid=(items,),
        flops=0,
        moved=0,
        name="attention_back",
    )


def body(
    tokens,
    time_embed,
    class_embed,
    valid_mask,
    routes,
    gate_logits,
    ada_weight,
    ada_bias,
    qkv_weight,
    out_weight,
    out_bias,
    fc1_weight,
    fc1_bias,
    fc2_weight,
    fc2_bias,
    expert_in,
    expert_out,
    out_grad,
):
    items, local, width = tokens.shape
    ranks = lax.axis_size("tensor")
    rank = lax.axis_index("tensor")
    dp_size = lax.axis_size("dp")
    dp_rank = lax.axis_index("dp")
    length = local * ranks
    head_width = qkv_weight.shape[2]
    cols = ada_weight.shape[2]
    rows = width // dp_size
    start = rank * local
    bits = dp_size.bit_length() - 1
    forth = list(range(bits))
    back = [0] + list(range(bits - 1, 0, -1))
    dp_index = dp_rank.astype(I32).reshape(1)

    def own_rows(values):
        return lax.dynamic_slice_in_dim(values, start, local, 1)

    tokens_full = lax.all_gather(tokens, "tensor", axis=1, tiled=True)
    out_turned = out_weight.T
    share_rows = head_width // dp_size
    piece = lax.dynamic_slice_in_dim(out_turned, dp_rank * share_rows, share_rows, 0)
    pieces = jnp.concatenate(gather_parts(piece), axis=0)
    condition = time_embed + class_embed
    cond_wide, silu_pull = jax.vjp(jax.nn.silu, condition)
    cond_low = cond_wide.astype(BF16)
    bias_cols = lax.dynamic_slice_in_dim(ada_bias, rank * cols, cols, 1)
    modulation_local = dot("id,dsk->isk", cond_low, ada_weight) + bias_cols.astype(F32)[None]
    modulation = jnp.concatenate(gather_parts(modulation_local), axis=2)
    modulation = swing(modulation, width - rank * cols, 2)

    first = after(expert_in, modulation).transpose(1, 0, 2)
    second = after(expert_out, modulation).transpose(1, 0, 2)
    qkv = qkv_weight.reshape(width, 3 * head_width)
    chosen = routes.transpose(0, 2, 1)
    live = valid_mask[:, None, :] > 0
    expert_ids = jnp.arange(E, dtype=I32)
    named = (chosen[:, :, None, :] == expert_ids[None, None, :, None]) & live[:, :, None, :]
    choose = jnp.any(named, axis=1)
    place = jnp.arange(length, dtype=I32)
    earlier = (place[:, None] < place[None, :]).astype(BF16)
    before = dot("iet,ts->ies", choose.astype(BF16), earlier).astype(I32)
    position = jnp.sum(jnp.where(named, before[:, None], 0), axis=2)
    marks = jnp.where(live, chosen * CAP + position, -1)
    columns = marks.transpose(0, 2, 1)
    gate_soft = jax.nn.softmax(gate_logits, axis=-1)
    share = gate_soft.transpose(0, 2, 1) * live

    every = dp_gather(jnp.concatenate([pieces, cond_low], axis=0))
    cond_every = every[:, ranks * share_rows :]
    out_full = every[:, : ranks * share_rows].reshape(dp_size, ranks, share_rows, width)
    out_full = out_full.swapaxes(0, 1).reshape(ranks, head_width, width)
    out_full = swing(out_full, ranks - rank, 0)
    fc2_row = fc2_bias[None] * 1
    modulation = after(modulation, first, second, marks, columns, share, fc2_row)
    projected, mixed = attention(tokens_full, modulation, qkv, valid_mask[:, None, :])
    mixed_full = lax.all_gather(mixed, "tensor", axis=0)
    grad_full = lax.all_gather(after(out_grad, mixed_full, out_full), "tensor", axis=1, tiled=True)

    middle, branch_attn, normed_mlp = middle_part(
        after(mixed_full, out_full), out_full, out_bias[None], tokens_full, modulation
    )
    buffer, expert_act, expert_slope, hidden_act, hidden_slope, mlp_part = forward_part(
        normed_mlp, marks, share, columns, fc1_weight, fc1_bias[None], fc2_weight, first, second
    )
    mlp_sum = lax.psum_scatter(mlp_part, "tensor", scatter_dimension=1, tiled=True)

    quick = rows % 16 == 0 and dp_size == 8
    halfway = E // 2

    def start_sum(keep, send):
        return keep, dp_exchange(send, 0)

    def second_step(pair, order, weight=4_000_000):
        keep, other = pair
        if not quick:
            return keep, other
        kept, sent = halve(keep, other, 0 if order[0] == 2 else 1, weight)
        return kept, sent

    def third_step(pair, order, weight=4_000_000):
        if not quick:
            return pair
        kept, sent = pair
        return halve(kept, dp_exchange(sent, order[0]), 0, weight)

    def final_step(pair, order):
        if not quick:
            keep, other = pair
            return dp_scatter((keep.astype(F32) + other.astype(F32)).astype(BF16), order, BF16)
        kept, sent = pair
        return kept[0], dp_exchange(sent, order[1])[0]

    def whole_sum(pairs):
        if quick:
            return last(pairs, halfway)
        experts = jnp.concatenate([pair[:halfway] for pair in pairs], axis=0).swapaxes(0, 1).astype(F32)
        return [experts] + [pair[halfway].astype(F32) for pair in pairs if pair.shape[0] > halfway]

    ahead, behind = forth[1:], back[1:]
    branch_grad, branch_slot, keep, send = slots_part(
        0, halfway, marks, expert_act, dp_index, dp_size, grad=grad_full, mod=modulation, hidden=hidden_act
    )
    out_low = start_sum(keep, send)
    branch_slot, keep, send = slots_part(
        halfway, E - halfway, marks, expert_act, dp_index, dp_size, branch=branch_grad, held=branch_slot
    )
    out_high = start_sum(keep, send)
    out_low = second_step(out_low, ahead)
    out_high = second_step(out_high, behind)
    own = jnp.stack([start, start + local]).astype(I32)
    up_grad, hidden_grad, fc1_bias_part, dots, middle_grad, low_grad, mixed_parts, sums = back_part(
        branch_grad,
        after(columns, out_low[1], out_high[1]),
        fc1_weight,
        fc2_weight,
        hidden_slope,
        branch_slot,
        expert_act,
        expert_slope,
        first,
        second,
        middle,
        branch_attn,
        grad_full,
        mlp_part,
        modulation,
        out_full,
        own,
    )
    mixed_grad = lax.psum_scatter(mixed_parts, "tensor", scatter_dimension=0)

    marker = after(dp_index, mixed_parts, mlp_sum)
    out_low = third_step((after(out_low[0], marker), out_low[1]), ahead)
    out_high = third_step((after(out_high[0], marker), out_high[1]), behind)
    rank_index = rank.astype(I32).reshape(1)
    out_parts = out_grad_parts(
        low_grad, mixed_full, head_width, after(rank_index, marker, out_low[1], out_high[1])
    )
    in_low = start_sum(
        *first_part(0, halfway, buffer, up_grad, after(marker, out_parts[0]), dp_size)
    )
    out_low = final_step(out_low, ahead)
    out_high = final_step(out_high, behind)
    in_high = start_sum(
        *first_part(
            halfway,
            E - halfway,
            buffer,
            up_grad,
            after(marker, in_low[0], *out_low, *out_high),
            dp_size,
            dense=(normed_mlp, hidden_grad),
        )
    )
    in_low = second_step((after(in_low[0], in_high[0]), in_low[1]), ahead)
    branch_mlp = after(mlp_sum, in_low[1]).astype(F32) + fc2_row.astype(F32)[None]
    output = (own_rows(middle) + modulation[:, 5][:, None] * branch_mlp).astype(BF16)
    late_start = after(start, in_low[1])
    fc2_bias_part = jnp.sum(
        lax.dynamic_slice_in_dim(branch_grad, late_start, local, 1).astype(F32), axis=(0, 1)
    )[None]
    in_high = second_step(
        (after(in_high[0], in_low[1], mixed_grad, output, fc2_bias_part), in_high[1]), behind
    )
    out_parts = after(tuple(out_parts), mixed_grad)
    out_parts = [out_parts[0]] + [to_rank(out_parts[step], step) for step in range(1, ranks)]

    gate = after(modulation, in_low[1], in_high[1])
    tokens_part, attn_sums, qkv_grad = attention_back(
        tokens_full, gate, qkv, valid_mask[:, None, :], projected, mixed_grad, middle_grad
    )
    tokens_grad = lax.psum_scatter(tokens_part, "tensor", scatter_dimension=1, tiled=True)
    packed = tail_part(ranks, rank_index, dots, marks, sums, attn_sums, fc2_row, out_grad, fc2_bias_part)
    late = start_sum(*late_part(qkv_grad, out_parts, after(dp_index, packed), dp_size))
    late = second_step(late, ahead, 0)
    in_low_other = dp_exchange(in_low[1], ahead[0]) if quick else in_low[1]
    in_high_other = dp_exchange(in_high[1], behind[0]) if quick else in_high[1]
    small = scatter_sum(list(after(tuple(packed[step] for step in range(ranks)), in_low_other, in_high_other)))
    if quick:
        in_high = halve(after(in_high[0], late[1]), in_high_other, 0, 0)
        in_low = halve(after(in_low[0], late[1], small), in_low_other, 0, 0)
    late = third_step((after(late[0], in_low[1], in_high[1]), late[1]), ahead)

    six, two = 6 * items, 2 * items
    modulation_grad = small[:six, :cols].reshape(items, 6, cols).astype(BF16)
    gate_grad = small[six : six + two, :local].reshape(items, 2, local).transpose(0, 2, 1)
    gate_logits_grad = gate_grad - own_rows(gate_soft) * jnp.sum(gate_grad, axis=-1, keepdims=True)
    cond_act_grad = dot("isk,dsk->id", modulation_grad, ada_weight)
    condition_part = silu_pull(cond_act_grad)[0]
    condition_part = swing(condition_part, rank * cols, 1)
    condition_grad = scatter_sum(
        [condition_part[:, step * cols : (step + 1) * cols] for step in range(ranks)]
    )

    biases = small[six + two :].reshape(width // 256, 2, 256).swapaxes(0, 1)
    payload = jnp.concatenate(
        [modulation_grad.astype(F32).reshape(-1), biases.reshape(-1), fc1_bias_part[0]]
    )
    payload = dp_gather(payload, tokens_grad, 1)
    middle_cut = items * 6 * cols
    modulation_every = payload[:, :middle_cut].astype(BF16).reshape(dp_size * items, 6, cols)
    cond_every = cond_every.reshape(dp_size * items, width)
    cond_rows = lax.dynamic_slice_in_dim(cond_every, dp_rank * rows, rows, 1)
    ada_weight_sum = dot("id,isk->dsk", cond_rows, after(modulation_every, tokens_grad))
    ada_bias_sum = jnp.sum(modulation_every.astype(F32), axis=0)
    ada_bias_sum = lax.dynamic_slice_in_dim(
        ada_bias_sum, dp_rank * (cols // dp_size), cols // dp_size, 1
    )
    fine = rows // ranks
    bias_every = jnp.sum(payload[:, middle_cut:], axis=0).reshape(-1, width)
    bias_pair = lax.dynamic_slice_in_dim(bias_every[:2], dp_rank * rows + rank * fine, fine, 1)
    fc1_bias_sum = lax.dynamic_slice_in_dim(bias_every[2], dp_rank * rows, rows, 0)

    out_low, out_high = lax.optimization_barrier((out_low, out_high, in_low[1], in_high[1]))[:2]
    expert_out_sum, fc2_sum = whole_sum([out_low, out_high])

    in_low = final_step(in_low, ahead)
    in_high = final_step(in_high, behind)
    expert_in_sum, fc1_sum = whole_sum([after(in_low, tokens_grad), in_high])
    late = final_step(late, ahead)
    late_sum = (late[0].astype(F32) + late[1].astype(F32))[0] if quick else late[0].astype(F32)
    out_sum = late_sum[:, 3 * head_width :]
    qkv_sum = late_sum[:, : 3 * head_width].reshape(rows, 3, head_width)

    return (
        output,
        tokens_grad,
        condition_grad,
        gate_logits_grad,
        ada_weight_sum,
        ada_bias_sum,
        qkv_sum,
        out_sum,
        bias_pair[1],
        fc1_sum,
        fc1_bias_sum,
        fc2_sum,
        bias_pair[0],
        expert_in_sum,
        expert_out_sum,
    )


def solution(mesh):
    in_specs = (
        P("dp", "tensor", None),
        P("dp", None),
        P("dp", None),
        P("dp", None),
        P("dp", None, None),
        P("dp", None, None),
        P(None, None, "tensor"),
        P(),
        P(None, None, "tensor"),
        P(None, "tensor"),
        P(),
        P(None, "tensor"),
        P("tensor"),
        P(None, "tensor"),
        P(),
        P(None, None, "tensor"),
        P(None, None, "tensor"),
        P("dp", "tensor", None),
    )
    out_specs = (
        P("dp", "tensor", None),
        P("dp", "tensor", None),
        P("dp", "tensor"),
        P("dp", "tensor", None),
        P("dp", None, "tensor"),
        P(None, ("tensor", "dp")),
        P("dp", None, "tensor"),
        P("dp", "tensor"),
        P(("dp", "tensor")),
        P("dp", "tensor"),
        P(("tensor", "dp")),
        P("dp", "tensor"),
        P(("dp", "tensor")),
        P("dp", None, "tensor"),
        P("dp", None, "tensor"),
    )
    return jax.shard_map(body, mesh=mesh, in_specs=in_specs, out_specs=out_specs, check_vma=False)
```
